32 devices in a mesh: ctx: 16 (over z, y, core), head: 2 (over x).
Axes of the slice: x: 2, y: 2, z: 4, core: 2. Of those that a mesh axis runs over, the one named last changes fastest.
Arguments:
- query_raw: bfloat16 [2048, 4096], P('ctx', 'head'), may hold values from -6 to 6
- key_raw: bfloat16 [2048, 512], P('ctx', 'head'), may hold values from -6 to 6
- value_in: bfloat16 [2048, 512], P('ctx', 'head'), may hold values from -6 to 6
- grad_out: bfloat16 [2048, 4096], P('ctx', 'head'), may hold values from -16 to 16
- query_gain: float32 [128], replicated, may hold values from 0.25 to 1.75
- key_gain: float32 [128], replicated, may hold values from 0.25 to 1.75
- loss_table: float32 [16], replicated, may hold values from 0.5 to 8
- loss_bucket: int32 [2048], P('ctx'), may hold values from 0 to 15
- block_docs: int32 [16], P('ctx'), may hold values from 0 to 3, never falling along the last dimension, each value on 1 to 11 neighbouring positions
- query_weight: bfloat16 [4096, 4096], P(None, 'head'), may hold values from -0.09375 to 0.09375
Outputs:
- grad_input: bfloat16 [2048, 4096], P('ctx', 'head')
- grad_key: bfloat16 [2048, 512], P('ctx', 'head')
- grad_value: bfloat16 [2048, 512], P('ctx', 'head')
The draws below stay inside these ranges and needn't reach their ends.
Inputs may be any that keep to these rules, and one draw needn't show every extreme that they name: `block_docs`: document ids never decrease along the sequence; every document covers 1 to 11 consecutive blocks, and some document covers exactly 11.
All inputs are finite; a program needn't handle non-finite values.
Results may differ from the reference program's by a relative error of at most 0.012.
Values may be sent and summed in bfloat16 or wider, within the bound.
No kernel may reach another device: no remote copies, remote signals or barrier semaphores. Data moves between devices by JAX's collectives and lax.ppermute only.
A program may use at most 64 MiB of HBM per device.

```python
import math
import jax
import jax.numpy as jnp
import numpy as np
from jax import lax

D = 4096
QH = 32
KVH = 4
HD = 128
TOK_DEV = 128
BLOCK = 128
HOPS = 10
NBUCKET = 16
SEQ = 2048
NBLK = 16
MOST = 11
N_CTX = 16


def plant(values, key, low, high):
    longest = values.shape.index(max(values.shape))
    spots = []
    for shift in (0, 1):
        where = [jax.random.randint(jax.random.fold_in(key, axis), (), 0, length) for axis, length in enumerate(values.shape)]
        where[longest] = (where[longest] + shift) % values.shape[longest]
        spots.append(tuple(where))
    return values.at[spots[0]].set(low).at[spots[1]].set(high)


def steps_of(key, shape, shards, low, high):
    level = 1.0
    for dim, parts in shards:
        steps = jax.random.uniform(jax.random.fold_in(jax.random.fold_in(key, 6), dim), (parts,), jnp.float32, low / len(shards), high / len(shards))
        level = level * jnp.repeat(jnp.exp(steps), shape[dim] // parts).reshape((-1,) + (1,) * (len(shape) - 1 - dim))
    return level


def split_up(number_of, total, reach, slope):
    portions = [(1 << 20) // math.isqrt(standing ** slope) + 1 for standing in range(2, number_of + 1)]
    rest, counts = total - reach - (number_of - 1), [1] * (number_of - 1)
    while rest > 0:
        candidates = [i for i in range(number_of - 1) if counts[i] < reach]
        mass, remaining = sum([portions[i] for i in candidates]), rest
        for i in candidates:
            extra = min(reach - counts[i], max(1, remaining * portions[i] // mass), rest)
            counts[i] = counts[i] + extra
            rest = rest - extra
    return np.array([reach] + counts)


def ragged(key, amount, total, bound, lean):
    if amount == 2:
        one = jax.random.randint(key, (), max(1, total - bound), min(bound, total - 1) + 1)
        return jnp.stack([one, total - one])
    lengths = jnp.asarray(split_up(amount, total, bound, lean), jnp.int32)
    twos = (amount - 1) // 2
    giver, sink = lengths[1:1 + 2 * twos:2], lengths[2:2 + 2 * twos:2]
    room = jnp.minimum(giver - 1, bound - sink)
    passed = jax.random.randint(jax.random.fold_in(key, 1), (twos,), 0, 1 << 20) % (room + 1)
    lengths = lengths.at[1:1 + 2 * twos:2].set(giver - passed).at[2:2 + 2 * twos:2].set(sink + passed)
    return lengths[jax.random.permutation(jax.random.fold_in(key, 2), amount)]


def gaussian(key, extent, width, bound, pieces=(), kind=jnp.bfloat16):
    values = jax.random.normal(key, extent, jnp.float32) * width
    if len(pieces) > 0:
        values = steps_of(key, extent, pieces, -0.22, 0.18) * values
    return jnp.clip(values, min=-bound, max=bound).astype(kind)


def setup_inputs(seed: int = 0) -> dict:
    key_list = jax.random.split(jax.random.key(seed), 11)
    return {
        "query_raw": gaussian(key_list[0], (SEQ, QH * HD), 1.0, 6.0, ((0, 16), (1, 2))),
        "key_raw": gaussian(key_list[1], (SEQ, KVH * HD), 1.0, 6.0, ((0, 16), (1, 2))),
        "value_in": gaussian(key_list[2], (SEQ, KVH * HD), 1.0, 6.0, ((0, 16), (1, 2))),
        "grad_out": gaussian(key_list[3], (SEQ, QH * HD), 4.0, 16.0, ((0, 16), (1, 2))),
        "query_gain": jnp.clip(1.0 + 0.15 * jax.random.normal(key_list[4], (HD,), jnp.float32), 0.25, 1.75),
        "key_gain": jnp.clip(1.0 + 0.15 * jax.random.normal(key_list[5], (HD,), jnp.float32), 0.25, 1.75),
        "loss_table": jnp.clip(jnp.exp(jax.random.uniform(key_list[6], (NBUCKET,), jnp.float32, math.log(0.5), math.log(8.0))), 0.5, 8.0),
        "loss_bucket": plant(jax.random.randint(key_list[7], (SEQ,), 0, NBUCKET), jax.random.fold_in(key_list[7], 1), 0, NBUCKET - 1).astype(jnp.int32),
        "block_docs": jnp.searchsorted(jnp.cumsum(ragged(key_list[8], NBLK // 4, NBLK, MOST, 2)), jnp.arange(NBLK), side="right").astype(jnp.int32),
        "query_weight": gaussian(key_list[9], (D, QH * HD), D ** -0.5, 0.09375, ((1, 2),)),
    }


norm_eps = 1e-06

def rms_apply(values, gain):
    mean_square = lax.optimization_barrier(jnp.mean(values * values, axis=-1, keepdims=True))
    return values * lax.rsqrt(mean_square + norm_eps) * gain

def rms_back(values, gain, cotangent):
    result, pullback = jax.vjp(lambda inner: rms_apply(inner, gain), values)
    return pullback(cotangent)[0]

def round_trip(values):
    return lax.optimization_barrier(values.astype(jnp.bfloat16)).astype(jnp.float32)

def reference(query_raw, key_raw, value_in, grad_out, query_gain, key_gain, loss_table, loss_bucket, block_docs, query_weight):
    group = QH // KVH
    scale = HD ** (-0.5)
    margin = HOPS * TOK_DEV
    span = margin + TOK_DEV
    q_float = query_raw.astype(jnp.float32).reshape(SEQ, KVH, group, HD)
    q_hat = rms_apply(q_float, query_gain).astype(jnp.bfloat16)
    k_float = key_raw.astype(jnp.float32).reshape(SEQ, KVH, HD)
    k_hat = rms_apply(k_float, key_gain).astype(jnp.bfloat16)
    values = value_in.reshape(SEQ, KVH, HD)
    grad_rows = grad_out.reshape(SEQ, KVH, group, HD)
    picks = loss_bucket[:, None] == jnp.arange(NBUCKET, dtype=jnp.int32)[None, :]
    tok_weight = lax.optimization_barrier(jnp.sum(jnp.where(picks, loss_table[None, :], jnp.float32(0.0)), axis=1))
    tok_docs = jnp.broadcast_to(block_docs[:, None], (NBLK, BLOCK)).reshape(SEQ)
    k_pad = jnp.concatenate([jnp.zeros((margin, KVH, HD), jnp.bfloat16), k_hat], axis=0)
    v_pad = jnp.concatenate([jnp.zeros((margin, KVH, HD), jnp.bfloat16), values], axis=0)
    doc_pad = jnp.concatenate([jnp.full((margin,), -1, jnp.int32), tok_docs.astype(jnp.int32)], axis=0)
    zero_pad = jnp.zeros((margin + SEQ, KVH, HD), jnp.float32)

    def one_block(carry, index):
        dk_acc, dv_acc = carry
        start = (index * TOK_DEV).astype(jnp.int32)
        q_blk = lax.dynamic_slice_in_dim(q_hat, start, TOK_DEV, 0).astype(jnp.float32)
        qf_blk = lax.dynamic_slice_in_dim(q_float, start, TOK_DEV, 0)
        g_blk = lax.dynamic_slice_in_dim(grad_rows, start, TOK_DEV, 0).astype(jnp.float32)
        w_blk = lax.dynamic_slice_in_dim(tok_weight, start, TOK_DEV, 0)
        qd_blk = lax.dynamic_slice_in_dim(tok_docs, start, TOK_DEV, 0)
        k_win = lax.dynamic_slice_in_dim(k_pad, start, span, 0).astype(jnp.float32)
        v_win = lax.dynamic_slice_in_dim(v_pad, start, span, 0).astype(jnp.float32)
        d_win = lax.dynamic_slice_in_dim(doc_pad, start, span, 0)
        q_pos = start + jnp.arange(TOK_DEV, dtype=jnp.int32)
        k_pos = start - margin + jnp.arange(span, dtype=jnp.int32)
        allowed = (qd_blk[:, None] == d_win[None, :]) & (k_pos[None, :] <= q_pos[:, None]) & (k_pos[None, :] >= 0)
        scores = jnp.einsum('tkgd,skd->kgts', q_blk, k_win) * scale
        exponent = jnp.where(allowed[None, None], jnp.exp(scores), jnp.float32(0.0))
        total = lax.optimization_barrier(jnp.sum(exponent, axis=-1))
        weighted = jnp.einsum('kgts,skd->tkgd', round_trip(exponent), v_win)
        attn_out = weighted / jnp.transpose(total, (2, 0, 1))[..., None]
        delta = w_blk[:, None, None] * lax.optimization_barrier(jnp.sum(g_blk * attn_out, axis=-1))
        attention = exponent / total[..., None]
        weight_row = w_blk[None, None, :, None]
        value_dots = jnp.einsum('tkgd,skd->kgts', g_blk, v_win)
        score_grad = attention * (weight_row * value_dots - jnp.transpose(delta, (1, 2, 0))[..., None])
        ds_half = round_trip(score_grad)
        pw_half = round_trip(attention * weight_row)
        dv_win = jnp.einsum('kgts,tkgd->skd', pw_half, g_blk)
        dk_win = jnp.einsum('kgts,tkgd->skd', ds_half, q_blk) * scale
        dq_hat = jnp.einsum('kgts,skd->tkgd', ds_half, k_win) * scale
        dq_raw = rms_back(qf_blk, query_gain, dq_hat).astype(jnp.bfloat16).reshape(TOK_DEV, QH * HD)
        dx_blk = jnp.dot(dq_raw, query_weight.T, preferred_element_type=jnp.float32).astype(jnp.bfloat16)
        dk_acc = lax.dynamic_update_slice_in_dim(dk_acc, lax.dynamic_slice_in_dim(dk_acc, start, span, 0) + dk_win, start, 0)
        dv_acc = lax.dynamic_update_slice_in_dim(dv_acc, lax.dynamic_slice_in_dim(dv_acc, start, span, 0) + dv_win, start, 0)
        return ((dk_acc, dv_acc), dx_blk)
    (dk_acc, dv_acc), dx_rows = lax.scan(one_block, (zero_pad, zero_pad), jnp.arange(N_CTX, dtype=jnp.int32))
    grad_input = dx_rows.reshape(SEQ, D)
    grad_key = rms_back(k_float, key_gain, dk_acc[margin:]).astype(jnp.bfloat16).reshape(SEQ, KVH * HD)
    grad_value = dv_acc[margin:].astype(jnp.bfloat16).reshape(SEQ, KVH * HD)
    return (grad_input, grad_key, grad_value)
```

```python
import functools
import math

import jax
import jax.numpy as jnp
from jax import lax
from jax.experimental import pallas as pl
from jax.experimental.pallas import tpu as pltpu
from jax.sharding import PartitionSpec as P

HD = 128
BLOCK = 128
EXTRA = 16
norm_eps = 1e-06
SCALE = HD ** (-0.5)
NEG = -1e30
NT = (((1,), (1,)), ((), ()))
F32 = jnp.float32
BF16 = jnp.bfloat16


def moved(array, axis, target):
    size = lax.axis_size(axis)
    pairs = [(i, target(i)) for i in range(size)]
    return lax.ppermute(array, axis, [(i, t) for i, t in pairs if t is not None and 0 <= t < size])


def vmem(shape=None):
    return pl.BlockSpec(memory_space=pltpu.VMEM)


def smem():
    return pl.BlockSpec(memory_space=pltpu.SMEM)


def params(mib):
    return pltpu.CompilerParams(vmem_limit_bytes=mib << 20)


def keys_kernel(kv_local, pos, docs, key, value, gain, bucket, keep, send):
    core = pos[0]
    mine = core if kv_local > 1 else 0
    for out, head in ((keep, mine), (send, (1 - core) if kv_local > 1 else 0)):
        lanes = pl.ds(pl.multiple_of(head * HD, HD), HD)
        raw = key[:, lanes].astype(F32)
        mean_square = jnp.mean(raw * raw, axis=-1, keepdims=True)
        out[:BLOCK, :HD] = (raw * lax.rsqrt(mean_square + norm_eps) * gain[...]).astype(BF16)
        out[:BLOCK, HD:] = value[:, lanes]
        row = lax.broadcasted_iota(jnp.int32, (EXTRA, HD), 0)
        doc = jnp.full((EXTRA, HD), docs[0] + 1, jnp.int32).astype(F32)
        buckets = jnp.broadcast_to(bucket[...].astype(F32), (EXTRA, HD))
        extra = jnp.where(row == 0, doc, jnp.where(row == 1, buckets, 0.0)).astype(BF16)
        out[BLOCK:, :HD] = extra
        out[BLOCK:, HD:] = extra


def join_kernel(keep, recv, out):
    out[:BLOCK, :] = keep[:BLOCK, :]
    out[BLOCK : 2 * BLOCK, :] = recv[:BLOCK, :]
    first = keep[BLOCK:, :].astype(F32)
    second = recv[BLOCK:, :].astype(F32)
    row = lax.broadcasted_iota(jnp.int32, (EXTRA, 2 * HD), 0)
    top = jnp.broadcast_to(first[0:1], (EXTRA, 2 * HD))
    next_row = jnp.broadcast_to(second[0:1], (EXTRA, 2 * HD))
    extra = jnp.where(row == 0, top, jnp.where(row == 1, next_row, 0.0))
    out[2 * BLOCK :, :] = extra.astype(BF16)


def split_kernel(half, pos, query, grad, out):
    other = pl.ds(pl.multiple_of((1 - pos[0]) * half, HD), half)
    out[:, :half] = query[:, other]
    out[:, half:] = grad[:, other]


def queries_kernel(
    heads, pos, table, query, grad, other, gain, keep, recv, q_hat, rows, raw_t, inverse_t, weight
):
    half = heads * HD
    own = pl.ds(pl.multiple_of(pos[0] * half, HD), half)
    for side in range(2):
        if side == 0:
            raw_all, grad_all = query[:, own], grad[:, own]
        else:
            raw_all, grad_all = other[:, :half], other[:, half:]
        for head in range(heads):
            at = (side * heads + head) * BLOCK
            raw = raw_all[:, head * HD : (head + 1) * HD].astype(F32)
            mean_square = jnp.mean(raw * raw, axis=-1, keepdims=True)
            q_hat[at : at + BLOCK, :] = (
                raw * lax.rsqrt(mean_square + norm_eps) * gain[...]
            ).astype(BF16)
            rows[at : at + BLOCK, :] = grad_all[:, head * HD : (head + 1) * HD]
            turned = raw.T
            raw_t[:, at : at + BLOCK] = turned.astype(BF16)
            mean_t = jnp.mean(turned * turned, axis=0, keepdims=True)
            inverse_t[:, at : at + BLOCK] = jnp.broadcast_to(
                lax.rsqrt(mean_t + norm_eps), (8, BLOCK)
            )
    for side, source in enumerate((keep, recv)):
        picks = source[BLOCK:, :HD].astype(F32)[1:2]
        found = jnp.zeros((1, HD), F32)
        for b in range(table.shape[0]):
            found = found + jnp.where(picks == float(b), table[b], 0.0)
        weight[:, side * HD : (side + 1) * HD] = jnp.broadcast_to(found, (8, HD))


def attention_kernel(
    heads,
    pos,
    own,
    far_a,
    far_b,
    far_c,
    far_d,
    far_e,
    q_hat,
    rows,
    raw_t,
    inverse_t,
    weight,
    gain,
    dq_keep,
    dq_send,
    part_own,
    part_a,
    part_b,
    part_c,
    part_d,
    part_e,
    keys,
    values,
    keys_t,
    expo,
    dots,
    pw_half,
    ds_half,
    dk,
    dv,
):
    core = pos[0]
    sources = (own, far_a, far_b, far_c, far_d, far_e)
    outs = (part_own, part_a, part_b, part_c, part_d, part_e)
    span = 2 * BLOCK
    wide = 2 * BLOCK
    total_rows = len(sources) * span
    for index, source in enumerate(sources):
        at = index * span
        block = source[:span, :HD]
        keys[at : at + span, :] = block
        values[at : at + span, :] = source[:span, HD:]
        keys_t[:, at : at + span] = block.astype(F32).T.astype(BF16)
    dk[...] = jnp.zeros_like(dk)
    dv[...] = jnp.zeros_like(dv)
    docs = [source[span:, :].astype(F32) for source in sources]
    own_docs = docs[0]
    row = lax.broadcasted_iota(jnp.int32, (BLOCK, wide), 0)
    col = lax.rem(lax.broadcasted_iota(jnp.int32, (BLOCK, wide), 1), BLOCK)
    triangle = row <= col
    factor = SCALE * math.log2(math.e)
    gain_t = gain[...]
    pairs = heads // 2

    for side in range(2):
        q_doc = own_docs[side : side + 1]
        bias = []
        for index in range(len(sources)):
            for block in range(2):
                k_doc = docs[index][block : block + 1]
                same = (k_doc == q_doc) & (k_doc > 0.0)
                if index == 0 and block != side:
                    later = (core == 1) if side == 0 else (core == 0)
                    same = same & later
                bias.append(jnp.where(same, 0.0, NEG))
        w_row = jnp.concatenate([weight[0:1, side * HD : (side + 1) * HD]] * 2, axis=1)

        def one_pair(pair, _, side=side, bias=bias, w_row=w_row):
            at = pl.multiple_of(side * heads * BLOCK + pair * wide, wide)
            here = pl.ds(at, wide)
            q_two = q_hat[here, :]
            g_two = rows[here, :]
            expo[...] = lax.dot_general(keys[...], q_two, NT, preferred_element_type=F32)
            dots[...] = lax.dot_general(values[...], g_two, NT, preferred_element_type=F32)
            total = jnp.zeros((8, wide), F32)
            weighted = jnp.zeros((8, wide), F32)
            for block in range(len(bias)):
                r = slice(block * BLOCK, (block + 1) * BLOCK)
                value = jnp.exp2(expo[r, :] * factor + bias[block])
                if block == side:
                    value = jnp.where(triangle, value, 0.0)
                expo[r, :] = value
                total = total + jnp.sum(value.reshape(BLOCK // 8, 8, wide), axis=0)
                weighted = weighted + jnp.sum(
                    (value * dots[r, :]).reshape(BLOCK // 8, 8, wide), axis=0
                )
            inverse = 1.0 / jnp.sum(total, axis=0, keepdims=True)
            shift = jnp.sum(weighted, axis=0, keepdims=True) * inverse
            level = inverse * w_row
            for block in range(len(bias)):
                r = slice(block * BLOCK, (block + 1) * BLOCK)
                scaled = expo[r, :] * level
                pw_half[r, :] = scaled.astype(BF16)
                ds_half[r, :] = (scaled * (dots[r, :] - shift)).astype(BF16)
            dv[...] += jnp.dot(pw_half[...], g_two, preferred_element_type=F32)
            dk[...] += jnp.dot(ds_half[...], q_two, preferred_element_type=F32)
            dq_t = jnp.dot(keys_t[...], ds_half[...], preferred_element_type=F32)
            x = raw_t[:, here].astype(F32)
            r_row = inverse_t[0:1, here]
            dy = dq_t * (gain_t * SCALE)
            inner = jnp.mean(x * dy, axis=0, keepdims=True)
            dx = r_row * dy - x * (r_row * r_row * r_row * inner)
            out = dq_keep if side == 0 else dq_send
            for part in range(2):
                lanes = pl.ds(pl.multiple_of(pair * wide + part * HD, HD), HD)
                out[:, lanes] = dx[:, part * BLOCK : (part + 1) * BLOCK].T.astype(BF16)
            return 0

        lax.fori_loop(0, pairs, one_pair, 0)

    for index, out in enumerate(outs):
        r = slice(index * span, (index + 1) * span)
        out[:, :HD] = (dk[r, :] * SCALE).astype(out.dtype)
        out[:, HD:] = dv[r, :].astype(out.dtype)


def project_kernel(half, pos, keep, recv, weight, out, lhs):
    @pl.when(pl.program_id(0) == 0)
    def _():
        core = pos[0]
        lhs[:, pl.ds(pl.multiple_of(core * half, HD), half)] = keep[...]
        lhs[:, pl.ds(pl.multiple_of((1 - core) * half, HD), half)] = recv[...]

    out[...] = lax.dot_general(
        lhs[...], weight[...], NT, preferred_element_type=F32
    ).astype(out.dtype)


def project(pos, keep, recv, query_weight, slice_index, width, out_dtype):
    tokens, half = keep.shape
    features = query_weight.shape[1]
    tile = min(512, width)
    steps = width // tile
    where = jnp.stack([pos[0], slice_index]).astype(jnp.int32)
    return pl.pallas_call(
        functools.partial(project_kernel, half),
        grid_spec=pltpu.PrefetchScalarGridSpec(
            num_scalar_prefetch=1,
            grid=(steps,),
            in_specs=[
                pl.BlockSpec((tokens, half), lambda i, w: (0, 0)),
                pl.BlockSpec((tokens, half), lambda i, w: (0, 0)),
                pl.BlockSpec((tile, features), lambda i, w: (w[1] * steps + i, 0)),
            ],
            out_specs=pl.BlockSpec((tokens, tile), lambda i, w: (0, i)),
            scratch_shapes=[pltpu.VMEM((tokens, features), BF16)],
        ),
        out_shape=jax.ShapeDtypeStruct((tokens, width), out_dtype),
        compiler_params=params(24),
        cost_estimate=pl.CostEstimate(
            flops=2 * tokens * features * width,
            bytes_accessed=2 * features * width,
            transcendentals=0,
        ),
    )(where, keep, recv, query_weight)


def collect_kernel(part_own, a, b, c, d, e, keep, send):
    result = part_own[...]
    for back in (a, b, c, d, e):
        result = result + back[...].astype(F32)
    keep[...] = result[:BLOCK]
    send[...] = result[BLOCK:].astype(BF16)


def finish_kernel(kv_local, pos, keep, recv, key, gain, grad_key, grad_value):
    core = pos[0]
    parts = []
    if kv_local > 1:
        parts = [(core, keep[...]), (1 - core, recv[...].astype(F32))]
    else:
        parts = [(0, keep[...] + recv[...].astype(F32))]
    for head, part in parts:
        lanes = pl.ds(pl.multiple_of(head * HD, HD), HD)
        raw = key[:, lanes].astype(F32)
        inverse = lax.rsqrt(jnp.mean(raw * raw, axis=-1, keepdims=True) + norm_eps)
        dy = part[:, :HD] * gain[...]
        inner = jnp.mean(raw * dy, axis=-1, keepdims=True)
        dx = inverse * dy - raw * (inverse * inverse * inverse * inner)
        grad_key[:, lanes] = dx.astype(BF16)
        grad_value[:, lanes] = part[:, HD:].astype(BF16)


def local(
    query_raw,
    key_raw,
    value_in,
    grad_out,
    query_gain,
    key_gain,
    loss_table,
    loss_bucket,
    block_docs,
    query_weight,
):
    tokens = query_raw.shape[0]
    kv_local = key_raw.shape[1] // HD
    half = query_raw.shape[1] // 2
    heads = half // HD
    rank = lax.axis_index("ctx")
    pos = jnp.stack([rank % 2]).astype(jnp.int32)
    key_row = key_gain.reshape(1, HD)
    query_row = query_gain.reshape(1, HD)
    query_col = query_gain.reshape(HD, 1)
    shape = jax.ShapeDtypeStruct

    keep, send = pl.pallas_call(
        functools.partial(keys_kernel, kv_local),
        in_specs=[smem(), smem(), vmem(), vmem(), vmem(), vmem()],
        out_specs=[vmem(), vmem()],
        out_shape=[shape((BLOCK + EXTRA, 2 * HD), BF16)] * 2,
    )(pos, block_docs, key_raw, value_in, key_row, loss_bucket.reshape(1, tokens))
    partner = lambda i: i ^ 1
    recv = moved(send, "ctx", partner)
    message = pl.pallas_call(
        join_kernel,
        in_specs=[vmem(), vmem()],
        out_specs=vmem(),
        out_shape=shape((2 * BLOCK + EXTRA, 2 * HD), BF16),
    )(keep, recv)

    far_d = moved(message, "ctx", lambda i: i + 8)
    far_b = moved(message, "ctx", lambda i: i + 4)
    far_a = moved(message, "ctx", lambda i: i + 2 if (i // 2) % 2 == 0 else i + 10)
    far_c = moved(far_b, "ctx", lambda i: i ^ 2)
    far_e = moved(far_d, "ctx", lambda i: i ^ 2)

    halves = pl.pallas_call(
        functools.partial(split_kernel, half),
        in_specs=[smem(), vmem(), vmem()],
        out_specs=vmem(),
        out_shape=shape((tokens, 2 * half), BF16),
    )(pos, query_raw, grad_out)
    other = moved(halves, "ctx", partner)
    total = 2 * heads * BLOCK
    q_hat, rows, raw_t, inverse_t, weight = pl.pallas_call(
        functools.partial(queries_kernel, heads),
        in_specs=[smem(), smem()] + [vmem()] * 6,
        out_specs=[vmem()] * 5,
        out_shape=[
            shape((total, HD), BF16),
            shape((total, HD), BF16),
            shape((HD, total), BF16),
            shape((8, total), F32),
            shape((8, 2 * HD), F32),
        ],
        compiler_params=params(24),
        cost_estimate=pl.CostEstimate(
            flops=20 * total * HD, bytes_accessed=12 * total * HD, transcendentals=0
        ),
    )(pos, loss_table, query_raw, grad_out, other, query_row, keep, recv)

    span = 2 * BLOCK
    n_rows = 6 * span
    far_shape = shape((span, 2 * HD), BF16)
    outs = pl.pallas_call(
        functools.partial(attention_kernel, heads),
        in_specs=[smem()] + [vmem()] * 12,
        out_specs=[vmem()] * 8,
        out_shape=[
            shape((tokens, half), BF16),
            shape((tokens, half), BF16),
            shape((span, 2 * HD), F32),
        ]
        + [far_shape] * 5,
        scratch_shapes=[
            pltpu.VMEM((n_rows, HD), BF16),
            pltpu.VMEM((n_rows, HD), BF16),
            pltpu.VMEM((HD, n_rows), BF16),
            pltpu.VMEM((n_rows, span), F32),
            pltpu.VMEM((n_rows, span), F32),
            pltpu.VMEM((n_rows, span), BF16),
            pltpu.VMEM((n_rows, span), BF16),
            pltpu.VMEM((n_rows, HD), F32),
            pltpu.VMEM((n_rows, HD), F32),
        ],
        compiler_params=params(32),
        cost_estimate=pl.CostEstimate(
            flops=10 * n_rows * total * HD,
            bytes_accessed=12 * total * HD,
            transcendentals=n_rows * total,
        ),
    )(
        pos,
        message,
        far_a,
        far_b,
        far_c,
        far_d,
        far_e,
        q_hat,
        rows,
        raw_t,
        inverse_t,
        weight,
        query_col,
    )
    dq_keep, dq_send, part_own, part_a, part_b, part_c, part_d, part_e = outs

    dq_recv = moved(dq_send, "ctx", partner)
    n_head = lax.axis_size("head")
    head = lax.axis_index("head")
    width = query_weight.shape[0] // n_head
    arrived = []
    for shift in range(1, n_head):
        term = project(
            pos, dq_keep, dq_recv, query_weight, (head + shift) % n_head, width, BF16
        )
        arrived.append(moved(term, "head", lambda i, s=shift: (i + s) % n_head))
    mine = project(pos, dq_keep, dq_recv, query_weight, head, width, F32)

    back_d = moved(part_d, "ctx", lambda i: i - 8)
    back_e = moved(part_e, "ctx", lambda i: (i ^ 2) - 8)
    back_c = moved(part_c, "ctx", lambda i: (i ^ 2) - 4)
    back_b = moved(part_b, "ctx", lambda i: i - 4)
    back_a = moved(part_a, "ctx", lambda i: i - 2 if (i // 2) % 2 == 1 else i - 10)
    sum_keep, sum_send = pl.pallas_call(
        collect_kernel,
        in_specs=[vmem()] * 6,
        out_specs=[vmem()] * 2,
        out_shape=[shape((BLOCK, 2 * HD), F32), shape((BLOCK, 2 * HD), BF16)],
    )(part_own, back_a, back_b, back_c, back_d, back_e)
    sum_recv = moved(sum_send, "ctx", partner)
    grad_key, grad_value = pl.pallas_call(
        functools.partial(finish_kernel, kv_local),
        in_specs=[smem()] + [vmem()] * 4,
        out_specs=[vmem()] * 2,
        out_shape=[shape(key_raw.shape, BF16), shape(value_in.shape, BF16)],
    )(pos, sum_keep, sum_recv, key_raw, key_row)

    grad_input = mine
    for piece in arrived:
        grad_input = grad_input + piece.astype(F32)
    return (grad_input.astype(BF16), grad_key, grad_value)


def solution(mesh):
    placed = (
        P("ctx", "head"),
        P("ctx", "head"),
        P("ctx", "head"),
        P("ctx", "head"),
        P(),
        P(),
        P(),
        P("ctx"),
        P("ctx"),
        P(None, "head"),
    )
    return jax.shard_map(
        local,
        mesh=mesh,
        in_specs=placed,
        out_specs=(P("ctx", "head"), P("ctx", "head"), P("ctx", "head")),
        check_vma=False,
    )
```

```python
import functools
import math

import jax
import jax.numpy as jnp
from jax import lax
from jax.experimental import pallas as pl
from jax.experimental.pallas import tpu as pltpu
from jax.sharding import PartitionSpec as P

HD = 128
BLOCK = 128
EXTRA = 16
norm_eps = 1e-06
SCALE = HD ** (-0.5)
NEG = -1e30
NT = (((1,), (1,)), ((), ()))
F32 = jnp.float32
BF16 = jnp.bfloat16


def moved(array, axis, target):
    size = lax.axis_size(axis)
    pairs = [(i, target(i)) for i in range(size)]
    return lax.ppermute(array, axis, [(i, t) for i, t in pairs if t is not None and 0 <= t < size])


def vmem():
    return pl.BlockSpec(memory_space=pltpu.VMEM)


def hbm():
    return pl.BlockSpec(memory_space=pltpu.HBM)


def smem():
    return pl.BlockSpec(memory_space=pltpu.SMEM)


def params(mib):
    return pltpu.CompilerParams(vmem_limit_bytes=mib << 20)


def message_kernel(
    kv_local, docs, docs_p, key, value, gain, key_p, value_p, out, key_v, value_v, gain_v, sems
):
    core = lax.rem(lax.axis_index("ctx"), 2)
    lanes = pl.ds(pl.multiple_of((core if kv_local > 1 else 0) * HD, HD), HD)
    copies = [
        pltpu.make_async_copy(source, target, sems.at[i])
        for i, (source, target) in enumerate(
            ((key.at[:, lanes], key_v), (value.at[:, lanes], value_v), (gain, gain_v))
        )
    ]
    for copy in copies:
        copy.start()
    for copy in copies:
        copy.wait()
    for side in range(2):
        at = side * BLOCK
        raw = (key_v[...] if side == 0 else key_p[:, lanes]).astype(F32)
        mean_square = jnp.mean(raw * raw, axis=-1, keepdims=True)
        out[at : at + BLOCK, :HD] = (
            raw * lax.rsqrt(mean_square + norm_eps) * gain_v[...]
        ).astype(BF16)
        out[at : at + BLOCK, HD:] = value_v[...] if side == 0 else value_p[:, lanes]
    row = lax.broadcasted_iota(jnp.int32, (EXTRA, 2 * HD), 0)
    extra = jnp.where(row == 0, docs[0] + 1, jnp.where(row == 1, docs_p[0] + 1, 0))
    out[2 * BLOCK :, :] = extra.astype(F32).astype(BF16)


def queries_kernel(
    heads,
    table,
    bucket,
    bucket_p,
    query,
    grad,
    gain,
    query_p,
    grad_p,
    q_hat,
    rows,
    raw_t,
    inverse_t,
    weight,
    query_v,
    grad_v,
    gain_v,
    sems,
):
    half = heads * HD
    core = lax.rem(lax.axis_index("ctx"), 2)
    own = pl.ds(pl.multiple_of(core * half, HD), half)
    copies = [
        pltpu.make_async_copy(source, target, sems.at[i])
        for i, (source, target) in enumerate(
            ((query.at[:, own], query_v), (grad.at[:, own], grad_v), (gain, gain_v))
        )
    ]
    for copy in copies:
        copy.start()
    for copy in copies:
        copy.wait()
    for side in range(2):
        if side == 0:
            raw_all, grad_all = query_v[...], grad_v[...]
        else:
            raw_all, grad_all = query_p[:, own], grad_p[:, own]
        for head in range(heads):
            at = (side * heads + head) * BLOCK
            raw = raw_all[:, head * HD : (head + 1) * HD].astype(F32)
            mean_square = jnp.mean(raw * raw, axis=-1, keepdims=True)
            q_hat[at : at + BLOCK, :] = (
                raw * lax.rsqrt(mean_square + norm_eps) * gain_v[...]
            ).astype(BF16)
            rows[at : at + BLOCK, :] = grad_all[:, head * HD : (head + 1) * HD]
            turned = raw.T
            raw_t[:, at : at + BLOCK] = turned.astype(BF16)
            mean_t = jnp.mean(turned * turned, axis=0, keepdims=True)
            inverse_t[:, at : at + BLOCK] = jnp.broadcast_to(
                lax.rsqrt(mean_t + norm_eps), (8, BLOCK)
            )
    for side, source in enumerate((bucket, bucket_p)):
        picks = source[...]
        found = jnp.zeros((1, HD), F32)
        for b in range(table.shape[0]):
            found = found + jnp.where(picks == b, table[b], 0.0)
        weight[:, side * HD : (side + 1) * HD] = jnp.broadcast_to(found, (8, HD))


def attention_kernel(
    heads,
    own,
    far_a,
    far_b,
    far_c,
    far_d,
    far_e,
    q_hat,
    rows,
    raw_t,
    inverse_t,
    weight,
    gain,
    dq_keep,
    dq_send,
    part_own,
    part_a,
    part_b,
    part_c,
    part_d,
    part_e,
    keys,
    values,
    keys_t,
    expo,
    dots,
    pw_half,
    ds_half,
    dk,
    dv,
):
    core = lax.rem(lax.axis_index("ctx"), 2)
    sources = (own, far_a, far_b, far_c, far_d, far_e)
    outs = (part_own, part_a, part_b, part_c, part_d, part_e)
    span = 2 * BLOCK
    wide = 2 * BLOCK
    total_rows = len(sources) * span
    for index, source in enumerate(sources):
        at = index * span
        block = source[:span, :HD]
        keys[at : at + span, :] = block
        values[at : at + span, :] = source[:span, HD:]
        keys_t[:, at : at + span] = block.astype(F32).T.astype(BF16)
    dk[...] = jnp.zeros_like(dk)
    dv[...] = jnp.zeros_like(dv)
    docs = [source[span:, :].astype(F32) for source in sources]
    own_docs = docs[0]
    row = lax.broadcasted_iota(jnp.int32, (BLOCK, wide), 0)
    col = lax.rem(lax.broadcasted_iota(jnp.int32, (BLOCK, wide), 1), BLOCK)
    triangle = row <= col
    factor = SCALE * math.log2(math.e)
    gain_t = gain[...]
    pairs = heads // 2

    for side in range(2):
        q_doc = own_docs[side : side + 1]
        bias = []
        for index in range(len(sources)):
            for block in range(2):
                k_doc = docs[index][block : block + 1]
                same = (k_doc == q_doc) & (k_doc > 0.0)
                if index == 0 and block != side:
                    later = (core == 1) if side == 0 else (core == 0)
                    same = same & later
                bias.append(jnp.where(same, 0.0, NEG))
        w_row = jnp.concatenate([weight[0:1, side * HD : (side + 1) * HD]] * 2, axis=1)

        def one_pair(pair, _, side=side, bias=bias, w_row=w_row):
            at = pl.multiple_of(side * heads * BLOCK + pair * wide, wide)
            here = pl.ds(at, wide)
            q_two = q_hat[here, :]
            g_two = rows[here, :]
            expo[...] = lax.dot_general(keys[...], q_two, NT, preferred_element_type=F32)
            dots[...] = lax.dot_general(values[...], g_two, NT, preferred_element_type=F32)
            total = jnp.zeros((8, wide), F32)
            weighted = jnp.zeros((8, wide), F32)
            for block in range(len(bias)):
                r = slice(block * BLOCK, (block + 1) * BLOCK)
                value = jnp.exp2(expo[r, :] * factor + bias[block])
                if block == side:
                    value = jnp.where(triangle, value, 0.0)
                expo[r, :] = value
                total = total + jnp.sum(value.reshape(BLOCK // 8, 8, wide), axis=0)
                weighted = weighted + jnp.sum(
                    (value * dots[r, :]).reshape(BLOCK // 8, 8, wide), axis=0
                )
            inverse = 1.0 / jnp.sum(total, axis=0, keepdims=True)
            shift = jnp.sum(weighted, axis=0, keepdims=True) * inverse
            level = inverse * w_row
            for block in range(len(bias)):
                r = slice(block * BLOCK, (block + 1) * BLOCK)
                scaled = expo[r, :] * level
                pw_half[r, :] = scaled.astype(BF16)
                ds_half[r, :] = (scaled * (dots[r, :] - shift)).astype(BF16)
            dv[...] += jnp.dot(pw_half[...], g_two, preferred_element_type=F32)
            dk[...] += jnp.dot(ds_half[...], q_two, preferred_element_type=F32)
            dq_t = jnp.dot(keys_t[...], ds_half[...], preferred_element_type=F32)
            x = raw_t[:, here].astype(F32)
            r_row = inverse_t[0:1, here]
            dy = dq_t * (gain_t * SCALE)
            inner = jnp.mean(x * dy, axis=0, keepdims=True)
            dx = r_row * dy - x * (r_row * r_row * r_row * inner)
            out = dq_keep if side == 0 else dq_send
            for part in range(2):
                features = pl.ds(pl.multiple_of(pair * wide + part * HD, HD), HD)
                out[features, :] = dx[:, part * BLOCK : (part + 1) * BLOCK].astype(BF16)
            return 0

        lax.fori_loop(0, pairs, one_pair, 0)

    for index, out in enumerate(outs):
        r = slice(index * span, (index + 1) * span)
        out[:, :HD] = (dk[r, :] * SCALE).astype(out.dtype)
        out[:, HD:] = dv[r, :].astype(out.dtype)


def project_kernel(half, chunks, width, where, keep, recv, weight, out, lhs, held, sems):
    rows = width // chunks
    copies = [
        pltpu.make_async_copy(
            weight.at[pl.ds(pl.multiple_of(where[0] * width + i * rows, rows), rows), :],
            held.at[pl.ds(i * rows, rows), :],
            sems.at[i],
        )
        for i in range(chunks)
    ]
    for copy in copies:
        copy.start()
    core = lax.rem(lax.axis_index("ctx"), 2)
    lhs[pl.ds(pl.multiple_of(core * half, HD), half), :] = keep[...]
    lhs[pl.ds(pl.multiple_of((1 - core) * half, HD), half), :] = recv[...]
    for i, copy in enumerate(copies):
        copy.wait()
        term = jnp.dot(held[i * rows : (i + 1) * rows, :], lhs[...], preferred_element_type=F32)
        out[:, i * rows : (i + 1) * rows] = term.T.astype(out.dtype)


def project(keep, recv, query_weight, slice_index, width, out_dtype):
    half, tokens = keep.shape
    features = query_weight.shape[1]
    chunks = max(1, width // 512)
    return pl.pallas_call(
        functools.partial(project_kernel, half, chunks, width),
        in_specs=[smem(), vmem(), vmem(), hbm()],
        out_specs=vmem(),
        scratch_shapes=[
            pltpu.VMEM((features, tokens), BF16),
            pltpu.VMEM((width, features), BF16),
            pltpu.SemaphoreType.DMA((chunks,)),
        ],
        out_shape=jax.ShapeDtypeStruct((tokens, width), out_dtype),
        compiler_params=params(24),
        cost_estimate=pl.CostEstimate(
            flops=2 * tokens * features * width,
            bytes_accessed=2 * features * width,
            transcendentals=0,
        ),
    )(slice_index.reshape(1).astype(jnp.int32), keep, recv, query_weight)


def collect_kernel(part_own, a, b, c, d, e, keep, send):
    result = part_own[...]
    for back in (a, b, c, d, e):
        result = result + back[...].astype(F32)
    keep[...] = result[:BLOCK]
    send[...] = result[BLOCK:].astype(BF16)


def finish_kernel(
    kv_local, keep, recv, key, gain, grad_key, grad_value, key_v, gain_v, sems
):
    copies = [
        pltpu.make_async_copy(key, key_v, sems.at[0]),
        pltpu.make_async_copy(gain, gain_v, sems.at[1]),
    ]
    for copy in copies:
        copy.start()
    for copy in copies:
        copy.wait()
    core = lax.rem(lax.axis_index("ctx"), 2)
    if kv_local > 1:
        parts = [(core, keep[...]), (1 - core, recv[...].astype(F32))]
    else:
        parts = [(0, keep[...] + recv[...].astype(F32))]
    for head, part in parts:
        lanes = pl.ds(pl.multiple_of(head * HD, HD), HD)
        raw = key_v[:, lanes].astype(F32)
        inverse = lax.rsqrt(jnp.mean(raw * raw, axis=-1, keepdims=True) + norm_eps)
        dy = part[:, :HD] * gain_v[...]
        inner = jnp.mean(raw * dy, axis=-1, keepdims=True)
        dx = inverse * dy - raw * (inverse * inverse * inverse * inner)
        grad_key[:, lanes] = dx.astype(BF16)
        grad_value[:, lanes] = part[:, HD:].astype(BF16)


def local(
    query_raw,
    key_raw,
    value_in,
    grad_out,
    query_gain,
    key_gain,
    loss_table,
    loss_bucket,
    block_docs,
    query_weight,
):
    tokens = query_raw.shape[0]
    kv_local = key_raw.shape[1] // HD
    half = query_raw.shape[1] // 2
    heads = half // HD
    key_row = key_gain.reshape(1, HD)
    query_row = query_gain.reshape(1, HD)
    query_col = query_gain.reshape(HD, 1)
    shape = jax.ShapeDtypeStruct

    partner = lambda i: i ^ 1
    key_p = moved(key_raw, "ctx", partner)
    value_p = moved(value_in, "ctx", partner)
    docs_p = moved(block_docs, "ctx", partner)
    bucket_p = moved(loss_bucket, "ctx", partner)
    message = pl.pallas_call(
        functools.partial(message_kernel, kv_local),
        in_specs=[smem(), smem(), hbm(), hbm(), hbm(), vmem(), vmem()],
        out_specs=vmem(),
        out_shape=shape((2 * BLOCK + EXTRA, 2 * HD), BF16),
        scratch_shapes=[
            pltpu.VMEM((BLOCK, HD), BF16),
            pltpu.VMEM((BLOCK, HD), BF16),
            pltpu.VMEM((1, HD), F32),
            pltpu.SemaphoreType.DMA((3,)),
        ],
        compiler_params=params(16),
    )(block_docs, docs_p, key_raw, value_in, key_row, key_p, value_p)

    far_d = moved(message, "ctx", lambda i: i + 8)
    far_b = moved(message, "ctx", lambda i: i + 4)
    far_a = moved(message, "ctx", lambda i: i + 2 if (i // 2) % 2 == 0 else i + 10)
    query_in, grad_in, _ = lax.optimization_barrier((query_raw, grad_out, message))
    query_p = moved(query_in, "ctx", partner)
    grad_p = moved(grad_in, "ctx", partner)
    total = 2 * heads * BLOCK
    q_hat, rows, raw_t, inverse_t, weight = pl.pallas_call(
        functools.partial(queries_kernel, heads),
        in_specs=[smem(), vmem(), vmem(), hbm(), hbm(), hbm(), vmem(), vmem()],
        out_specs=[vmem()] * 5,
        out_shape=[
            shape((total, HD), BF16),
            shape((total, HD), BF16),
            shape((HD, total), BF16),
            shape((8, total), F32),
            shape((8, 2 * HD), F32),
        ],
        scratch_shapes=[
            pltpu.VMEM((BLOCK, half), BF16),
            pltpu.VMEM((BLOCK, half), BF16),
            pltpu.VMEM((1, HD), F32),
            pltpu.SemaphoreType.DMA((3,)),
        ],
        compiler_params=params(16),
    )(
        loss_table,
        loss_bucket.reshape(1, tokens),
        bucket_p.reshape(1, tokens),
        query_raw,
        grad_out,
        query_row,
        query_p,
        grad_p,
    )
    far_c = moved(far_b, "ctx", lambda i: i ^ 2)
    far_d, q_hat = lax.optimization_barrier((far_d, q_hat))
    far_e = moved(far_d, "ctx", lambda i: i ^ 2)

    span = 2 * BLOCK
    n_rows = 6 * span
    far_shape = shape((span, 2 * HD), BF16)
    outs = pl.pallas_call(
        functools.partial(attention_kernel, heads),
        in_specs=[vmem()] * 12,
        out_specs=[vmem()] * 8,
        out_shape=[
            shape((half, tokens), BF16),
            shape((half, tokens), BF16),
            shape((span, 2 * HD), F32),
        ]
        + [far_shape] * 5,
        scratch_shapes=[
            pltpu.VMEM((n_rows, HD), BF16),
            pltpu.VMEM((n_rows, HD), BF16),
            pltpu.VMEM((HD, n_rows), BF16),
            pltpu.VMEM((n_rows, span), F32),
            pltpu.VMEM((n_rows, span), F32),
            pltpu.VMEM((n_rows, span), BF16),
            pltpu.VMEM((n_rows, span), BF16),
            pltpu.VMEM((n_rows, HD), F32),
            pltpu.VMEM((n_rows, HD), F32),
        ],
        compiler_params=params(32),
        cost_estimate=pl.CostEstimate(
            flops=10 * n_rows * total * HD,
            bytes_accessed=12 * total * HD,
            transcendentals=n_rows * total,
        ),
    )(
        message,
        far_a,
        far_b,
        far_c,
        far_d,
        far_e,
        q_hat,
        rows,
        raw_t,
        inverse_t,
        weight,
        query_col,
    )
    dq_keep, dq_send, part_own, part_a, part_b, part_c, part_d, part_e = outs

    dq_recv = moved(dq_send, "ctx", partner)
    n_head = lax.axis_size("head")
    head = lax.axis_index("head")
    width = query_weight.shape[0] // n_head
    arrived = []
    for shift in range(1, n_head):
        term = project(dq_keep, dq_recv, query_weight, (head + shift) % n_head, width, BF16)
        arrived.append(moved(term, "head", lambda i, s=shift: (i + s) % n_head))
    mine = project(dq_keep, dq_recv, query_weight, head, width, F32)

    back_d = moved(part_d, "ctx", lambda i: i - 8)
    back_e = moved(part_e, "ctx", lambda i: (i ^ 2) - 8)
    back_c = moved(part_c, "ctx", lambda i: (i ^ 2) - 4)
    back_b = moved(part_b, "ctx", lambda i: i - 4)
    back_a = moved(part_a, "ctx", lambda i: i - 2 if (i // 2) % 2 == 1 else i - 10)
    sum_keep, sum_send = pl.pallas_call(
        collect_kernel,
        in_specs=[vmem()] * 6,
        out_specs=[vmem()] * 2,
        out_shape=[shape((BLOCK, 2 * HD), F32), shape((BLOCK, 2 * HD), BF16)],
        compiler_params=params(16),
    )(part_own, back_a, back_b, back_c, back_d, back_e)
    sum_recv = moved(sum_send, "ctx", partner)
    grad_key, grad_value = pl.pallas_call(
        functools.partial(finish_kernel, kv_local),
        in_specs=[vmem(), vmem(), hbm(), hbm()],
        out_specs=[vmem()] * 2,
        out_shape=[shape(key_raw.shape, BF16), shape(value_in.shape, BF16)],
        scratch_shapes=[
            pltpu.VMEM(key_raw.shape, BF16),
            pltpu.VMEM((1, HD), F32),
            pltpu.SemaphoreType.DMA((2,)),
        ],
        compiler_params=params(16),
    )(sum_keep, sum_recv, key_raw, key_row)

    grad_input = mine
    for piece in arrived:
        grad_input = grad_input + piece.astype(F32)
    return (grad_input.astype(BF16), grad_key, grad_value)


def solution(mesh):
    placed = (
        P("ctx", "head"),
        P("ctx", "head"),
        P("ctx", "head"),
        P("ctx", "head"),
        P(),
        P(),
        P(),
        P("ctx"),
        P("ctx"),
        P(None, "head"),
    )
    return jax.shard_map(
        local,
        mesh=mesh,
        in_specs=placed,
        out_specs=(P("ctx", "head"), P("ctx", "head"), P("ctx", "head")),
        check_vma=False,
    )
```

```python
import functools
import math

import jax
import jax.numpy as jnp
from jax import lax
from jax.experimental import pallas as pl
from jax.experimental.pallas import tpu as pltpu
from jax.sharding import PartitionSpec as P

HD = 128
BLOCK = 128
EXTRA = 16
HOPS = 10
norm_eps = 1e-06
SCALE = HD ** (-0.5)
NEG = -1e30
NT = (((1,), (1,)), ((), ()))
F32 = jnp.float32
BF16 = jnp.bfloat16


def moved(array, axis, target):
    size = lax.axis_size(axis)
    pairs = [(i, target(i)) for i in range(size)]
    return lax.ppermute(array, axis, [(i, t) for i, t in pairs if t is not None and 0 <= t < size])


def vmem():
    return pl.BlockSpec(memory_space=pltpu.VMEM)


def hbm():
    return pl.BlockSpec(memory_space=pltpu.HBM)


def smem():
    return pl.BlockSpec(memory_space=pltpu.SMEM)


def params(mib):
    return pltpu.CompilerParams(vmem_limit_bytes=mib << 20)


def normed(raw, gain):
    mean_square = jnp.mean(raw * raw, axis=-1, keepdims=True)
    return raw * lax.rsqrt(mean_square + norm_eps) * gain


def message_kernel(
    kv_local, docs, table, key, value, key_gain, query_gain, bucket, out, facts
):
    core = lax.rem(lax.axis_index("ctx"), 2)
    for part in range(kv_local):
        head = part if kv_local == 1 else (core if part == 0 else 1 - core)
        lanes = pl.ds(pl.multiple_of(head * HD, HD), HD)
        rows = slice(part * BLOCK, (part + 1) * BLOCK)
        out[rows, :HD] = normed(key[:, lanes].astype(F32), key_gain[...]).astype(BF16)
        out[rows, HD:] = value[:, lanes]
    doc = jnp.full((EXTRA, 2 * HD), docs[0] + 1, jnp.int32).astype(F32)
    out[kv_local * BLOCK :, :] = doc.astype(BF16)
    facts[:8, :] = jnp.broadcast_to(query_gain[...], (8, HD))
    picks = bucket[...]
    found = jnp.zeros((1, HD), F32)
    for b in range(table.shape[0]):
        found = found + jnp.where(picks == b, table[b], 0.0)
    facts[8:, :] = jnp.broadcast_to(found, (8, HD))


def queries_kernel(
    heads,
    query,
    grad,
    facts,
    message,
    query_p,
    grad_p,
    facts_p,
    q_hat,
    rows,
    raw_t,
    both,
    kept,
):
    half = heads * HD
    core = lax.rem(lax.axis_index("ctx"), 2)
    own = pl.ds(pl.multiple_of(core * half, HD), half)
    gain = facts[0:1]
    for side in range(2):
        raw_all = query_p[:, own] if side else query[:, own]
        grad_all = grad_p[:, own] if side else grad[:, own]
        parity = 1 - core if side else core
        for head in range(heads):
            here = pl.ds(pl.multiple_of(parity * half + head * BLOCK, BLOCK), BLOCK)
            raw = raw_all[:, head * HD : (head + 1) * HD].astype(F32)
            q_hat[here, :] = normed(raw, gain).astype(BF16)
            rows[here, :] = grad_all[:, head * HD : (head + 1) * HD]
            raw_t[:, here] = raw.T.astype(BF16)
        weight = facts_p if side else facts
        both[pl.ds(pl.multiple_of(8 + 8 * parity, 8), 8), :] = weight[8:]
    both[:8, :] = facts[:8]
    kept[...] = message[...]


def attention_kernel(kv_local, heads, hops, *refs):
    n_src = hops // 2 + 1
    mine, others = refs[:n_src], refs[n_src : 2 * n_src]
    q_hat, rows, raw_t, facts, weight = refs[2 * n_src : 2 * n_src + 5]
    dq, held = refs[2 * n_src + 5 : 2 * n_src + 7]
    outs = refs[2 * n_src + 7 : 3 * n_src + 7]
    docs, keys, values, keys_t, expo, dots, pw_half, ds_half, dk, dv, sems = refs[3 * n_src + 7 :]
    half = heads * HD
    rank = lax.axis_index("ctx")
    core = lax.rem(rank, 2)
    odd_chip = lax.rem(lax.div(rank, 2), 2)

    features = pl.ds(pl.multiple_of(core * half, HD), half)
    pieces = sems.shape[0]
    part = held.shape[0] // pieces
    copies = [
        pltpu.make_async_copy(
            weight.at[pl.ds(i * part, part), features],
            held.at[pl.ds(i * part, part), :],
            sems.at[i],
        )
        for i in range(pieces)
    ]
    for copy in copies:
        copy.start()

    blocks = 2 * n_src
    chips_back = (
        0,
        jnp.where(odd_chip == 1, 1, 5),
        2,
        jnp.where(odd_chip == 1, 3, 1),
        4,
        jnp.where(odd_chip == 1, 5, 3),
    )
    after = (kv_local - 1) * BLOCK
    slots = []
    for index, back in enumerate(chips_back):
        for source, first, parity in (
            (mine[index], 0, core),
            (others[index], after, 1 - core),
        ):
            slot = 2 * (n_src - 1 - back) + parity
            at = pl.ds(pl.multiple_of(slot * BLOCK, BLOCK), BLOCK)
            key = source[first : first + BLOCK, :HD]
            keys[at, :] = key
            values[at, :] = source[first : first + BLOCK, HD:]
            keys_t[:, at] = key.astype(F32).T.astype(BF16)
            docs[slot] = source[kv_local * BLOCK :, :].astype(F32)[0:8]
            slots.append(at)

    wide = 2 * BLOCK
    reach = (blocks - 1) * BLOCK
    row = lax.broadcasted_iota(jnp.int32, (BLOCK, wide), 0)
    col = lax.rem(lax.broadcasted_iota(jnp.int32, (BLOCK, wide), 1), BLOCK)
    triangle = row <= col
    factor = SCALE * math.log2(math.e)
    gain_t = jnp.broadcast_to(facts[0:1] * SCALE, (HD, HD)).T
    gain_t = jnp.concatenate([gain_t] * 2, axis=1)
    pairs = heads // 2
    doc_rows = [docs[slot][0:1] for slot in range(blocks)]
    biases, weights = [], []
    for side in range(2):
        own_doc = doc_rows[blocks - 2 + side]
        biases.append(
            [
                jnp.where((doc == own_doc) & (doc > 0.0), 0.0, NEG)
                for doc in doc_rows[side : side + blocks - 1]
            ]
        )
        weights.append(jnp.concatenate([facts[8 * (side + 1) : 8 * (side + 1) + 1]] * 2, axis=1))

    def scores(step):
        side, here, buf = step // pairs, slice(step * wide, (step + 1) * wide), step % 2
        span = slice(side * BLOCK, side * BLOCK + reach)
        expo[buf] = lax.dot_general(
            keys[span, :], q_hat[here, :], NT, preferred_element_type=F32
        )
        dots[buf] = lax.dot_general(
            values[span, :], rows[here, :], NT, preferred_element_type=F32
        )

    def middle(step):
        side, buf = step // pairs, step % 2
        total = jnp.zeros((8, wide), F32)
        weighted = jnp.zeros((8, wide), F32)
        for block in range(blocks - 1):
            r = slice(block * BLOCK, (block + 1) * BLOCK)
            value = jnp.exp2(expo[buf, r, :] * factor + biases[side][block])
            if block == blocks - 2:
                value = jnp.where(triangle, value, 0.0)
            expo[buf, r, :] = value
            total = total + jnp.sum(value.reshape(BLOCK // 8, 8, wide), axis=0)
            weighted = weighted + jnp.sum(
                (value * dots[buf, r, :]).reshape(BLOCK // 8, 8, wide), axis=0
            )
        inverse = 1.0 / jnp.sum(total, axis=0, keepdims=True)
        shift = jnp.sum(weighted, axis=0, keepdims=True) * inverse
        level = inverse * weights[side]
        for block in range(blocks - 1):
            r = slice(block * BLOCK, (block + 1) * BLOCK)
            scaled = expo[buf, r, :] * level
            pw_half[buf, r, :] = scaled.astype(BF16)
            ds_half[buf, r, :] = (scaled * (dots[buf, r, :] - shift)).astype(BF16)

    def backward(step):
        side, here, buf = step // pairs, slice(step * wide, (step + 1) * wide), step % 2
        span = slice(side * BLOCK, side * BLOCK + reach)
        dv_part = jnp.dot(pw_half[buf], rows[here, :], preferred_element_type=F32)
        dk_part = jnp.dot(ds_half[buf], q_hat[here, :], preferred_element_type=F32)
        if step == 0:
            dv[span, :] = dv_part
            dk[span, :] = dk_part
            dv[reach:, :] = jnp.zeros((BLOCK, HD), F32)
            dk[reach:, :] = jnp.zeros((BLOCK, HD), F32)
        else:
            dv[span, :] += dv_part
            dk[span, :] += dk_part
        dq_t = jnp.dot(keys_t[:, span], ds_half[buf], preferred_element_type=F32)
        x = raw_t[:, here].astype(F32)
        inverse = lax.rsqrt(jnp.mean(x * x, axis=0, keepdims=True) + norm_eps)
        dy = dq_t * gain_t
        inner = jnp.mean(x * dy, axis=0, keepdims=True)
        dx = inverse * dy - x * (inverse * inverse * inverse * inner)
        for part in range(2):
            at = (step % pairs) * wide + part * HD
            dq[at : at + HD, side * BLOCK : (side + 1) * BLOCK] = dx[
                :, part * BLOCK : (part + 1) * BLOCK
            ].astype(BF16)

    steps = 2 * pairs
    scores(0)
    for step in range(steps):
        if step + 1 < steps:
            scores(step + 1)
        middle(step)
        backward(step)

    for index, out in enumerate(outs):
        for block in range(2):
            at = slots[2 * index + block]
            r = slice(block * BLOCK, (block + 1) * BLOCK)
            out[r, :HD] = (dk[at, :] * SCALE).astype(out.dtype)
            out[r, HD:] = dv[at, :].astype(out.dtype)
    for copy in copies:
        copy.wait()


def project_kernel(width, where, dq, weight, keep, send):
    core = lax.rem(lax.axis_index("ctx"), 2)
    rows = min(256, width)
    for i in range(width // rows):
        lanes = slice(i * rows, (i + 1) * rows)
        at = pl.ds(pl.multiple_of(where[0] * width + i * rows, rows), rows)
        term = jnp.dot(weight[at, :], dq[...], preferred_element_type=F32).T
        even, odd = term[:BLOCK], term[BLOCK:]
        keep[:, lanes] = jnp.where(core == 0, even, odd).astype(keep.dtype)
        send[:, lanes] = jnp.where(core == 0, odd, even).astype(send.dtype)


def project(dq, weight, slice_index, width):
    tokens = dq.shape[1]
    out = jax.ShapeDtypeStruct((tokens // 2, width), BF16)
    return pl.pallas_call(
        functools.partial(project_kernel, width),
        in_specs=[smem(), vmem(), vmem()],
        out_specs=[vmem()] * 2,
        out_shape=[out, out],
        compiler_params=params(16),
        cost_estimate=pl.CostEstimate(flops=1, bytes_accessed=1, transcendentals=0),
    )(slice_index.reshape(1).astype(jnp.int32), dq, weight)


def add_kernel(a, b, out):
    out[...] = (a[...].astype(F32) + b[...].astype(F32)).astype(out.dtype)


def add_three_kernel(a, b, c, out):
    out[...] = (a[...].astype(F32) + b[...].astype(F32) + c[...].astype(F32)).astype(out.dtype)


def collect_kernel(part_own, a, b, c, d, e, keep, send):
    result = part_own[...]
    for back in (a, b, c, d, e):
        result = result + back[...].astype(F32)
    keep[...] = result[:BLOCK]
    send[...] = result[BLOCK:].astype(BF16)


def finish_kernel(
    kv_local, keep, recv, key, gain, grad_key, grad_value, key_v, gain_v, sems
):
    copies = [
        pltpu.make_async_copy(key, key_v, sems.at[0]),
        pltpu.make_async_copy(gain, gain_v, sems.at[1]),
    ]
    for copy in copies:
        copy.start()
    for copy in copies:
        copy.wait()
    core = lax.rem(lax.axis_index("ctx"), 2)
    if kv_local > 1:
        parts = [(core, keep[...]), (1 - core, recv[...].astype(F32))]
    else:
        parts = [(0, keep[...] + recv[...].astype(F32))]
    for head, part in parts:
        lanes = pl.ds(pl.multiple_of(head * HD, HD), HD)
        raw = key_v[:, lanes].astype(F32)
        inverse = lax.rsqrt(jnp.mean(raw * raw, axis=-1, keepdims=True) + norm_eps)
        dy = part[:, :HD] * gain_v[...]
        inner = jnp.mean(raw * dy, axis=-1, keepdims=True)
        dx = inverse * dy - raw * (inverse * inverse * inverse * inner)
        grad_key[:, lanes] = dx.astype(BF16)
        grad_value[:, lanes] = part[:, HD:].astype(BF16)


def local(
    query_raw,
    key_raw,
    value_in,
    grad_out,
    query_gain,
    key_gain,
    loss_table,
    loss_bucket,
    block_docs,
    query_weight,
):
    tokens = query_raw.shape[0]
    kv_local = key_raw.shape[1] // HD
    half = query_raw.shape[1] // 2
    heads = half // HD
    key_row = key_gain.reshape(1, HD)
    query_row = query_gain.reshape(1, HD)
    shape = jax.ShapeDtypeStruct

    partner = lambda i: i ^ 1
    message, facts = pl.pallas_call(
        functools.partial(message_kernel, kv_local),
        in_specs=[smem(), smem()] + [vmem()] * 5,
        out_specs=[vmem()] * 2,
        out_shape=[
            shape((kv_local * BLOCK + EXTRA, 2 * HD), BF16),
            shape((16, HD), F32),
        ],
    )(
        block_docs,
        loss_table,
        key_raw,
        value_in,
        key_row,
        query_row,
        loss_bucket.reshape(1, tokens),
    )

    far_d = moved(message, "ctx", lambda i: i + 8)
    far_b = moved(message, "ctx", lambda i: i + 4)
    far_a = moved(message, "ctx", lambda i: i + 2 if (i // 2) % 2 == 0 else i + 10)
    query_in, grad_in, _ = lax.optimization_barrier((query_raw, grad_out, message))
    query_p = moved(query_in, "ctx", partner)
    grad_p = moved(grad_in, "ctx", partner)
    facts_p = moved(facts, "ctx", partner)
    total = 2 * heads * BLOCK
    queries = pl.pallas_call(
        functools.partial(queries_kernel, heads),
        in_specs=[vmem()] * 7,
        out_specs=[vmem()] * 5,
        out_shape=[
            shape((total, HD), BF16),
            shape((total, HD), BF16),
            shape((HD, total), BF16),
            shape((24, HD), F32),
            shape(message.shape, BF16),
        ],
        compiler_params=params(16),
    )(query_in, grad_in, facts, message, query_p, grad_p, facts_p)
    far_c = moved(far_b, "ctx", lambda i: i ^ 2)
    far_d, *queries = lax.optimization_barrier((far_d, *queries))
    far_e = moved(far_d, "ctx", lambda i: i ^ 2)
    *queries, kept = queries
    sources = (kept, far_a, far_b, far_c, far_d, far_e)
    shared = [moved(source, "ctx", partner) for source in (message, *sources[1:])]

    span = 2 * BLOCK
    n_rows = 6 * span
    far_shape = shape((span, 2 * HD), BF16)
    reach = n_rows - BLOCK
    dq, weight, part_own, part_a, part_b, part_c, part_d, part_e = pl.pallas_call(
        functools.partial(attention_kernel, kv_local, heads, HOPS),
        in_specs=[vmem()] * 16 + [hbm()],
        out_specs=[vmem()] * 8,
        out_shape=[
            shape((half, 2 * tokens), BF16),
            shape((query_weight.shape[0], half), BF16),
            shape((span, 2 * HD), F32),
        ]
        + [far_shape] * 5,
        scratch_shapes=[
            pltpu.VMEM((12, 8, 2 * HD), F32),
            pltpu.VMEM((n_rows, HD), BF16),
            pltpu.VMEM((n_rows, HD), BF16),
            pltpu.VMEM((HD, n_rows), BF16),
            pltpu.VMEM((2, reach, span), F32),
            pltpu.VMEM((2, reach, span), F32),
            pltpu.VMEM((2, reach, span), BF16),
            pltpu.VMEM((2, reach, span), BF16),
            pltpu.VMEM((n_rows, HD), F32),
            pltpu.VMEM((n_rows, HD), F32),
            pltpu.SemaphoreType.DMA((4,)),
        ],
        compiler_params=params(36),
    )(*sources, *shared, *queries, query_weight)

    n_head = lax.axis_size("head")
    head = lax.axis_index("head")
    width = query_weight.shape[0] // n_head
    term_shape = shape((tokens, width), BF16)
    arrived = []
    for shift in range(1, n_head):
        keep, send = project(dq, weight, (head + shift) % n_head, width)
        recv = moved(send, "ctx", partner)
        term = pl.pallas_call(
            add_kernel,
            in_specs=[vmem()] * 2,
            out_specs=vmem(),
            out_shape=term_shape,
            compiler_params=params(16),
        )(keep, recv)
        arrived.append(moved(term, "head", lambda i, s=shift: (i + s) % n_head))
    dq, weight, part_a, part_b, part_c, _ = lax.optimization_barrier(
        (dq, weight, part_a, part_b, part_c, term)
    )
    mine, mine_send = project(dq, weight, head, width)
    mine_recv = moved(mine_send, "ctx", partner)

    back_d = moved(part_d, "ctx", lambda i: i - 8)
    back_e = moved(part_e, "ctx", lambda i: (i ^ 2) - 8)
    back_c = moved(part_c, "ctx", lambda i: (i ^ 2) - 4)
    back_b = moved(part_b, "ctx", lambda i: i - 4)
    back_a = moved(part_a, "ctx", lambda i: i - 2 if (i // 2) % 2 == 1 else i - 10)
    grad_input = mine
    for index, piece in enumerate(arrived):
        last = index == len(arrived) - 1
        grad_input = pl.pallas_call(
            add_three_kernel if last else add_kernel,
            in_specs=[vmem()] * (3 if last else 2),
            out_specs=vmem(),
            out_shape=shape((tokens, width), BF16 if last else F32),
            compiler_params=params(16),
        )(grad_input, *([mine_recv] if last else []), piece)
    back_a, grad_input = lax.optimization_barrier((back_a, grad_input))
    sum_keep, sum_send = pl.pallas_call(
        collect_kernel,
        in_specs=[vmem()] * 6,
        out_specs=[vmem()] * 2,
        out_shape=[shape((BLOCK, 2 * HD), F32), shape((BLOCK, 2 * HD), BF16)],
        compiler_params=params(16),
    )(part_own, back_a, back_b, back_c, back_d, back_e)
    sum_recv = moved(sum_send, "ctx", partner)
    grad_key, grad_value = pl.pallas_call(
        functools.partial(finish_kernel, kv_local),
        in_specs=[vmem(), vmem(), hbm(), hbm()],
        out_specs=[vmem()] * 2,
        out_shape=[shape(key_raw.shape, BF16), shape(value_in.shape, BF16)],
        scratch_shapes=[
            pltpu.VMEM(key_raw.shape, BF16),
            pltpu.VMEM((1, HD), F32),
            pltpu.SemaphoreType.DMA((2,)),
        ],
        compiler_params=params(16),
    )(sum_keep, sum_recv, key_raw, key_row)

    return grad_input, grad_key, grad_value


def solution(mesh):
    placed = (
        P("ctx", "head"),
        P("ctx", "head"),
        P("ctx", "head"),
        P("ctx", "head"),
        P(),
        P(),
        P(),
        P("ctx"),
        P("ctx"),
        P(None, "head"),
    )
    return jax.shard_map(
        local,
        mesh=mesh,
        in_specs=placed,
        out_specs=(P("ctx", "head"), P("ctx", "head"), P("ctx", "head")),
        check_vma=False,
    )
```

```python
import functools
import math

import jax
import jax.numpy as jnp
from jax import lax
from jax.experimental import pallas as pl
from jax.experimental.pallas import tpu as pltpu
from jax.sharding import PartitionSpec as P

HD = 128
BLOCK = 128
EXTRA = 16
norm_eps = 1e-06
SCALE = HD ** (-0.5)
NEG = -1e30
NT = (((1,), (1,)), ((), ()))
F32 = jnp.float32
BF16 = jnp.bfloat16
SMALL = pl.CostEstimate(flops=1, bytes_accessed=1, transcendentals=0)


def moved(array, axis, target):
    size = lax.axis_size(axis)
    pairs = [(i, target(i)) for i in range(size)]
    return lax.ppermute(array, axis, [(i, t) for i, t in pairs if t is not None and 0 <= t < size])


def vmem():
    return pl.BlockSpec(memory_space=pltpu.VMEM)


def hbm():
    return pl.BlockSpec(memory_space=pltpu.HBM)


def smem():
    return pl.BlockSpec(memory_space=pltpu.SMEM)


def params(mib):
    return pltpu.CompilerParams(vmem_limit_bytes=mib << 20)


def normed(raw, gain):
    mean_square = jnp.mean(raw * raw, axis=-1, keepdims=True)
    return raw * lax.rsqrt(mean_square + norm_eps) * gain


def message_kernel(
    kv_local, docs, table, key, value, key_gain, query_gain, bucket, out, facts
):
    core = lax.rem(lax.axis_index("ctx"), 2)
    for part in range(kv_local):
        head = part if kv_local == 1 else (core if part == 0 else 1 - core)
        lanes = pl.ds(pl.multiple_of(head * HD, HD), HD)
        rows = slice(part * BLOCK, (part + 1) * BLOCK)
        out[rows, :HD] = normed(key[:, lanes].astype(F32), key_gain[...]).astype(BF16)
        out[rows, HD:] = value[:, lanes]
    doc = jnp.full((EXTRA, 2 * HD), docs[0] + 1, jnp.int32).astype(F32)
    out[kv_local * BLOCK :, :] = doc.astype(BF16)
    facts[:8, :] = jnp.broadcast_to(query_gain[...], (8, HD))
    picks = bucket[...]
    found = jnp.zeros((1, HD), F32)
    for b in range(table.shape[0]):
        found = found + jnp.where(picks == b, table[b], 0.0)
    facts[8:, :] = jnp.broadcast_to(found, (8, HD))


def fetch(weight, held, sems, heads):
    n_head = lax.axis_size("head")
    width = weight.shape[0] // n_head
    core = lax.rem(lax.axis_index("ctx"), 2)
    features = pl.ds(pl.multiple_of(core * heads * HD, HD), heads * HD)
    pieces = sems.shape[0] // n_head
    part = width // pieces
    copies = []
    for i in range(sems.shape[0]):
        owner = lax.rem(lax.axis_index("head") + i // pieces, n_head)
        at = pl.multiple_of(owner * width + (i % pieces) * part, part)
        copies.append(
            pltpu.make_async_copy(
                weight.at[pl.ds(at, part), features],
                held.at[pl.ds(i * part, part), :],
                sems.at[i],
            )
        )
        copies[-1].start()
    return copies


def queries_kernel(
    heads,
    query,
    grad,
    facts,
    message,
    query_p,
    grad_p,
    facts_p,
    q_hat,
    rows,
    raw_t,
    both,
    kept,
):
    half = heads * HD
    core = lax.rem(lax.axis_index("ctx"), 2)
    own = pl.ds(pl.multiple_of(core * half, HD), half)
    gain = facts[0:1]
    for side in range(2):
        raw_all = query_p[:, own] if side else query[:, own]
        grad_all = grad_p[:, own] if side else grad[:, own]
        parity = 1 - core if side else core
        for head in range(heads):
            here = pl.ds(pl.multiple_of(parity * half + head * BLOCK, BLOCK), BLOCK)
            raw = raw_all[:, head * HD : (head + 1) * HD].astype(F32)
            q_hat[here, :] = normed(raw, gain).astype(BF16)
            rows[here, :] = grad_all[:, head * HD : (head + 1) * HD]
            raw_t[:, here] = raw.T.astype(BF16)
        source = facts_p if side else facts
        both[pl.ds(pl.multiple_of(8 + 8 * parity, 8), 8), :] = source[8:]
    both[:8, :] = facts[:8]
    kept[...] = message[...]


def place(kv_local, source, other, first, core, keys, values, keys_t, docs):
    after = (kv_local - 1) * BLOCK
    for block, skip, parity in ((source, 0, core), (other, after, 1 - core)):
        at = pl.ds(pl.multiple_of((first + parity) * BLOCK, BLOCK), BLOCK)
        key = block[skip : skip + BLOCK, :HD]
        keys[at, :] = key
        values[at, :] = block[skip : skip + BLOCK, HD:]
        keys_t[:, at] = key.astype(F32).T.astype(BF16)
        docs[first + parity] = block[kv_local * BLOCK :, :].astype(F32)[0:8]


def masks(own_doc, docs):
    return [jnp.where((doc == own_doc) & (doc > 0.0), 0.0, NEG) for doc in docs]


def exponents(scores, expo, dots, at, bias, triangle, total, weighted):
    value = jnp.exp2(scores * (SCALE * math.log2(math.e)) + bias)
    if triangle is not None:
        value = jnp.where(triangle, value, 0.0)
    expo[at] = value.astype(expo.dtype)
    wide = value.shape[1]
    total = total + jnp.sum(value.reshape(BLOCK // 8, 8, wide), axis=0)
    weighted = weighted + jnp.sum((value * dots[at]).reshape(BLOCK // 8, 8, wide), axis=0)
    return total, weighted


def near_kernel(kv_local, heads, n_near, *refs):
    mine, others = refs[:n_near], refs[n_near : 2 * n_near]
    q_hat, rows, weight = refs[2 * n_near : 2 * n_near + 3]
    held, keys_t, expo, dots, sums, keys, values, docs, raw, sems = refs[2 * n_near + 3 :]
    core = lax.rem(lax.axis_index("ctx"), 2)

    copies = fetch(weight, held, sems, heads)
    blocks = 2 * n_near
    for index in range(n_near):
        first = blocks - 2 - 2 * index
        place(kv_local, mine[index], others[index], first, core, keys, values, keys_t, docs)
    wide = 2 * BLOCK
    row = lax.broadcasted_iota(jnp.int32, (BLOCK, wide), 0)
    col = lax.rem(lax.broadcasted_iota(jnp.int32, (BLOCK, wide), 1), BLOCK)
    triangle = row <= col
    doc_rows = [docs[slot][0:1] for slot in range(blocks)]
    pairs = heads // 2
    for side in range(2):
        count = blocks - 1 + side
        reach = count * BLOCK
        bias = masks(doc_rows[blocks - 2 + side], doc_rows[:count])
        for pair in range(pairs):
            step = side * pairs + pair
            here = slice(step * wide, (step + 1) * wide)
            raw[step % 2, :reach, :] = lax.dot_general(
                keys[:reach, :], q_hat[here, :], NT, preferred_element_type=F32
            )
            dots[step, :reach, :] = lax.dot_general(
                values[:reach, :], rows[here, :], NT, preferred_element_type=F32
            )
            total = jnp.zeros((8, wide), F32)
            weighted = jnp.zeros((8, wide), F32)
            for block in range(count):
                r = slice(block * BLOCK, (block + 1) * BLOCK)
                total, weighted = exponents(
                    raw[step % 2, r, :],
                    expo,
                    dots,
                    (step, r, slice(None)),
                    bias[block],
                    triangle if block == count - 1 else None,
                    total,
                    weighted,
                )
            sums[step, :8, :] = total
            sums[step, 8:, :] = weighted
    for copy in copies:
        copy.wait()


def sum_products(step, side_rows, dk, dv, pw, ds, q_two, g_two):
    span = slice(0, side_rows)
    dv_part = jnp.dot(pw, g_two, preferred_element_type=F32)
    dk_part = jnp.dot(ds, q_two, preferred_element_type=F32)
    if step == 0:
        dv[span, :] = dv_part
        dk[span, :] = dk_part
        if side_rows < dk.shape[0]:
            dv[side_rows:, :] = jnp.zeros((dk.shape[0] - side_rows, HD), F32)
            dk[side_rows:, :] = jnp.zeros((dk.shape[0] - side_rows, HD), F32)
    else:
        dv[span, :] += dv_part
        dk[span, :] += dk_part


def hand_out(core, firsts, outs, dk, dv):
    for first, out in zip(firsts, outs):
        for block, parity in ((0, core), (1, 1 - core)):
            at = pl.ds(pl.multiple_of((first + parity) * BLOCK, BLOCK), BLOCK)
            r = slice(block * BLOCK, (block + 1) * BLOCK)
            out[r, :HD] = (dk[at, :] * SCALE).astype(out.dtype)
            out[r, HD:] = dv[at, :].astype(out.dtype)


def far_kernel(kv_local, heads, n_near, n_far, *refs):
    mine, others = refs[: 1 + n_far], refs[1 + n_far : 2 + 2 * n_far]
    q_hat, rows, facts, near_expo, near_dots, sums = refs[2 + 2 * n_far : 8 + 2 * n_far]
    keys_t, pw_near, ds, *parts = refs[8 + 2 * n_far : 13 + 2 * n_far]
    keys, values, docs, expo, dots, pw_far, dk, dv = refs[13 + 2 * n_far :]
    core = lax.rem(lax.axis_index("ctx"), 2)
    blocks = 2 * n_far
    for index in range(n_far):
        source, other = mine[1 + index], others[1 + index]
        place(kv_local, source, other, 2 * index, core, keys, values, keys_t, docs)
    for source, parity in ((mine[0], core), (others[0], 1 - core)):
        docs[blocks + parity] = source[kv_local * BLOCK :, :].astype(F32)[0:8]
    wide = 2 * BLOCK
    far_rows = blocks * BLOCK
    doc_rows = [docs[slot][0:1] for slot in range(blocks + 2)]
    pairs = heads // 2
    steps = 2 * pairs
    biases, weights = [], []
    for side in range(2):
        biases.append(masks(doc_rows[blocks + side], doc_rows[:blocks]))
        weights.append(jnp.concatenate([facts[8 * (side + 1) : 8 * (side + 1) + 1]] * 2, axis=1))

    def scores(step):
        here, buf = slice(step * wide, (step + 1) * wide), step % 2
        expo[buf] = lax.dot_general(keys[...], q_hat[here, :], NT, preferred_element_type=F32)
        dots[buf] = lax.dot_general(values[...], rows[here, :], NT, preferred_element_type=F32)

    def middle(step):
        side, buf = step // pairs, step % 2
        total, weighted = sums[step, :8, :], sums[step, 8:, :]
        for block in range(blocks):
            at = (buf, slice(block * BLOCK, (block + 1) * BLOCK), slice(None))
            total, weighted = exponents(
                expo[at], expo, dots, at, biases[side][block], None, total, weighted
            )
        inverse = 1.0 / jnp.sum(total, axis=0, keepdims=True)
        shift = jnp.sum(weighted, axis=0, keepdims=True) * inverse
        level = inverse * weights[side]
        for block in range(blocks):
            r = slice(block * BLOCK, (block + 1) * BLOCK)
            scaled = expo[buf, r, :] * level
            pw_far[buf, r, :] = scaled.astype(BF16)
            ds[step, r, :] = (scaled * (dots[buf, r, :] - shift)).astype(BF16)
        for block in range(2 * n_near - 1 + side):
            r = slice(block * BLOCK, (block + 1) * BLOCK)
            scaled = near_expo[step, r, :].astype(F32) * level
            pw_near[step, r, :] = scaled.astype(BF16)
            to = slice(far_rows + block * BLOCK, far_rows + (block + 1) * BLOCK)
            ds[step, to, :] = (scaled * (near_dots[step, r, :] - shift)).astype(BF16)

    scores(0)
    for step in range(steps):
        if step + 1 < steps:
            scores(step + 1)
        middle(step)
        here = slice(step * wide, (step + 1) * wide)
        sum_products(
            step,
            far_rows,
            dk,
            dv,
            pw_far[step % 2],
            ds[step, :far_rows, :],
            q_hat[here, :],
            rows[here, :],
        )
    part_a, part_ce = parts
    span = 2 * BLOCK
    outs = [part_a, part_ce.at[:span, :], part_ce.at[span:, :]]
    hand_out(core, [2 * index for index in range(n_far)], outs, dk, dv)


def last_kernel(heads, n_near, n_far, *refs):
    q_hat, rows, raw_t, facts, near_t, far_t, pw_near, ds = refs[:8]
    dq, *parts = refs[8 : 9 + n_near]
    dk, dv = refs[9 + n_near :]
    core = lax.rem(lax.axis_index("ctx"), 2)
    wide = 2 * BLOCK
    far_rows = 2 * n_far * BLOCK
    gain_t = jnp.broadcast_to(facts[0:1] * SCALE, (HD, HD)).T
    gain_t = jnp.concatenate([gain_t] * 2, axis=1)
    pairs = heads // 2
    for step in range(2 * pairs):
        side, here = step // pairs, slice(step * wide, (step + 1) * wide)
        reach = (2 * n_near - 1 + side) * BLOCK
        to = slice(far_rows, far_rows + reach)
        sum_products(
            step,
            reach,
            dk,
            dv,
            pw_near[step, :reach, :],
            ds[step, to, :],
            q_hat[here, :],
            rows[here, :],
        )
        dq_t = jnp.dot(far_t[...], ds[step, :far_rows, :], preferred_element_type=F32)
        dq_t = dq_t + jnp.dot(near_t[:, :reach], ds[step, to, :], preferred_element_type=F32)
        x = raw_t[:, here].astype(F32)
        inverse = lax.rsqrt(jnp.mean(x * x, axis=0, keepdims=True) + norm_eps)
        dy = dq_t * gain_t
        inner = jnp.mean(x * dy, axis=0, keepdims=True)
        dx = inverse * dy - x * (inverse * inverse * inverse * inner)
        for part in range(2):
            at = (step % pairs) * wide + part * HD
            dq[at : at + HD, side * BLOCK : (side + 1) * BLOCK] = dx[
                :, part * BLOCK : (part + 1) * BLOCK
            ].astype(BF16)
    firsts = [2 * n_near - 2 - 2 * index for index in range(n_near)]
    hand_out(core, firsts, parts, dk, dv)


def project_kernel(first, dq, weight, keep, *sends):
    core = lax.rem(lax.axis_index("ctx"), 2)
    width = keep.shape[1]
    piece = width // len(sends)
    rows = min(256, piece)
    for i in range(width // rows):
        lanes = slice(i * rows, (i + 1) * rows)
        at = slice(first + i * rows, first + (i + 1) * rows)
        term = jnp.dot(weight[at, :], dq[...], preferred_element_type=F32).T
        even, odd = term[:BLOCK], term[BLOCK:]
        keep[:, lanes] = jnp.where(core == 0, even, odd).astype(keep.dtype)
        send = sends[i * rows // piece]
        inside = slice(i * rows % piece, i * rows % piece + rows)
        send[:, inside] = jnp.where(core == 0, odd, even).astype(send.dtype)


def project(dq, weight, first, width, pieces):
    tokens = dq.shape[1] // 2
    keep = jax.ShapeDtypeStruct((tokens, width), BF16)
    send = jax.ShapeDtypeStruct((tokens, width // pieces), BF16)
    return pl.pallas_call(
        functools.partial(project_kernel, first),
        in_specs=[vmem()] * 2,
        out_specs=[vmem()] * (1 + pieces),
        out_shape=[keep] + [send] * pieces,
        compiler_params=params(16),
        cost_estimate=SMALL,
    )(dq, weight)


def add_kernel(*refs):
    *terms, out = refs
    result = terms[0][...].astype(F32)
    for term in terms[1:]:
        result = result + term[...].astype(F32)
    out[...] = result.astype(out.dtype)


def add_pieces_kernel(whole, *refs):
    *pieces, out = refs
    width = pieces[0].shape[1]
    for i, piece in enumerate(pieces):
        lanes = slice(i * width, (i + 1) * width)
        out[:, lanes] = (whole[:, lanes].astype(F32) + piece[...].astype(F32)).astype(out.dtype)


def add_pieces(whole, pieces):
    return pl.pallas_call(
        add_pieces_kernel,
        in_specs=[vmem()] * (1 + len(pieces)),
        out_specs=vmem(),
        out_shape=jax.ShapeDtypeStruct(whole.shape, whole.dtype),
        compiler_params=params(16),
        cost_estimate=SMALL,
    )(whole, *pieces)


def add(first, second, dtype, *more):
    return pl.pallas_call(
        add_kernel,
        in_specs=[vmem()] * (2 + len(more)),
        out_specs=vmem(),
        out_shape=jax.ShapeDtypeStruct(first.shape, dtype),
        compiler_params=params(16),
        cost_estimate=SMALL,
    )(first, second, *more)


def two_sums_kernel(b, d, turn, sum_b, sum_d):
    half = turn.shape[0] // 2
    sum_b[...] = (b[...].astype(F32) + turn[:half].astype(F32)).astype(sum_b.dtype)
    sum_d[...] = (d[...].astype(F32) + turn[half:].astype(F32)).astype(sum_d.dtype)


def collect_kernel(part_own, a, b, d, keep, send):
    result = part_own[...]
    for back in (a, b, d):
        result = result + back[...].astype(F32)
    keep[...] = result[:BLOCK]
    send[...] = result[BLOCK:].astype(BF16)


def finish_kernel(
    kv_local, keep, recv, key, gain, grad_key, grad_value, key_v, gain_v, sems
):
    copies = [
        pltpu.make_async_copy(key, key_v, sems.at[0]),
        pltpu.make_async_copy(gain, gain_v, sems.at[1]),
    ]
    for copy in copies:
        copy.start()
    for copy in copies:
        copy.wait()
    core = lax.rem(lax.axis_index("ctx"), 2)
    if kv_local > 1:
        parts = [(core, keep[...]), (1 - core, recv[...].astype(F32))]
    else:
        parts = [(0, keep[...] + recv[...].astype(F32))]
    for head, part in parts:
        lanes = pl.ds(pl.multiple_of(head * HD, HD), HD)
        raw = key_v[:, lanes].astype(F32)
        inverse = lax.rsqrt(jnp.mean(raw * raw, axis=-1, keepdims=True) + norm_eps)
        dy = part[:, :HD] * gain_v[...]
        inner = jnp.mean(raw * dy, axis=-1, keepdims=True)
        dx = inverse * dy - raw * (inverse * inverse * inverse * inner)
        grad_key[:, lanes] = dx.astype(BF16)
        grad_value[:, lanes] = part[:, HD:].astype(BF16)


def local(
    query_raw,
    key_raw,
    value_in,
    grad_out,
    query_gain,
    key_gain,
    loss_table,
    loss_bucket,
    block_docs,
    query_weight,
):
    tokens = query_raw.shape[0]
    kv_local = key_raw.shape[1] // HD
    half = query_raw.shape[1] // 2
    heads = half // HD
    key_row = key_gain.reshape(1, HD)
    query_row = query_gain.reshape(1, HD)
    shape = jax.ShapeDtypeStruct
    n_head = lax.axis_size("head")
    width = query_weight.shape[0] // n_head

    partner = lambda i: i ^ 1
    message, facts = pl.pallas_call(
        functools.partial(message_kernel, kv_local),
        in_specs=[smem(), smem()] + [vmem()] * 5,
        out_specs=[vmem()] * 2,
        out_shape=[
            shape((kv_local * BLOCK + EXTRA, 2 * HD), BF16),
            shape((16, HD), F32),
        ],
    )(
        block_docs,
        loss_table,
        key_raw,
        value_in,
        key_row,
        query_row,
        loss_bucket.reshape(1, tokens),
    )

    far_d = moved(message, "ctx", lambda i: i + 8)
    far_b = moved(message, "ctx", lambda i: i + 4)
    far_a = moved(message, "ctx", lambda i: i + 2 if (i // 2) % 2 == 0 else i + 10)
    query_in, grad_in, _ = lax.optimization_barrier((query_raw, grad_out, message))
    query_p = moved(query_in, "ctx", partner)
    grad_p = moved(grad_in, "ctx", partner)
    facts_p = moved(facts, "ctx", partner)
    total = 2 * heads * BLOCK
    queries = pl.pallas_call(
        functools.partial(queries_kernel, heads),
        in_specs=[vmem()] * 7,
        out_specs=[vmem()] * 5,
        out_shape=[
            shape((total, HD), BF16),
            shape((total, HD), BF16),
            shape((HD, total), BF16),
            shape((24, HD), F32),
            shape(message.shape, BF16),
        ],
        compiler_params=params(16),
    )(query_in, grad_in, facts, message, query_p, grad_p, facts_p)
    far_c = moved(far_b, "ctx", lambda i: i ^ 2 if i >= 4 else None)
    far_d, *queries = lax.optimization_barrier((far_d, *queries))
    far_e = moved(far_d, "ctx", lambda i: i ^ 2 if i >= 8 else None)
    *queries, kept = queries
    q_hat, rows, raw_t, both = queries
    near = (kept, far_b, far_d)
    near_shared = [moved(source, "ctx", partner) for source in (message, far_b, far_d)]
    n_near, n_far = 3, 3
    steps = heads
    span = 2 * BLOCK
    near_rows, far_rows = n_near * span, n_far * span
    weight, near_t, near_expo, near_dots, sums = pl.pallas_call(
        functools.partial(near_kernel, kv_local, heads, n_near),
        in_specs=[vmem()] * (2 * n_near + 2) + [hbm()],
        out_specs=[vmem()] * 5,
        out_shape=[
            shape((query_weight.shape[0], half), BF16),
            shape((HD, near_rows), BF16),
            shape((steps, near_rows, span), BF16),
            shape((steps, near_rows, span), F32),
            shape((steps, 16, span), F32),
        ],
        scratch_shapes=[
            pltpu.VMEM((near_rows, HD), BF16),
            pltpu.VMEM((near_rows, HD), BF16),
            pltpu.VMEM((2 * n_near, 8, 2 * HD), F32),
            pltpu.VMEM((2, near_rows, span), F32),
            pltpu.SemaphoreType.DMA((2 * n_head,)),
        ],
        compiler_params=params(20),
    )(*near, *near_shared, q_hat, rows, query_weight)

    far_e, sums = lax.optimization_barrier((far_e, sums))
    far = (far_a, far_c, far_e)
    far_shared = [moved(source, "ctx", partner) for source in far]
    part_shape = shape((span, 2 * HD), BF16)
    far_t, pw_near, ds, part_a, part_ce = pl.pallas_call(
        functools.partial(far_kernel, kv_local, heads, n_near, n_far),
        in_specs=[vmem()] * (2 * n_far + 8),
        out_specs=[vmem()] * 5,
        out_shape=[
            shape((HD, far_rows), BF16),
            shape((steps, near_rows, span), BF16),
            shape((steps, far_rows + near_rows, span), BF16),
            part_shape,
            shape((2 * span, 2 * HD), BF16),
        ],
        input_output_aliases={2 * n_far + 5: 1},
        scratch_shapes=[
            pltpu.VMEM((far_rows, HD), BF16),
            pltpu.VMEM((far_rows, HD), BF16),
            pltpu.VMEM((2 * n_far + 2, 8, 2 * HD), F32),
            pltpu.VMEM((2, far_rows, span), F32),
            pltpu.VMEM((2, far_rows, span), F32),
            pltpu.VMEM((2, far_rows, span), BF16),
            pltpu.VMEM((far_rows, HD), F32),
            pltpu.VMEM((far_rows, HD), F32),
        ],
        compiler_params=params(20),
        cost_estimate=SMALL,
    )(
        kept,
        *far,
        near_shared[0],
        *far_shared,
        q_hat,
        rows,
        both,
        near_expo,
        near_dots,
        sums,
    )

    back_a = moved(part_a, "ctx", lambda i: i - 2 if (i // 2) % 2 == 1 else i - 10)
    turn = moved(part_ce, "ctx", lambda i: i ^ 2 if i >= 4 else None)

    dq, part_own, part_b, part_d = pl.pallas_call(
        functools.partial(last_kernel, heads, n_near, n_far),
        in_specs=[vmem()] * 8,
        out_specs=[vmem()] * 4,
        out_shape=[shape((half, 2 * tokens), BF16), shape((span, 2 * HD), F32)] + [part_shape] * 2,
        scratch_shapes=[pltpu.VMEM((near_rows, HD), F32)] * 2,
        compiler_params=params(20),
        cost_estimate=SMALL,
    )(q_hat, rows, raw_t, both, near_t, far_t, pw_near, ds)

    arrived = []
    for shift in range(1, n_head):
        keep, *sends = project(dq, weight, shift * width, width, 4)
        term = add_pieces(keep, [moved(send, "ctx", partner) for send in sends])
        term, turn = lax.optimization_barrier((term, turn))
        arrived.append(moved(term, "head", lambda i, s=shift: (i + s) % n_head))
    sum_b, sum_d = pl.pallas_call(
        two_sums_kernel,
        in_specs=[vmem()] * 3,
        out_specs=[vmem()] * 2,
        out_shape=[part_shape] * 2,
        compiler_params=params(16),
        cost_estimate=SMALL,
    )(part_b, part_d, turn)
    back_d = moved(sum_d, "ctx", lambda i: i - 8)
    back_b = moved(sum_b, "ctx", lambda i: i - 4)
    mine, mine_send = project(dq, weight, 0, width, 1)
    mine_recv = moved(mine_send, "ctx", partner)

    grad_input = mine
    for index, piece in enumerate(arrived):
        last = index == len(arrived) - 1
        grad_input = add(grad_input, piece, BF16 if last else F32, *([mine_recv] if last else []))
    back_b, grad_input = lax.optimization_barrier((back_b, grad_input))
    sum_keep, sum_send = pl.pallas_call(
        collect_kernel,
        in_specs=[vmem()] * 4,
        out_specs=[vmem()] * 2,
        out_shape=[shape((BLOCK, 2 * HD), F32), shape((BLOCK, 2 * HD), BF16)],
        compiler_params=params(16),
    )(part_own, back_a, back_b, back_d)
    sum_recv = moved(sum_send, "ctx", partner)
    grad_key, grad_value = pl.pallas_call(
        functools.partial(finish_kernel, kv_local),
        in_specs=[vmem(), vmem(), hbm(), hbm()],
        out_specs=[vmem()] * 2,
        out_shape=[shape(key_raw.shape, BF16), shape(value_in.shape, BF16)],
        scratch_shapes=[
            pltpu.VMEM(key_raw.shape, BF16),
            pltpu.VMEM((1, HD), F32),
            pltpu.SemaphoreType.DMA((2,)),
        ],
        compiler_params=params(16),
    )(sum_keep, sum_recv, key_raw, key_row)

    return grad_input, grad_key, grad_value


def solution(mesh):
    placed = (
        P("ctx", "head"),
        P("ctx", "head"),
        P("ctx", "head"),
        P("ctx", "head"),
        P(),
        P(),
        P(),
        P("ctx"),
        P("ctx"),
        P(None, "head"),
    )
    return jax.shard_map(
        local,
        mesh=mesh,
        in_specs=placed,
        out_specs=(P("ctx", "head"), P("ctx", "head"), P("ctx", "head")),
        check_vma=False,
    )
```

```python
import functools
import math

import jax
import jax.numpy as jnp
from jax import lax
from jax.experimental import pallas as pl
from jax.experimental.pallas import tpu as pltpu
from jax.sharding import PartitionSpec as P

HD = 128
BLOCK = 128
EXTRA = 16
norm_eps = 1e-06
SCALE = HD ** (-0.5)
NEG = -1e30
NT = (((1,), (1,)), ((), ()))
F32 = jnp.float32
BF16 = jnp.bfloat16
SMALL = pl.CostEstimate(flops=1, bytes_accessed=1, transcendentals=0)


def moved(array, axis, target, around=False):
    size = lax.axis_size(axis)
    pairs = [(i, target(i)) for i in range(size)]
    if around:
        return lax.ppermute(array, axis, [(i, t % size) for i, t in pairs])
    return lax.ppermute(array, axis, [(i, t) for i, t in pairs if 0 <= t < size])


def vmem():
    return pl.BlockSpec(memory_space=pltpu.VMEM)


def hbm():
    return pl.BlockSpec(memory_space=pltpu.HBM)


def smem():
    return pl.BlockSpec(memory_space=pltpu.SMEM)


def params(mib):
    return pltpu.CompilerParams(vmem_limit_bytes=mib << 20)


def normed(raw, gain):
    mean_square = jnp.mean(raw * raw, axis=-1, keepdims=True)
    return raw * lax.rsqrt(mean_square + norm_eps) * gain


def message_kernel(
    kv_local, docs, table, key, value, key_gain, query_gain, bucket, out, facts
):
    core = lax.rem(lax.axis_index("ctx"), 2)
    for part in range(kv_local):
        head = part if kv_local == 1 else (core if part == 0 else 1 - core)
        lanes = pl.ds(pl.multiple_of(head * HD, HD), HD)
        rows = slice(part * BLOCK, (part + 1) * BLOCK)
        out[rows, :HD] = normed(key[:, lanes].astype(F32), key_gain[...]).astype(BF16)
        out[rows, HD:] = value[:, lanes]
    doc = jnp.full((EXTRA, 2 * HD), docs[0] + 1, jnp.int32).astype(F32)
    out[kv_local * BLOCK :, :] = doc.astype(BF16)
    facts[:8, :] = jnp.broadcast_to(query_gain[...], (8, HD))
    picks = bucket[...]
    found = jnp.zeros((1, HD), F32)
    for b in range(table.shape[0]):
        found = found + jnp.where(picks == b, table[b], 0.0)
    facts[8:, :] = jnp.broadcast_to(found, (8, HD))


def fetch(weight, held, sems, heads):
    n_head = lax.axis_size("head")
    width = weight.shape[0] // n_head
    core = lax.rem(lax.axis_index("ctx"), 2)
    features = pl.ds(pl.multiple_of(core * heads * HD, HD), heads * HD)
    pieces = sems.shape[0] // n_head
    part = width // pieces
    copies = []
    for i in range(sems.shape[0]):
        owner = lax.rem(lax.axis_index("head") + i // pieces, n_head)
        at = pl.multiple_of(owner * width + (i % pieces) * part, part)
        copies.append(
            pltpu.make_async_copy(
                weight.at[pl.ds(at, part), features],
                held.at[pl.ds(i * part, part), :],
                sems.at[i],
            )
        )
        copies[-1].start()
    return copies


def queries_kernel(
    heads,
    query,
    grad,
    facts,
    message,
    query_p,
    grad_p,
    facts_p,
    q_hat,
    rows,
    raw_t,
    both,
    kept,
):
    half = heads * HD
    core = lax.rem(lax.axis_index("ctx"), 2)
    own = pl.ds(pl.multiple_of(core * half, HD), half)
    gain = facts[0:1]
    for side in range(2):
        raw_all = query_p[:, own] if side else query[...]
        grad_all = grad_p[:, own] if side else grad[...]
        parity = 1 - core if side else core
        for head in range(heads):
            here = pl.ds(pl.multiple_of(parity * half + head * BLOCK, BLOCK), BLOCK)
            raw = raw_all[:, head * HD : (head + 1) * HD].astype(F32)
            q_hat[here, :] = normed(raw, gain).astype(BF16)
            rows[here, :] = grad_all[:, head * HD : (head + 1) * HD]
            raw_t[:, here] = raw.T.astype(BF16)
        source = facts_p if side else facts
        both[pl.ds(pl.multiple_of(8 + 8 * parity, 8), 8), :] = source[8:]
    both[:8, :] = facts[:8]
    kept[...] = message[...]


def place(kv_local, source, other, first, steps_back, core, keys, values, keys_t, docs):
    there = lax.div(lax.axis_index("ctx"), 4) >= steps_back
    after = (kv_local - 1) * BLOCK
    for block, skip, parity in ((source, 0, core), (other, after, 1 - core)):
        at = pl.ds(pl.multiple_of((first + parity) * BLOCK, BLOCK), BLOCK)
        key = block[skip : skip + BLOCK, :HD]
        keys[at, :] = key
        values[at, :] = block[skip : skip + BLOCK, HD:]
        keys_t[:, at] = key.astype(F32).T.astype(BF16)
        ids = block[kv_local * BLOCK :, :].astype(F32)[0:8]
        docs[first + parity] = jnp.where(there, ids, 0.0)


def masks(own_doc, docs):
    return [jnp.where((doc == own_doc) & (doc > 0.0), 0.0, NEG) for doc in docs]


def exponents(scores, expo, dots, at, bias, triangle, total, weighted):
    value = jnp.exp2(scores * (SCALE * math.log2(math.e)) + bias)
    if triangle is not None:
        value = jnp.where(triangle, value, 0.0)
    expo[at] = value.astype(expo.dtype)
    wide = value.shape[1]
    total = total + jnp.sum(value.reshape(BLOCK // 8, 8, wide), axis=0)
    weighted = weighted + jnp.sum((value * dots[at]).reshape(BLOCK // 8, 8, wide), axis=0)
    return total, weighted


def near_kernel(kv_local, heads, n_near, *refs):
    mine, others = refs[:n_near], refs[n_near : 2 * n_near]
    q_hat, rows, weight = refs[2 * n_near : 2 * n_near + 3]
    held, keys_t, expo, dots, sums, keys, values, docs, raw, sems = refs[2 * n_near + 3 :]
    core = lax.rem(lax.axis_index("ctx"), 2)

    copies = fetch(weight, held, sems, heads)
    blocks = 2 * n_near
    for index in range(n_near):
        first = blocks - 2 - 2 * index
        place(kv_local, mine[index], others[index], first, index, core, keys, values, keys_t, docs)
    wide = 2 * BLOCK
    row = lax.broadcasted_iota(jnp.int32, (BLOCK, wide), 0)
    col = lax.rem(lax.broadcasted_iota(jnp.int32, (BLOCK, wide), 1), BLOCK)
    triangle = row <= col
    doc_rows = [docs[slot][0:1] for slot in range(blocks)]
    pairs = heads // 2
    for side in range(2):
        count = blocks - 1 + side
        reach = count * BLOCK
        bias = masks(doc_rows[blocks - 2 + side], doc_rows[:count])
        for pair in range(pairs):
            step = side * pairs + pair
            here = slice(step * wide, (step + 1) * wide)
            raw[step % 2, :reach, :] = lax.dot_general(
                keys[:reach, :], q_hat[here, :], NT, preferred_element_type=F32
            )
            dots[step, :reach, :] = lax.dot_general(
                values[:reach, :], rows[here, :], NT, preferred_element_type=F32
            )
            total = jnp.zeros((8, wide), F32)
            weighted = jnp.zeros((8, wide), F32)
            for block in range(count):
                r = slice(block * BLOCK, (block + 1) * BLOCK)
                total, weighted = exponents(
                    raw[step % 2, r, :],
                    expo,
                    dots,
                    (step, r, slice(None)),
                    bias[block],
                    triangle if block == count - 1 else None,
                    total,
                    weighted,
                )
            sums[step, :8, :] = total
            sums[step, 8:, :] = weighted
    for copy in copies:
        copy.wait()


def sum_products(step, side_rows, dk, dv, pw, ds, q_two, g_two):
    span = slice(0, side_rows)
    dv_part = jnp.dot(pw, g_two, preferred_element_type=F32)
    dk_part = jnp.dot(ds, q_two, preferred_element_type=F32)
    if step == 0:
        dv[span, :] = dv_part
        dk[span, :] = dk_part
        if side_rows < dk.shape[0]:
            dv[side_rows:, :] = jnp.zeros((dk.shape[0] - side_rows, HD), F32)
            dk[side_rows:, :] = jnp.zeros((dk.shape[0] - side_rows, HD), F32)
    else:
        dv[span, :] += dv_part
        dk[span, :] += dk_part


def hand_out(core, firsts, outs, dk, dv):
    for first, out in zip(firsts, outs):
        for block, parity in ((0, core), (1, 1 - core)):
            at = pl.ds(pl.multiple_of((first + parity) * BLOCK, BLOCK), BLOCK)
            r = slice(block * BLOCK, (block + 1) * BLOCK)
            out[r, :HD] = (dk[at, :] * SCALE).astype(out.dtype)
            out[r, HD:] = dv[at, :].astype(out.dtype)


def far_kernel(kv_local, heads, n_near, n_far, *refs):
    mine, others = refs[: 1 + n_far], refs[1 + n_far : 2 + 2 * n_far]
    q_hat, rows, facts, near_expo, near_dots, sums = refs[2 + 2 * n_far : 8 + 2 * n_far]
    keys_t, pw_near, ds, *parts = refs[8 + 2 * n_far : 13 + 2 * n_far]
    keys, values, docs, expo, dots, pw_far, dk, dv = refs[13 + 2 * n_far :]
    core = lax.rem(lax.axis_index("ctx"), 2)
    blocks = 2 * n_far
    for index in range(n_far):
        source, other = mine[1 + index], others[1 + index]
        place(kv_local, source, other, 2 * index, index, core, keys, values, keys_t, docs)
    for source, parity in ((mine[0], core), (others[0], 1 - core)):
        docs[blocks + parity] = source[kv_local * BLOCK :, :].astype(F32)[0:8]
    wide = 2 * BLOCK
    far_rows = blocks * BLOCK
    doc_rows = [docs[slot][0:1] for slot in range(blocks + 2)]
    pairs = heads // 2
    steps = 2 * pairs
    biases, weights = [], []
    for side in range(2):
        biases.append(masks(doc_rows[blocks + side], doc_rows[:blocks]))
        weights.append(jnp.concatenate([facts[8 * (side + 1) : 8 * (side + 1) + 1]] * 2, axis=1))

    def scores(step):
        here, buf = slice(step * wide, (step + 1) * wide), step % 2
        expo[buf] = lax.dot_general(keys[...], q_hat[here, :], NT, preferred_element_type=F32)
        dots[buf] = lax.dot_general(values[...], rows[here, :], NT, preferred_element_type=F32)

    def middle(step):
        side, buf = step // pairs, step % 2
        total, weighted = sums[step, :8, :], sums[step, 8:, :]
        for block in range(blocks):
            at = (buf, slice(block * BLOCK, (block + 1) * BLOCK), slice(None))
            total, weighted = exponents(
                expo[at], expo, dots, at, biases[side][block], None, total, weighted
            )
        inverse = 1.0 / jnp.sum(total, axis=0, keepdims=True)
        shift = jnp.sum(weighted, axis=0, keepdims=True) * inverse
        level = inverse * weights[side]
        for block in range(blocks):
            r = slice(block * BLOCK, (block + 1) * BLOCK)
            scaled = expo[buf, r, :] * level
            pw_far[buf, r, :] = scaled.astype(BF16)
            ds[step, r, :] = (scaled * (dots[buf, r, :] - shift)).astype(BF16)
        for block in range(2 * n_near - 1 + side):
            r = slice(block * BLOCK, (block + 1) * BLOCK)
            scaled = near_expo[step, r, :].astype(F32) * level
            pw_near[step, r, :] = scaled.astype(BF16)
            to = slice(far_rows + block * BLOCK, far_rows + (block + 1) * BLOCK)
            ds[step, to, :] = (scaled * (near_dots[step, r, :] - shift)).astype(BF16)

    scores(0)
    for step in range(steps):
        if step + 1 < steps:
            scores(step + 1)
        middle(step)
        here = slice(step * wide, (step + 1) * wide)
        sum_products(
            step,
            far_rows,
            dk,
            dv,
            pw_far[step % 2],
            ds[step, :far_rows, :],
            q_hat[here, :],
            rows[here, :],
        )
    part_a, part_ce = parts
    span = 2 * BLOCK
    outs = [part_a, part_ce.at[:span, :], part_ce.at[span:, :]]
    hand_out(core, [2 * index for index in range(n_far)], outs, dk, dv)


def last_kernel(heads, n_near, n_far, *refs):
    q_hat, rows, raw_t, facts, near_t, far_t, pw_near, ds = refs[:8]
    dq, *parts = refs[8 : 9 + n_near]
    dk, dv = refs[9 + n_near :]
    core = lax.rem(lax.axis_index("ctx"), 2)
    wide = 2 * BLOCK
    far_rows = 2 * n_far * BLOCK
    gain_t = jnp.broadcast_to(facts[0:1] * SCALE, (HD, HD)).T
    gain_t = jnp.concatenate([gain_t] * 2, axis=1)
    pairs = heads // 2
    for step in range(2 * pairs):
        side, here = step // pairs, slice(step * wide, (step + 1) * wide)
        reach = (2 * n_near - 1 + side) * BLOCK
        to = slice(far_rows, far_rows + reach)
        sum_products(
            step,
            reach,
            dk,
            dv,
            pw_near[step, :reach, :],
            ds[step, to, :],
            q_hat[here, :],
            rows[here, :],
        )
        dq_t = jnp.dot(far_t[...], ds[step, :far_rows, :], preferred_element_type=F32)
        dq_t = dq_t + jnp.dot(near_t[:, :reach], ds[step, to, :], preferred_element_type=F32)
        x = raw_t[:, here].astype(F32)
        inverse = lax.rsqrt(jnp.mean(x * x, axis=0, keepdims=True) + norm_eps)
        dy = dq_t * gain_t
        inner = jnp.mean(x * dy, axis=0, keepdims=True)
        dx = inverse * dy - x * (inverse * inverse * inverse * inner)
        for part in range(2):
            at = (step % pairs) * wide + part * HD
            dq[at : at + HD, side * BLOCK : (side + 1) * BLOCK] = dx[
                :, part * BLOCK : (part + 1) * BLOCK
            ].astype(BF16)
    firsts = [2 * n_near - 2 - 2 * index for index in range(n_near)]
    hand_out(core, firsts, parts, dk, dv)


def project_kernel(first, dq, weight, keep, *sends):
    core = lax.rem(lax.axis_index("ctx"), 2)
    width = keep.shape[1]
    piece = width // len(sends)
    rows = min(256, piece)
    for i in range(width // rows):
        lanes = slice(i * rows, (i + 1) * rows)
        at = slice(first + i * rows, first + (i + 1) * rows)
        term = jnp.dot(weight[at, :], dq[...], preferred_element_type=F32).T
        even, odd = term[:BLOCK], term[BLOCK:]
        keep[:, lanes] = jnp.where(core == 0, even, odd).astype(keep.dtype)
        send = sends[i * rows // piece]
        inside = slice(i * rows % piece, i * rows % piece + rows)
        send[:, inside] = jnp.where(core == 0, odd, even).astype(send.dtype)


def project(dq, weight, first, width, pieces):
    tokens = dq.shape[1] // 2
    keep = jax.ShapeDtypeStruct((tokens, width), BF16)
    send = jax.ShapeDtypeStruct((tokens, width // pieces), BF16)
    return pl.pallas_call(
        functools.partial(project_kernel, first),
        in_specs=[vmem()] * 2,
        out_specs=[vmem()] * (1 + pieces),
        out_shape=[keep] + [send] * pieces,
        compiler_params=params(16),
        cost_estimate=SMALL,
    )(dq, weight)


def add_kernel(*refs):
    *terms, out = refs
    result = terms[0][...].astype(F32)
    for term in terms[1:]:
        result = result + term[...].astype(F32)
    out[...] = result.astype(out.dtype)


def add_pieces_kernel(whole, *refs):
    *pieces, out = refs
    width = pieces[0].shape[1]
    for i, piece in enumerate(pieces):
        lanes = slice(i * width, (i + 1) * width)
        out[:, lanes] = (whole[:, lanes].astype(F32) + piece[...].astype(F32)).astype(out.dtype)


def add_pieces(whole, pieces):
    return pl.pallas_call(
        add_pieces_kernel,
        in_specs=[vmem()] * (1 + len(pieces)),
        out_specs=vmem(),
        out_shape=jax.ShapeDtypeStruct(whole.shape, whole.dtype),
        compiler_params=params(16),
        cost_estimate=SMALL,
    )(whole, *pieces)


def add(first, second, dtype, *more):
    return pl.pallas_call(
        add_kernel,
        in_specs=[vmem()] * (2 + len(more)),
        out_specs=vmem(),
        out_shape=jax.ShapeDtypeStruct(first.shape, dtype),
        compiler_params=params(16),
        cost_estimate=SMALL,
    )(first, second, *more)


def two_sums_kernel(b, d, turn, sum_b, sum_d):
    half = turn.shape[0] // 2
    sum_b[...] = (b[...].astype(F32) + turn[:half].astype(F32)).astype(sum_b.dtype)
    sum_d[...] = (d[...].astype(F32) + turn[half:].astype(F32)).astype(sum_d.dtype)


def collect_kernel(part, back, keep, send):
    result = part[...] + back[...].astype(F32)
    keep[...] = result[:BLOCK]
    send[...] = result[BLOCK:].astype(BF16)


def finish_kernel(
    kv_local, keep, recv, key, gain, grad_key, grad_value, key_v, gain_v, sems
):
    copies = [
        pltpu.make_async_copy(key, key_v, sems.at[0]),
        pltpu.make_async_copy(gain, gain_v, sems.at[1]),
    ]
    for copy in copies:
        copy.start()
    for copy in copies:
        copy.wait()
    core = lax.rem(lax.axis_index("ctx"), 2)
    if kv_local > 1:
        parts = [(core, keep[...]), (1 - core, recv[...].astype(F32))]
    else:
        parts = [(0, keep[...] + recv[...].astype(F32))]
    for head, part in parts:
        lanes = pl.ds(pl.multiple_of(head * HD, HD), HD)
        raw = key_v[:, lanes].astype(F32)
        inverse = lax.rsqrt(jnp.mean(raw * raw, axis=-1, keepdims=True) + norm_eps)
        dy = part[:, :HD] * gain_v[...]
        inner = jnp.mean(raw * dy, axis=-1, keepdims=True)
        dx = inverse * dy - raw * (inverse * inverse * inverse * inner)
        grad_key[:, lanes] = dx.astype(BF16)
        grad_value[:, lanes] = part[:, HD:].astype(BF16)


def local(
    query_raw,
    key_raw,
    value_in,
    grad_out,
    query_gain,
    key_gain,
    loss_table,
    loss_bucket,
    block_docs,
    query_weight,
):
    tokens = query_raw.shape[0]
    kv_local = key_raw.shape[1] // HD
    half = query_raw.shape[1] // 2
    heads = half // HD
    key_row = key_gain.reshape(1, HD)
    query_row = query_gain.reshape(1, HD)
    shape = jax.ShapeDtypeStruct
    n_head = lax.axis_size("head")
    width = query_weight.shape[0] // n_head

    partner = lambda i: i ^ 1
    message, facts = pl.pallas_call(
        functools.partial(message_kernel, kv_local),
        in_specs=[smem(), smem()] + [vmem()] * 5,
        out_specs=[vmem()] * 2,
        out_shape=[
            shape((kv_local * BLOCK + EXTRA, 2 * HD), BF16),
            shape((16, HD), F32),
        ],
    )(
        block_docs,
        loss_table,
        key_raw,
        value_in,
        key_row,
        query_row,
        loss_bucket.reshape(1, tokens),
    )

    far_d = moved(message, "ctx", lambda i: i + 8, around=True)
    far_b = moved(message, "ctx", lambda i: i + 4, around=True)
    far_a = moved(message, "ctx", lambda i: i + 2 if (i // 2) % 2 == 0 else i + 10)
    query_in, grad_in, _ = lax.optimization_barrier((query_raw, grad_out, message))
    query_p = moved(query_in, "ctx", partner)
    grad_p = moved(grad_in, "ctx", partner)
    facts_p = moved(facts, "ctx", partner)
    core = lax.axis_index("ctx") % 2
    query_o = lax.dynamic_slice_in_dim(query_in, core * half, half, 1)
    grad_o = lax.dynamic_slice_in_dim(grad_in, core * half, half, 1)
    total = 2 * heads * BLOCK
    queries = pl.pallas_call(
        functools.partial(queries_kernel, heads),
        in_specs=[vmem()] * 7,
        out_specs=[vmem()] * 5,
        out_shape=[
            shape((total, HD), BF16),
            shape((total, HD), BF16),
            shape((HD, total), BF16),
            shape((24, HD), F32),
            shape(message.shape, BF16),
        ],
        compiler_params=params(16),
    )(query_o, grad_o, facts, message, query_p, grad_p, facts_p)
    far_c = moved(far_b, "ctx", lambda i: i ^ 2)
    far_d, *queries = lax.optimization_barrier((far_d, *queries))
    far_e = moved(far_d, "ctx", lambda i: i ^ 2)
    *queries, kept = queries
    q_hat, rows, raw_t, both = queries
    near = (kept, far_b, far_d)
    near_shared = [moved(source, "ctx", partner) for source in (message, far_b, far_d)]
    n_near, n_far = 3, 3
    steps = heads
    span = 2 * BLOCK
    near_rows, far_rows = n_near * span, n_far * span
    weight, near_t, near_expo, near_dots, sums = pl.pallas_call(
        functools.partial(near_kernel, kv_local, heads, n_near),
        in_specs=[vmem()] * (2 * n_near + 2) + [hbm()],
        out_specs=[vmem()] * 5,
        out_shape=[
            shape((query_weight.shape[0], half), BF16),
            shape((HD, near_rows), BF16),
            shape((steps, near_rows, span), BF16),
            shape((steps, near_rows, span), F32),
            shape((steps, 16, span), F32),
        ],
        scratch_shapes=[
            pltpu.VMEM((near_rows, HD), BF16),
            pltpu.VMEM((near_rows, HD), BF16),
            pltpu.VMEM((2 * n_near, 8, 2 * HD), F32),
            pltpu.VMEM((2, near_rows, span), F32),
            pltpu.SemaphoreType.DMA((2 * n_head,)),
        ],
        compiler_params=params(20),
    )(*near, *near_shared, q_hat, rows, query_weight)

    far_e, sums = lax.optimization_barrier((far_e, sums))
    far = (far_a, far_c, far_e)
    far_shared = [moved(source, "ctx", partner) for source in far]
    part_shape = shape((span, 2 * HD), BF16)
    far_t, pw_near, ds, part_a, part_ce = pl.pallas_call(
        functools.partial(far_kernel, kv_local, heads, n_near, n_far),
        in_specs=[vmem()] * (2 * n_far + 8),
        out_specs=[vmem()] * 5,
        out_shape=[
            shape((HD, far_rows), BF16),
            shape((steps, near_rows, span), BF16),
            shape((steps, far_rows + near_rows, span), BF16),
            part_shape,
            shape((2 * span, 2 * HD), BF16),
        ],
        input_output_aliases={2 * n_far + 5: 1},
        scratch_shapes=[
            pltpu.VMEM((far_rows, HD), BF16),
            pltpu.VMEM((far_rows, HD), BF16),
            pltpu.VMEM((2 * n_far + 2, 8, 2 * HD), F32),
            pltpu.VMEM((2, far_rows, span), F32),
            pltpu.VMEM((2, far_rows, span), F32),
            pltpu.VMEM((2, far_rows, span), BF16),
            pltpu.VMEM((far_rows, HD), F32),
            pltpu.VMEM((far_rows, HD), F32),
        ],
        compiler_params=params(20),
        cost_estimate=SMALL,
    )(
        kept,
        *far,
        near_shared[0],
        *far_shared,
        q_hat,
        rows,
        both,
        near_expo,
        near_dots,
        sums,
    )

    back_a = moved(part_a, "ctx", lambda i: i - 2 if (i // 2) % 2 == 1 else i - 10)
    turn = moved(part_ce, "ctx", lambda i: i ^ 2)

    dq, part_own, part_b, part_d = pl.pallas_call(
        functools.partial(last_kernel, heads, n_near, n_far),
        in_specs=[vmem()] * 8,
        out_specs=[vmem()] * 4,
        out_shape=[shape((half, 2 * tokens), BF16), shape((span, 2 * HD), F32)] + [part_shape] * 2,
        scratch_shapes=[pltpu.VMEM((near_rows, HD), F32)] * 2,
        compiler_params=params(20),
        cost_estimate=SMALL,
    )(q_hat, rows, raw_t, both, near_t, far_t, pw_near, ds)

    arrived = []
    for shift in range(1, n_head):
        keep, *sends = project(dq, weight, shift * width, width, 4)
        term = add_pieces(keep, [moved(send, "ctx", partner) for send in sends])
        term, turn = lax.optimization_barrier((term, turn))
        arrived.append(moved(term, "head", lambda i, s=shift: (i + s) % n_head))
    sum_b, sum_d = pl.pallas_call(
        two_sums_kernel,
        in_specs=[vmem()] * 3,
        out_specs=[vmem()] * 2,
        out_shape=[part_shape] * 2,
        compiler_params=params(16),
        cost_estimate=SMALL,
    )(part_b, part_d, turn)
    back_d = moved(sum_d, "ctx", lambda i: i - 8, around=True)
    back_b = moved(sum_b, "ctx", lambda i: i - 4, around=True)
    mine, mine_send = project(dq, weight, 0, width, 1)
    mine_recv = moved(mine_send, "ctx", partner)

    grad_input = mine
    for index, piece in enumerate(arrived):
        last = index == len(arrived) - 1
        grad_input = add(grad_input, piece, BF16 if last else F32, *([mine_recv] if last else []))
    back_b, grad_input = lax.optimization_barrier((back_b, grad_input))
    sum_keep, sum_send = pl.pallas_call(
        collect_kernel,
        in_specs=[vmem()] * 2,
        out_specs=[vmem()] * 2,
        out_shape=[shape((BLOCK, 2 * HD), F32), shape((BLOCK, 2 * HD), BF16)],
        compiler_params=params(16),
    )(add(add(part_own, back_d, F32), back_b, F32), back_a)
    sum_recv = moved(sum_send, "ctx", partner)
    grad_key, grad_value = pl.pallas_call(
        functools.partial(finish_kernel, kv_local),
        in_specs=[vmem(), vmem(), hbm(), hbm()],
        out_specs=[vmem()] * 2,
        out_shape=[shape(key_raw.shape, BF16), shape(value_in.shape, BF16)],
        scratch_shapes=[
            pltpu.VMEM(key_raw.shape, BF16),
            pltpu.VMEM((1, HD), F32),
            pltpu.SemaphoreType.DMA((2,)),
        ],
        compiler_params=params(16),
    )(sum_keep, sum_recv, key_raw, key_row)

    return grad_input, grad_key, grad_value


def solution(mesh):
    placed = (
        P("ctx", "head"),
        P("ctx", "head"),
        P("ctx", "head"),
        P("ctx", "head"),
        P(),
        P(),
        P(),
        P("ctx"),
        P("ctx"),
        P(None, "head"),
    )
    return jax.shard_map(
        local,
        mesh=mesh,
        in_specs=placed,
        out_specs=(P("ctx", "head"), P("ctx", "head"), P("ctx", "head")),
        check_vma=False,
    )
```

```python
import functools
import math

import jax
import jax.numpy as jnp
from jax import lax
from jax.experimental import pallas as pl
from jax.experimental.pallas import tpu as pltpu
from jax.sharding import PartitionSpec as P

HD = 128
BLOCK = 128
EXTRA = 16
norm_eps = 1e-06
SCALE = HD ** (-0.5)
NEG = -1e30
NT = (((1,), (1,)), ((), ()))
F32 = jnp.float32
BF16 = jnp.bfloat16
SMALL = pl.CostEstimate(flops=1, bytes_accessed=1, transcendentals=0)


def moved(array, axis, target, around=False):
    size = lax.axis_size(axis)
    pairs = [(i, target(i)) for i in range(size)]
    if around:
        return lax.ppermute(array, axis, [(i, t % size) for i, t in pairs])
    return lax.ppermute(array, axis, [(i, t) for i, t in pairs if 0 <= t < size])


def vmem():
    return pl.BlockSpec(memory_space=pltpu.VMEM)


def hbm():
    return pl.BlockSpec(memory_space=pltpu.HBM)


def smem():
    return pl.BlockSpec(memory_space=pltpu.SMEM)


def params(mib):
    return pltpu.CompilerParams(vmem_limit_bytes=mib << 20)


def normed(raw, gain):
    mean_square = jnp.mean(raw * raw, axis=-1, keepdims=True)
    return raw * lax.rsqrt(mean_square + norm_eps) * gain


def message_kernel(
    kv_local, docs, table, key, value, key_gain, query_gain, bucket, out, facts
):
    core = lax.rem(lax.axis_index("ctx"), 2)
    for part in range(kv_local):
        head = part if kv_local == 1 else (core if part == 0 else 1 - core)
        lanes = pl.ds(pl.multiple_of(head * HD, HD), HD)
        rows = slice(part * BLOCK, (part + 1) * BLOCK)
        out[rows, :HD] = normed(key[:, lanes].astype(F32), key_gain[...]).astype(BF16)
        out[rows, HD:] = value[:, lanes]
    doc = jnp.broadcast_to((docs[...] + 1).astype(F32), (EXTRA, 2 * HD))
    out[kv_local * BLOCK :, :] = doc.astype(BF16)
    facts[:8, :] = jnp.broadcast_to(query_gain[...], (8, HD))
    picks = bucket[...]
    found = jnp.zeros((1, HD), F32)
    for b in range(table.shape[1]):
        found = found + jnp.where(picks == b, table[:, b : b + 1], 0.0)
    facts[8:, :] = jnp.broadcast_to(found, (8, HD))


def fetch(weight, held, sems, heads):
    n_head = lax.axis_size("head")
    width = weight.shape[0] // n_head
    core = lax.rem(lax.axis_index("ctx"), 2)
    features = pl.ds(pl.multiple_of(core * heads * HD, HD), heads * HD)
    pieces = sems.shape[0] // n_head
    part = width // pieces
    copies = []
    for i in range(sems.shape[0]):
        owner = lax.rem(lax.axis_index("head") + i // pieces, n_head)
        at = pl.multiple_of(owner * width + (i % pieces) * part, part)
        copies.append(
            pltpu.make_async_copy(
                weight.at[pl.ds(at, part), features],
                held.at[pl.ds(i * part, part), :],
                sems.at[i],
            )
        )
        copies[-1].start()
    return copies


def queries_kernel(
    heads,
    query,
    grad,
    facts,
    message,
    query_p,
    grad_p,
    facts_p,
    q_hat,
    rows,
    raw_t,
    both,
    kept,
):
    half = heads * HD
    core = lax.rem(lax.axis_index("ctx"), 2)
    own = pl.ds(pl.multiple_of(core * half, HD), half)
    gain = facts[0:1]
    for side in range(2):
        raw_all = query_p[:, own] if side else query[...]
        grad_all = grad_p[:, own] if side else grad[...]
        parity = 1 - core if side else core
        for head in range(heads):
            here = pl.ds(pl.multiple_of(parity * half + head * BLOCK, BLOCK), BLOCK)
            raw = raw_all[:, head * HD : (head + 1) * HD].astype(F32)
            q_hat[here, :] = normed(raw, gain).astype(BF16)
            rows[here, :] = grad_all[:, head * HD : (head + 1) * HD]
            raw_t[:, here] = raw.T.astype(BF16)
        source = facts_p if side else facts
        both[pl.ds(pl.multiple_of(8 + 8 * parity, 8), 8), :] = source[8:]
    both[:8, :] = facts[:8]
    kept[...] = message[...]


def place(kv_local, source, other, first, steps_back, core, keys, values, keys_t, docs):
    there = lax.div(lax.axis_index("ctx"), 4) >= steps_back
    after = (kv_local - 1) * BLOCK
    for block, skip, parity in ((source, 0, core), (other, after, 1 - core)):
        at = pl.ds(pl.multiple_of((first + parity) * BLOCK, BLOCK), BLOCK)
        key = block[skip : skip + BLOCK, :HD]
        keys[at, :] = key
        values[at, :] = block[skip : skip + BLOCK, HD:]
        keys_t[:, at] = key.astype(F32).T.astype(BF16)
        ids = block[kv_local * BLOCK :, :].astype(F32)[0:8]
        docs[first + parity] = jnp.where(there, ids, 0.0)


def masks(own_doc, docs):
    return [jnp.where((doc == own_doc) & (doc > 0.0), 0.0, NEG) for doc in docs]


def exponents(scores, expo, dots, at, bias, triangle, total, weighted):
    value = jnp.exp2(scores * (SCALE * math.log2(math.e)) + bias)
    if triangle is not None:
        value = jnp.where(triangle, value, 0.0)
    expo[at] = value.astype(expo.dtype)
    wide = value.shape[1]
    total = total + jnp.sum(value.reshape(BLOCK // 8, 8, wide), axis=0)
    weighted = weighted + jnp.sum((value * dots[at]).reshape(BLOCK // 8, 8, wide), axis=0)
    return total, weighted


def near_kernel(kv_local, heads, n_near, *refs):
    mine, others = refs[:n_near], refs[n_near : 2 * n_near]
    q_hat, rows, weight = refs[2 * n_near : 2 * n_near + 3]
    held, keys_t, expo, dots, sums, keys, values, docs, raw, sems = refs[2 * n_near + 3 :]
    core = lax.rem(lax.axis_index("ctx"), 2)

    copies = fetch(weight, held, sems, heads)
    blocks = 2 * n_near
    for index in range(n_near):
        first = blocks - 2 - 2 * index
        place(kv_local, mine[index], others[index], first, index, core, keys, values, keys_t, docs)
    wide = 2 * BLOCK
    row = lax.broadcasted_iota(jnp.int32, (BLOCK, wide), 0)
    col = lax.rem(lax.broadcasted_iota(jnp.int32, (BLOCK, wide), 1), BLOCK)
    triangle = row <= col
    doc_rows = [docs[slot][0:1] for slot in range(blocks)]
    pairs = heads // 2
    for side in range(2):
        count = blocks - 1 + side
        reach = count * BLOCK
        bias = masks(doc_rows[blocks - 2 + side], doc_rows[:count])
        for pair in range(pairs):
            step = side * pairs + pair
            here = slice(step * wide, (step + 1) * wide)
            raw[step % 2, :reach, :] = lax.dot_general(
                keys[:reach, :], q_hat[here, :], NT, preferred_element_type=F32
            )
            dots[step, :reach, :] = lax.dot_general(
                values[:reach, :], rows[here, :], NT, preferred_element_type=F32
            )
            total = jnp.zeros((8, wide), F32)
            weighted = jnp.zeros((8, wide), F32)
            for block in range(count):
                r = slice(block * BLOCK, (block + 1) * BLOCK)
                total, weighted = exponents(
                    raw[step % 2, r, :],
                    expo,
                    dots,
                    (step, r, slice(None)),
                    bias[block],
                    triangle if block == count - 1 else None,
                    total,
                    weighted,
                )
            sums[step, :8, :] = total
            sums[step, 8:, :] = weighted
    for copy in copies:
        copy.wait()


def sum_products(step, side_rows, dk, dv, pw, ds, q_two, g_two):
    span = slice(0, side_rows)
    dv_part = jnp.dot(pw, g_two, preferred_element_type=F32)
    dk_part = jnp.dot(ds, q_two, preferred_element_type=F32)
    if step == 0:
        dv[span, :] = dv_part
        dk[span, :] = dk_part
        if side_rows < dk.shape[0]:
            dv[side_rows:, :] = jnp.zeros((dk.shape[0] - side_rows, HD), F32)
            dk[side_rows:, :] = jnp.zeros((dk.shape[0] - side_rows, HD), F32)
    else:
        dv[span, :] += dv_part
        dk[span, :] += dk_part


def hand_out(core, firsts, outs, dk, dv):
    for first, out in zip(firsts, outs):
        for block, parity in ((0, core), (1, 1 - core)):
            at = pl.ds(pl.multiple_of((first + parity) * BLOCK, BLOCK), BLOCK)
            r = slice(block * BLOCK, (block + 1) * BLOCK)
            out[r, :HD] = (dk[at, :] * SCALE).astype(out.dtype)
            out[r, HD:] = dv[at, :].astype(out.dtype)


def far_kernel(kv_local, heads, n_near, n_far, *refs):
    mine, others = refs[: 1 + n_far], refs[1 + n_far : 2 + 2 * n_far]
    q_hat, rows, facts, near_expo, near_dots, sums = refs[2 + 2 * n_far : 8 + 2 * n_far]
    keys_t, pw_near, ds, *parts = refs[8 + 2 * n_far : 13 + 2 * n_far]
    keys, values, docs, expo, dots, pw_far, dk, dv = refs[13 + 2 * n_far :]
    core = lax.rem(lax.axis_index("ctx"), 2)
    blocks = 2 * n_far
    for index in range(n_far):
        source, other = mine[1 + index], others[1 + index]
        place(kv_local, source, other, 2 * index, index, core, keys, values, keys_t, docs)
    for source, parity in ((mine[0], core), (others[0], 1 - core)):
        docs[blocks + parity] = source[kv_local * BLOCK :, :].astype(F32)[0:8]
    wide = 2 * BLOCK
    far_rows = blocks * BLOCK
    doc_rows = [docs[slot][0:1] for slot in range(blocks + 2)]
    pairs = heads // 2
    steps = 2 * pairs
    biases, weights = [], []
    for side in range(2):
        biases.append(masks(doc_rows[blocks + side], doc_rows[:blocks]))
        weights.append(jnp.concatenate([facts[8 * (side + 1) : 8 * (side + 1) + 1]] * 2, axis=1))

    def scores(step):
        here, buf = slice(step * wide, (step + 1) * wide), step % 2
        expo[buf] = lax.dot_general(keys[...], q_hat[here, :], NT, preferred_element_type=F32)
        dots[buf] = lax.dot_general(values[...], rows[here, :], NT, preferred_element_type=F32)

    def middle(step):
        side, buf = step // pairs, step % 2
        total, weighted = sums[step, :8, :], sums[step, 8:, :]
        for block in range(blocks):
            at = (buf, slice(block * BLOCK, (block + 1) * BLOCK), slice(None))
            total, weighted = exponents(
                expo[at], expo, dots, at, biases[side][block], None, total, weighted
            )
        inverse = 1.0 / jnp.sum(total, axis=0, keepdims=True)
        shift = jnp.sum(weighted, axis=0, keepdims=True) * inverse
        level = inverse * weights[side]
        for block in range(blocks):
            r = slice(block * BLOCK, (block + 1) * BLOCK)
            scaled = expo[buf, r, :] * level
            pw_far[buf, r, :] = scaled.astype(BF16)
            ds[step, r, :] = (scaled * (dots[buf, r, :] - shift)).astype(BF16)
        for block in range(2 * n_near - 1 + side):
            r = slice(block * BLOCK, (block + 1) * BLOCK)
            scaled = near_expo[step, r, :].astype(F32) * level
            pw_near[step, r, :] = scaled.astype(BF16)
            to = slice(far_rows + block * BLOCK, far_rows + (block + 1) * BLOCK)
            ds[step, to, :] = (scaled * (near_dots[step, r, :] - shift)).astype(BF16)

    scores(0)
    for step in range(steps):
        if step + 1 < steps:
            scores(step + 1)
        middle(step)
        here = slice(step * wide, (step + 1) * wide)
        sum_products(
            step,
            far_rows,
            dk,
            dv,
            pw_far[step % 2],
            ds[step, :far_rows, :],
            q_hat[here, :],
            rows[here, :],
        )
    part_a, part_ce = parts
    span = 2 * BLOCK
    outs = [part_a, part_ce.at[:span, :], part_ce.at[span:, :]]
    hand_out(core, [2 * index for index in range(n_far)], outs, dk, dv)


def last_kernel(heads, n_near, n_far, *refs):
    q_hat, rows, raw_t, facts, near_t, far_t, pw_near, ds = refs[:8]
    dq, *parts = refs[8 : 9 + n_near]
    dk, dv = refs[9 + n_near :]
    core = lax.rem(lax.axis_index("ctx"), 2)
    wide = 2 * BLOCK
    far_rows = 2 * n_far * BLOCK
    gain_t = jnp.broadcast_to(facts[0:1] * SCALE, (HD, HD)).T
    gain_t = jnp.concatenate([gain_t] * 2, axis=1)
    pairs = heads // 2
    for step in range(2 * pairs):
        side, here = step // pairs, slice(step * wide, (step + 1) * wide)
        reach = (2 * n_near - 1 + side) * BLOCK
        to = slice(far_rows, far_rows + reach)
        sum_products(
            step,
            reach,
            dk,
            dv,
            pw_near[step, :reach, :],
            ds[step, to, :],
            q_hat[here, :],
            rows[here, :],
        )
        dq_t = jnp.dot(far_t[...], ds[step, :far_rows, :], preferred_element_type=F32)
        dq_t = dq_t + jnp.dot(near_t[:, :reach], ds[step, to, :], preferred_element_type=F32)
        x = raw_t[:, here].astype(F32)
        inverse = lax.rsqrt(jnp.mean(x * x, axis=0, keepdims=True) + norm_eps)
        dy = dq_t * gain_t
        inner = jnp.mean(x * dy, axis=0, keepdims=True)
        dx = inverse * dy - x * (inverse * inverse * inverse * inner)
        for part in range(2):
            at = (step % pairs) * wide + part * HD
            dq[at : at + HD, side * BLOCK : (side + 1) * BLOCK] = dx[
                :, part * BLOCK : (part + 1) * BLOCK
            ].astype(BF16)
    firsts = [2 * n_near - 2 - 2 * index for index in range(n_near)]
    hand_out(core, firsts, parts, dk, dv)


def project_kernel(first, dq, weight, keep, *sends):
    core = lax.rem(lax.axis_index("ctx"), 2)
    width = keep.shape[1]
    piece = width // len(sends)
    rows = min(256, piece)
    for i in range(width // rows):
        lanes = slice(i * rows, (i + 1) * rows)
        at = slice(first + i * rows, first + (i + 1) * rows)
        term = jnp.dot(weight[at, :], dq[...], preferred_element_type=F32).T
        even, odd = term[:BLOCK], term[BLOCK:]
        keep[:, lanes] = jnp.where(core == 0, even, odd).astype(keep.dtype)
        send = sends[i * rows // piece]
        inside = slice(i * rows % piece, i * rows % piece + rows)
        send[:, inside] = jnp.where(core == 0, odd, even).astype(send.dtype)


def project(dq, weight, first, width, pieces):
    tokens = dq.shape[1] // 2
    keep = jax.ShapeDtypeStruct((tokens, width), BF16)
    send = jax.ShapeDtypeStruct((tokens, width // pieces), BF16)
    return pl.pallas_call(
        functools.partial(project_kernel, first),
        in_specs=[vmem()] * 2,
        out_specs=[vmem()] * (1 + pieces),
        out_shape=[keep] + [send] * pieces,
        compiler_params=params(16),
        cost_estimate=SMALL,
    )(dq, weight)


def add_kernel(*refs):
    *terms, out = refs
    result = terms[0][...].astype(F32)
    for term in terms[1:]:
        result = result + term[...].astype(F32)
    out[...] = result.astype(out.dtype)


def add_pieces_kernel(whole, *refs):
    *pieces, out = refs
    width = pieces[0].shape[1]
    for i, piece in enumerate(pieces):
        lanes = slice(i * width, (i + 1) * width)
        out[:, lanes] = (whole[:, lanes].astype(F32) + piece[...].astype(F32)).astype(out.dtype)


def add_pieces(whole, pieces):
    return pl.pallas_call(
        add_pieces_kernel,
        in_specs=[vmem()] * (1 + len(pieces)),
        out_specs=vmem(),
        out_shape=jax.ShapeDtypeStruct(whole.shape, whole.dtype),
        compiler_params=params(16),
        cost_estimate=SMALL,
    )(whole, *pieces)


def add(first, second, dtype, *more):
    return pl.pallas_call(
        add_kernel,
        in_specs=[vmem()] * (2 + len(more)),
        out_specs=vmem(),
        out_shape=jax.ShapeDtypeStruct(first.shape, dtype),
        compiler_params=params(16),
        cost_estimate=SMALL,
    )(first, second, *more)


def two_sums_kernel(b, d, turn, sum_b, sum_d):
    half = turn.shape[0] // 2
    sum_b[...] = (b[...].astype(F32) + turn[:half].astype(F32)).astype(sum_b.dtype)
    sum_d[...] = (d[...].astype(F32) + turn[half:].astype(F32)).astype(sum_d.dtype)


def collect_kernel(part, back, keep, send):
    result = part[...] + back[...].astype(F32)
    keep[...] = result[:BLOCK]
    send[...] = result[BLOCK:].astype(BF16)


def finish_kernel(
    kv_local, keep, recv, key, gain, grad_key, grad_value, key_v, gain_v, sems
):
    copies = [
        pltpu.make_async_copy(key, key_v, sems.at[0]),
        pltpu.make_async_copy(gain, gain_v, sems.at[1]),
    ]
    for copy in copies:
        copy.start()
    for copy in copies:
        copy.wait()
    core = lax.rem(lax.axis_index("ctx"), 2)
    if kv_local > 1:
        parts = [(core, keep[...]), (1 - core, recv[...].astype(F32))]
    else:
        parts = [(0, keep[...] + recv[...].astype(F32))]
    for head, part in parts:
        lanes = pl.ds(pl.multiple_of(head * HD, HD), HD)
        raw = key_v[:, lanes].astype(F32)
        inverse = lax.rsqrt(jnp.mean(raw * raw, axis=-1, keepdims=True) + norm_eps)
        dy = part[:, :HD] * gain_v[...]
        inner = jnp.mean(raw * dy, axis=-1, keepdims=True)
        dx = inverse * dy - raw * (inverse * inverse * inverse * inner)
        grad_key[:, lanes] = dx.astype(BF16)
        grad_value[:, lanes] = part[:, HD:].astype(BF16)


def local(
    query_raw,
    key_raw,
    value_in,
    grad_out,
    query_gain,
    key_gain,
    loss_table,
    loss_bucket,
    block_docs,
    query_weight,
):
    tokens = query_raw.shape[0]
    kv_local = key_raw.shape[1] // HD
    half = query_raw.shape[1] // 2
    heads = half // HD
    key_row = key_gain.reshape(1, HD)
    query_row = query_gain.reshape(1, HD)
    shape = jax.ShapeDtypeStruct
    n_head = lax.axis_size("head")
    width = query_weight.shape[0] // n_head

    partner = lambda i: i ^ 1
    message, facts = pl.pallas_call(
        functools.partial(message_kernel, kv_local),
        in_specs=[vmem()] * 7,
        out_specs=[vmem()] * 2,
        out_shape=[
            shape((kv_local * BLOCK + EXTRA, 2 * HD), BF16),
            shape((16, HD), F32),
        ],
    )(
        block_docs.reshape(1, 1),
        loss_table.reshape(1, -1),
        key_raw,
        value_in,
        key_row,
        query_row,
        loss_bucket.reshape(1, tokens),
    )

    far_d = moved(message, "ctx", lambda i: i + 8)
    far_b = moved(message, "ctx", lambda i: i + 4, around=True)
    far_a = moved(message, "ctx", lambda i: i + 2 if (i // 2) % 2 == 0 else i + 10)
    query_in, grad_in, _ = lax.optimization_barrier((query_raw, grad_out, message))
    query_p = moved(query_in, "ctx", partner)
    grad_p = moved(grad_in, "ctx", partner)
    facts_p = moved(facts, "ctx", partner)
    core = lax.axis_index("ctx") % 2
    query_o = lax.dynamic_slice_in_dim(query_in, core * half, half, 1)
    grad_o = lax.dynamic_slice_in_dim(grad_in, core * half, half, 1)
    total = 2 * heads * BLOCK
    queries = pl.pallas_call(
        functools.partial(queries_kernel, heads),
        in_specs=[vmem()] * 7,
        out_specs=[vmem()] * 5,
        out_shape=[
            shape((total, HD), BF16),
            shape((total, HD), BF16),
            shape((HD, total), BF16),
            shape((24, HD), F32),
            shape(message.shape, BF16),
        ],
        compiler_params=params(16),
    )(query_o, grad_o, facts, message, query_p, grad_p, facts_p)
    far_d, far_b, *queries = lax.optimization_barrier((far_d, far_b, *queries))
    far_c = moved(far_b, "ctx", lambda i: i ^ 2)
    far_e = moved(far_d, "ctx", lambda i: i ^ 2)
    *queries, kept = queries
    q_hat, rows, raw_t, both = queries
    near = (kept, far_b, far_d)
    near_shared = [moved(source, "ctx", partner) for source in (message, far_b, far_d)]
    n_near, n_far = 3, 3
    steps = heads
    span = 2 * BLOCK
    near_rows, far_rows = n_near * span, n_far * span
    weight, near_t, near_expo, near_dots, sums = pl.pallas_call(
        functools.partial(near_kernel, kv_local, heads, n_near),
        in_specs=[vmem()] * (2 * n_near + 2) + [hbm()],
        out_specs=[vmem()] * 5,
        out_shape=[
            shape((query_weight.shape[0], half), BF16),
            shape((HD, near_rows), BF16),
            shape((steps, near_rows, span), BF16),
            shape((steps, near_rows, span), F32),
            shape((steps, 16, span), F32),
        ],
        scratch_shapes=[
            pltpu.VMEM((near_rows, HD), BF16),
            pltpu.VMEM((near_rows, HD), BF16),
            pltpu.VMEM((2 * n_near, 8, 2 * HD), F32),
            pltpu.VMEM((2, near_rows, span), F32),
            pltpu.SemaphoreType.DMA((2 * n_head,)),
        ],
        compiler_params=params(20),
    )(*near, *near_shared, q_hat, rows, query_weight)

    far_e, sums = lax.optimization_barrier((far_e, sums))
    far = (far_a, far_c, far_e)
    far_shared = [moved(source, "ctx", partner) for source in far]
    part_shape = shape((span, 2 * HD), BF16)
    far_t, pw_near, ds, part_a, part_ce = pl.pallas_call(
        functools.partial(far_kernel, kv_local, heads, n_near, n_far),
        in_specs=[vmem()] * (2 * n_far + 8),
        out_specs=[vmem()] * 5,
        out_shape=[
            shape((HD, far_rows), BF16),
            shape((steps, near_rows, span), BF16),
            shape((steps, far_rows + near_rows, span), BF16),
            part_shape,
            shape((2 * span, 2 * HD), BF16),
        ],
        input_output_aliases={2 * n_far + 5: 1},
        scratch_shapes=[
            pltpu.VMEM((far_rows, HD), BF16),
            pltpu.VMEM((far_rows, HD), BF16),
            pltpu.VMEM((2 * n_far + 2, 8, 2 * HD), F32),
            pltpu.VMEM((2, far_rows, span), F32),
            pltpu.VMEM((2, far_rows, span), F32),
            pltpu.VMEM((2, far_rows, span), BF16),
            pltpu.VMEM((far_rows, HD), F32),
            pltpu.VMEM((far_rows, HD), F32),
        ],
        compiler_params=params(20),
        cost_estimate=SMALL,
    )(
        kept,
        *far,
        near_shared[0],
        *far_shared,
        q_hat,
        rows,
        both,
        near_expo,
        near_dots,
        sums,
    )

    back_a = moved(
        part_a, "ctx", lambda i: i - 2 if (i // 2) % 2 == 1 else i - 10, around=True
    )
    turn = moved(part_ce, "ctx", lambda i: i ^ 2)

    dq, part_own, part_b, part_d = pl.pallas_call(
        functools.partial(last_kernel, heads, n_near, n_far),
        in_specs=[vmem()] * 8,
        out_specs=[vmem()] * 4,
        out_shape=[shape((half, 2 * tokens), BF16), shape((span, 2 * HD), F32)] + [part_shape] * 2,
        scratch_shapes=[pltpu.VMEM((near_rows, HD), F32)] * 2,
        compiler_params=params(20),
        cost_estimate=SMALL,
    )(q_hat, rows, raw_t, both, near_t, far_t, pw_near, ds)

    mine, mine_send = project(dq, weight, 0, width, 1)
    arrived = []
    for shift in range(1, n_head):
        keep, *sends = project(dq, weight, shift * width, width, 4)
        term = add_pieces(keep, [moved(send, "ctx", partner) for send in sends])
        term, turn, mine_send = lax.optimization_barrier((term, turn, mine_send))
        arrived.append(moved(term, "head", lambda i, s=shift: (i + s) % n_head))
    sum_b, sum_d = pl.pallas_call(
        two_sums_kernel,
        in_specs=[vmem()] * 3,
        out_specs=[vmem()] * 2,
        out_shape=[part_shape] * 2,
        compiler_params=params(16),
        cost_estimate=SMALL,
    )(part_b, part_d, turn)
    back_d = moved(sum_d, "ctx", lambda i: i - 8, around=True)
    back_b = moved(sum_b, "ctx", lambda i: i - 4, around=True)
    mine_recv = moved(mine_send, "ctx", partner)

    sum_keep, sum_send = pl.pallas_call(
        collect_kernel,
        in_specs=[vmem()] * 2,
        out_specs=[vmem()] * 2,
        out_shape=[shape((BLOCK, 2 * HD), F32), shape((BLOCK, 2 * HD), BF16)],
        compiler_params=params(16),
    )(add(add(part_own, back_d, F32), back_b, F32), back_a)
    sum_recv = moved(sum_send, "ctx", partner)
    arrived[-1], sum_send = lax.optimization_barrier((arrived[-1], sum_send))
    grad_input = mine
    for index, piece in enumerate(arrived):
        last = index == len(arrived) - 1
        grad_input = add(grad_input, piece, BF16 if last else F32, *([mine_recv] if last else []))
    sum_recv, grad_input = lax.optimization_barrier((sum_recv, grad_input))
    grad_key, grad_value = pl.pallas_call(
        functools.partial(finish_kernel, kv_local),
        in_specs=[vmem(), vmem(), hbm(), hbm()],
        out_specs=[vmem()] * 2,
        out_shape=[shape(key_raw.shape, BF16), shape(value_in.shape, BF16)],
        scratch_shapes=[
            pltpu.VMEM(key_raw.shape, BF16),
            pltpu.VMEM((1, HD), F32),
            pltpu.SemaphoreType.DMA((2,)),
        ],
        compiler_params=params(16),
    )(sum_keep, sum_recv, key_raw, key_row)

    return grad_input, grad_key, grad_value


def solution(mesh):
    placed = (
        P("ctx", "head"),
        P("ctx", "head"),
        P("ctx", "head"),
        P("ctx", "head"),
        P(),
        P(),
        P(),
        P("ctx"),
        P("ctx"),
        P(None, "head"),
    )
    return jax.shard_map(
        local,
        mesh=mesh,
        in_specs=placed,
        out_specs=(P("ctx", "head"), P("ctx", "head"), P("ctx", "head")),
        check_vma=False,
    )
```

```python
import functools
import math

import jax
import jax.numpy as jnp
from jax import lax
from jax.experimental import pallas as pl
from jax.experimental.pallas import tpu as pltpu
from jax.sharding import PartitionSpec as P

HD = 128
BLOCK = 128
EXTRA = 16
norm_eps = 1e-06
SCALE = HD ** (-0.5)
NEG = -1e30
NT = (((1,), (1,)), ((), ()))
F32 = jnp.float32
BF16 = jnp.bfloat16
SMALL = pl.CostEstimate(flops=1, bytes_accessed=1, transcendentals=0)


def moved(array, axis, target, around=False):
    size = lax.axis_size(axis)
    pairs = [(i, target(i)) for i in range(size)]
    if around:
        return lax.ppermute(array, axis, [(i, t % size) for i, t in pairs])
    return lax.ppermute(array, axis, [(i, t) for i, t in pairs if 0 <= t < size])


def vmem():
    return pl.BlockSpec(memory_space=pltpu.VMEM)


def hbm():
    return pl.BlockSpec(memory_space=pltpu.HBM)


def smem():
    return pl.BlockSpec(memory_space=pltpu.SMEM)


def params(mib):
    return pltpu.CompilerParams(vmem_limit_bytes=mib << 20)


def normed(raw, gain):
    mean_square = jnp.mean(raw * raw, axis=-1, keepdims=True)
    return raw * lax.rsqrt(mean_square + norm_eps) * gain


def message_kernel(
    kv_local, docs, table, key, value, key_gain, query_gain, bucket, out, facts
):
    core = lax.rem(lax.axis_index("ctx"), 2)
    for part in range(kv_local):
        head = part if kv_local == 1 else (core if part == 0 else 1 - core)
        lanes = pl.ds(pl.multiple_of(head * HD, HD), HD)
        rows = slice(part * BLOCK, (part + 1) * BLOCK)
        out[rows, :HD] = normed(key[:, lanes].astype(F32), key_gain[...]).astype(BF16)
        out[rows, HD:] = value[:, lanes]
    doc = jnp.broadcast_to((docs[...] + 1).astype(F32), (EXTRA, 2 * HD))
    out[kv_local * BLOCK :, :] = doc.astype(BF16)
    facts[:8, :] = jnp.broadcast_to(query_gain[...], (8, HD))
    picks = bucket[...]
    found = jnp.zeros((1, HD), F32)
    for b in range(table.shape[1]):
        found = found + jnp.where(picks == b, table[:, b : b + 1], 0.0)
    facts[8:, :] = jnp.broadcast_to(found, (8, HD))


def fetch(weight, held, sems, heads):
    n_head = lax.axis_size("head")
    width = weight.shape[0] // n_head
    core = lax.rem(lax.axis_index("ctx"), 2)
    features = pl.ds(pl.multiple_of(core * heads * HD, HD), heads * HD)
    pieces = sems.shape[0] // n_head
    part = width // pieces
    copies = []
    for i in range(sems.shape[0]):
        owner = lax.rem(lax.axis_index("head") + i // pieces, n_head)
        at = pl.multiple_of(owner * width + (i % pieces) * part, part)
        copies.append(
            pltpu.make_async_copy(
                weight.at[pl.ds(at, part), features],
                held.at[pl.ds(i * part, part), :],
                sems.at[i],
            )
        )
        copies[-1].start()
    return copies


def queries_kernel(
    heads,
    query,
    grad,
    facts,
    message,
    query_p,
    grad_p,
    facts_p,
    q_hat,
    rows,
    raw_t,
    both,
    kept,
):
    half = heads * HD
    core = lax.rem(lax.axis_index("ctx"), 2)
    own = pl.ds(pl.multiple_of(core * half, HD), half)
    gain = facts[0:1]
    for side in range(2):
        raw_all = query_p[:, own] if side else query[...]
        grad_all = grad_p[:, own] if side else grad[...]
        parity = 1 - core if side else core
        for head in range(heads):
            here = pl.ds(pl.multiple_of(parity * half + head * BLOCK, BLOCK), BLOCK)
            raw = raw_all[:, head * HD : (head + 1) * HD].astype(F32)
            q_hat[here, :] = normed(raw, gain).astype(BF16)
            rows[here, :] = grad_all[:, head * HD : (head + 1) * HD]
            raw_t[:, here] = raw.T.astype(BF16)
        source = facts_p if side else facts
        both[pl.ds(pl.multiple_of(8 + 8 * parity, 8), 8), :] = source[8:]
    both[:8, :] = facts[:8]
    kept[...] = message[...]


def place(kv_local, source, other, first, steps_back, core, keys, values, keys_t, docs):
    there = lax.div(lax.axis_index("ctx"), 4) >= steps_back
    after = (kv_local - 1) * BLOCK
    for block, skip, parity in ((source, 0, core), (other, after, 1 - core)):
        at = pl.ds(pl.multiple_of((first + parity) * BLOCK, BLOCK), BLOCK)
        key = block[skip : skip + BLOCK, :HD]
        keys[at, :] = key
        values[at, :] = block[skip : skip + BLOCK, HD:]
        keys_t[:, at] = key.astype(F32).T.astype(BF16)
        ids = block[kv_local * BLOCK :, :].astype(F32)[0:8]
        docs[first + parity] = jnp.where(there, ids, 0.0)


def masks(own_doc, docs):
    return [jnp.where((doc == own_doc) & (doc > 0.0), 0.0, NEG) for doc in docs]


def exponents(scores, expo, dots, at, bias, triangle, total, weighted):
    value = jnp.exp2(scores * (SCALE * math.log2(math.e)) + bias)
    if triangle is not None:
        value = jnp.where(triangle, value, 0.0)
    expo[at] = value.astype(expo.dtype)
    wide = value.shape[1]
    total = total + jnp.sum(value.reshape(BLOCK // 8, 8, wide), axis=0)
    weighted = weighted + jnp.sum((value * dots[at]).reshape(BLOCK // 8, 8, wide), axis=0)
    return total, weighted


def near_kernel(kv_local, heads, n_near, *refs):
    mine, others = refs[:n_near], refs[n_near : 2 * n_near]
    q_hat, rows, weight = refs[2 * n_near : 2 * n_near + 3]
    held, keys_t, expo, dots, sums, keys, values, docs, raw, sems = refs[2 * n_near + 3 :]
    core = lax.rem(lax.axis_index("ctx"), 2)

    copies = fetch(weight, held, sems, heads)
    blocks = 2 * n_near
    for index in range(n_near):
        first = blocks - 2 - 2 * index
        place(kv_local, mine[index], others[index], first, index, core, keys, values, keys_t, docs)
    wide = 2 * BLOCK
    row = lax.broadcasted_iota(jnp.int32, (BLOCK, wide), 0)
    col = lax.rem(lax.broadcasted_iota(jnp.int32, (BLOCK, wide), 1), BLOCK)
    triangle = row <= col
    doc_rows = [docs[slot][0:1] for slot in range(blocks)]
    pairs = heads // 2
    for side in range(2):
        count = blocks - 1 + side
        reach = count * BLOCK
        bias = masks(doc_rows[blocks - 2 + side], doc_rows[:count])
        for pair in range(pairs):
            step = side * pairs + pair
            here = slice(step * wide, (step + 1) * wide)
            raw[step % 2, :reach, :] = lax.dot_general(
                keys[:reach, :], q_hat[here, :], NT, preferred_element_type=F32
            )
            dots[step, :reach, :] = lax.dot_general(
                values[:reach, :], rows[here, :], NT, preferred_element_type=F32
            )
            total = jnp.zeros((8, wide), F32)
            weighted = jnp.zeros((8, wide), F32)
            for block in range(count):
                r = slice(block * BLOCK, (block + 1) * BLOCK)
                total, weighted = exponents(
                    raw[step % 2, r, :],
                    expo,
                    dots,
                    (step, r, slice(None)),
                    bias[block],
                    triangle if block == count - 1 else None,
                    total,
                    weighted,
                )
            sums[step, :8, :] = total
            sums[step, 8:, :] = weighted
    for copy in copies:
        copy.wait()


def sum_products(step, side_rows, dk, dv, pw, ds, q_two, g_two):
    span = slice(0, side_rows)
    dv_part = jnp.dot(pw, g_two, preferred_element_type=F32)
    dk_part = jnp.dot(ds, q_two, preferred_element_type=F32)
    if step == 0:
        dv[span, :] = dv_part
        dk[span, :] = dk_part
        if side_rows < dk.shape[0]:
            dv[side_rows:, :] = jnp.zeros((dk.shape[0] - side_rows, HD), F32)
            dk[side_rows:, :] = jnp.zeros((dk.shape[0] - side_rows, HD), F32)
    else:
        dv[span, :] += dv_part
        dk[span, :] += dk_part


def hand_out(core, firsts, outs, dk, dv):
    for first, out in zip(firsts, outs):
        for block, parity in ((0, core), (1, 1 - core)):
            at = pl.ds(pl.multiple_of((first + parity) * BLOCK, BLOCK), BLOCK)
            r = slice(block * BLOCK, (block + 1) * BLOCK)
            out[r, :HD] = (dk[at, :] * SCALE).astype(out.dtype)
            out[r, HD:] = dv[at, :].astype(out.dtype)


def far_kernel(kv_local, heads, n_near, n_far, *refs):
    mine, others = refs[: 1 + n_far], refs[1 + n_far : 2 + 2 * n_far]
    q_hat, rows, facts, near_expo, near_dots, sums = refs[2 + 2 * n_far : 8 + 2 * n_far]
    keys_t, pw_near, ds, *parts = refs[8 + 2 * n_far : 13 + 2 * n_far]
    keys, values, docs, expo, dots, pw_far, dk, dv = refs[13 + 2 * n_far :]
    core = lax.rem(lax.axis_index("ctx"), 2)
    blocks = 2 * n_far
    for index in range(n_far):
        source, other = mine[1 + index], others[1 + index]
        place(kv_local, source, other, 2 * index, index, core, keys, values, keys_t, docs)
    for source, parity in ((mine[0], core), (others[0], 1 - core)):
        docs[blocks + parity] = source[kv_local * BLOCK :, :].astype(F32)[0:8]
    wide = 2 * BLOCK
    far_rows = blocks * BLOCK
    doc_rows = [docs[slot][0:1] for slot in range(blocks + 2)]
    pairs = heads // 2
    steps = 2 * pairs
    biases, weights = [], []
    for side in range(2):
        biases.append(masks(doc_rows[blocks + side], doc_rows[:blocks]))
        weights.append(jnp.concatenate([facts[8 * (side + 1) : 8 * (side + 1) + 1]] * 2, axis=1))

    def scores(step):
        here, buf = slice(step * wide, (step + 1) * wide), step % 2
        expo[buf] = lax.dot_general(keys[...], q_hat[here, :], NT, preferred_element_type=F32)
        dots[buf] = lax.dot_general(values[...], rows[here, :], NT, preferred_element_type=F32)

    def middle(step):
        side, buf = step // pairs, step % 2
        total, weighted = sums[step, :8, :], sums[step, 8:, :]
        for block in range(blocks):
            at = (buf, slice(block * BLOCK, (block + 1) * BLOCK), slice(None))
            total, weighted = exponents(
                expo[at], expo, dots, at, biases[side][block], None, total, weighted
            )
        inverse = 1.0 / jnp.sum(total, axis=0, keepdims=True)
        shift = jnp.sum(weighted, axis=0, keepdims=True) * inverse
        level = inverse * weights[side]
        for block in range(blocks):
            r = slice(block * BLOCK, (block + 1) * BLOCK)
            scaled = expo[buf, r, :] * level
            pw_far[buf, r, :] = scaled.astype(BF16)
            ds[step, r, :] = (scaled * (dots[buf, r, :] - shift)).astype(BF16)
        for block in range(2 * n_near - 1 + side):
            r = slice(block * BLOCK, (block + 1) * BLOCK)
            scaled = near_expo[step, r, :].astype(F32) * level
            pw_near[step, r, :] = scaled.astype(BF16)
            to = slice(far_rows + block * BLOCK, far_rows + (block + 1) * BLOCK)
            ds[step, to, :] = (scaled * (near_dots[step, r, :] - shift)).astype(BF16)

    scores(0)
    for step in range(steps):
        if step + 1 < steps:
            scores(step + 1)
        middle(step)
        here = slice(step * wide, (step + 1) * wide)
        sum_products(
            step,
            far_rows,
            dk,
            dv,
            pw_far[step % 2],
            ds[step, :far_rows, :],
            q_hat[here, :],
            rows[here, :],
        )
    part_a, part_ce = parts
    span = 2 * BLOCK
    outs = [part_a, part_ce.at[:span, :], part_ce.at[span:, :]]
    hand_out(core, [2 * index for index in range(n_far)], outs, dk, dv)


def last_kernel(heads, n_near, n_far, *refs):
    q_hat, rows, raw_t, facts, near_t, far_t, pw_near, ds = refs[:8]
    dq, *parts = refs[8 : 9 + n_near]
    dk, dv = refs[9 + n_near :]
    core = lax.rem(lax.axis_index("ctx"), 2)
    wide = 2 * BLOCK
    far_rows = 2 * n_far * BLOCK
    gain_t = jnp.broadcast_to(facts[0:1] * SCALE, (HD, HD)).T
    gain_t = jnp.concatenate([gain_t] * 2, axis=1)
    pairs = heads // 2
    for step in range(2 * pairs):
        side, here = step // pairs, slice(step * wide, (step + 1) * wide)
        reach = (2 * n_near - 1 + side) * BLOCK
        to = slice(far_rows, far_rows + reach)
        sum_products(
            step,
            reach,
            dk,
            dv,
            pw_near[step, :reach, :],
            ds[step, to, :],
            q_hat[here, :],
            rows[here, :],
        )
        dq_t = jnp.dot(far_t[...], ds[step, :far_rows, :], preferred_element_type=F32)
        dq_t = dq_t + jnp.dot(near_t[:, :reach], ds[step, to, :], preferred_element_type=F32)
        x = raw_t[:, here].astype(F32)
        inverse = lax.rsqrt(jnp.mean(x * x, axis=0, keepdims=True) + norm_eps)
        dy = dq_t * gain_t
        inner = jnp.mean(x * dy, axis=0, keepdims=True)
        dx = inverse * dy - x * (inverse * inverse * inverse * inner)
        for part in range(2):
            at = (step % pairs) * wide + part * HD
            dq[at : at + HD, side * BLOCK : (side + 1) * BLOCK] = dx[
                :, part * BLOCK : (part + 1) * BLOCK
            ].astype(BF16)
    firsts = [2 * n_near - 2 - 2 * index for index in range(n_near)]
    hand_out(core, firsts, parts, dk, dv)


def project_kernel(first, dq, weight, keep, *sends):
    core = lax.rem(lax.axis_index("ctx"), 2)
    width = keep.shape[1]
    piece = width // len(sends)
    rows = min(256, piece)
    for i in range(width // rows):
        lanes = slice(i * rows, (i + 1) * rows)
        at = slice(first + i * rows, first + (i + 1) * rows)
        term = jnp.dot(weight[at, :], dq[...], preferred_element_type=F32).T
        even, odd = term[:BLOCK], term[BLOCK:]
        keep[:, lanes] = jnp.where(core == 0, even, odd).astype(keep.dtype)
        send = sends[i * rows // piece]
        inside = slice(i * rows % piece, i * rows % piece + rows)
        send[:, inside] = jnp.where(core == 0, odd, even).astype(send.dtype)


def project(dq, weight, first, width, pieces):
    tokens = dq.shape[1] // 2
    keep = jax.ShapeDtypeStruct((tokens, width), BF16)
    send = jax.ShapeDtypeStruct((tokens, width // pieces), BF16)
    return pl.pallas_call(
        functools.partial(project_kernel, first),
        in_specs=[vmem()] * 2,
        out_specs=[vmem()] * (1 + pieces),
        out_shape=[keep] + [send] * pieces,
        compiler_params=params(16),
        cost_estimate=SMALL,
    )(dq, weight)


def add_kernel(*refs):
    *terms, out = refs
    result = terms[0][...].astype(F32)
    for term in terms[1:]:
        result = result + term[...].astype(F32)
    out[...] = result.astype(out.dtype)


def add_pieces_kernel(whole, *refs):
    *pieces, out = refs
    width = pieces[0].shape[1]
    for i, piece in enumerate(pieces):
        lanes = slice(i * width, (i + 1) * width)
        out[:, lanes] = (whole[:, lanes].astype(F32) + piece[...].astype(F32)).astype(out.dtype)


def add_pieces(whole, pieces):
    return pl.pallas_call(
        add_pieces_kernel,
        in_specs=[vmem()] * (1 + len(pieces)),
        out_specs=vmem(),
        out_shape=jax.ShapeDtypeStruct(whole.shape, whole.dtype),
        compiler_params=params(16),
        cost_estimate=SMALL,
    )(whole, *pieces)


def add(first, second, dtype, *more):
    return pl.pallas_call(
        add_kernel,
        in_specs=[vmem()] * (2 + len(more)),
        out_specs=vmem(),
        out_shape=jax.ShapeDtypeStruct(first.shape, dtype),
        compiler_params=params(16),
        cost_estimate=SMALL,
    )(first, second, *more)


def two_sums_kernel(b, d, turn, sum_b, sum_d):
    half = turn.shape[0] // 2
    sum_b[...] = (b[...].astype(F32) + turn[:half].astype(F32)).astype(sum_b.dtype)
    sum_d[...] = (d[...].astype(F32) + turn[half:].astype(F32)).astype(sum_d.dtype)


def collect_kernel(part, back, keep, send):
    result = part[...] + back[...].astype(F32)
    keep[...] = result[:BLOCK]
    send[...] = result[BLOCK:].astype(BF16)


def finish_kernel(
    kv_local, keep, recv, key, gain, grad_key, grad_value, key_v, gain_v, sems
):
    copies = [
        pltpu.make_async_copy(key, key_v, sems.at[0]),
        pltpu.make_async_copy(gain, gain_v, sems.at[1]),
    ]
    for copy in copies:
        copy.start()
    for copy in copies:
        copy.wait()
    core = lax.rem(lax.axis_index("ctx"), 2)
    if kv_local > 1:
        parts = [(core, keep[...]), (1 - core, recv[...].astype(F32))]
    else:
        parts = [(0, keep[...] + recv[...].astype(F32))]
    for head, part in parts:
        lanes = pl.ds(pl.multiple_of(head * HD, HD), HD)
        raw = key_v[:, lanes].astype(F32)
        inverse = lax.rsqrt(jnp.mean(raw * raw, axis=-1, keepdims=True) + norm_eps)
        dy = part[:, :HD] * gain_v[...]
        inner = jnp.mean(raw * dy, axis=-1, keepdims=True)
        dx = inverse * dy - raw * (inverse * inverse * inverse * inner)
        grad_key[:, lanes] = dx.astype(BF16)
        grad_value[:, lanes] = part[:, HD:].astype(BF16)


def local(
    query_raw,
    key_raw,
    value_in,
    grad_out,
    query_gain,
    key_gain,
    loss_table,
    loss_bucket,
    block_docs,
    query_weight,
):
    tokens = query_raw.shape[0]
    kv_local = key_raw.shape[1] // HD
    half = query_raw.shape[1] // 2
    heads = half // HD
    key_row = key_gain.reshape(1, HD)
    query_row = query_gain.reshape(1, HD)
    shape = jax.ShapeDtypeStruct
    n_head = lax.axis_size("head")
    width = query_weight.shape[0] // n_head

    partner = lambda i: i ^ 1
    message, facts = pl.pallas_call(
        functools.partial(message_kernel, kv_local),
        in_specs=[vmem()] * 7,
        out_specs=[vmem()] * 2,
        out_shape=[
            shape((kv_local * BLOCK + EXTRA, 2 * HD), BF16),
            shape((16, HD), F32),
        ],
    )(
        block_docs.reshape(1, 1),
        loss_table.reshape(1, -1),
        key_raw,
        value_in,
        key_row,
        query_row,
        loss_bucket.reshape(1, tokens),
    )

    far_d = moved(message, "ctx", lambda i: i + 8)
    far_b = moved(message, "ctx", lambda i: i + 4, around=True)
    far_a = moved(message, "ctx", lambda i: i + 2 if (i // 2) % 2 == 0 else i + 10)
    query_in, grad_in, _ = lax.optimization_barrier((query_raw, grad_out, message))
    query_p = moved(query_in, "ctx", partner)
    grad_p = moved(grad_in, "ctx", partner)
    facts_p = moved(facts, "ctx", partner)
    core = lax.axis_index("ctx") % 2
    query_o = lax.dynamic_slice_in_dim(query_in, core * half, half, 1)
    grad_o = lax.dynamic_slice_in_dim(grad_in, core * half, half, 1)
    total = 2 * heads * BLOCK
    queries = pl.pallas_call(
        functools.partial(queries_kernel, heads),
        in_specs=[vmem()] * 7,
        out_specs=[vmem()] * 5,
        out_shape=[
            shape((total, HD), BF16),
            shape((total, HD), BF16),
            shape((HD, total), BF16),
            shape((24, HD), F32),
            shape(message.shape, BF16),
        ],
        compiler_params=params(16),
    )(query_o, grad_o, facts, message, query_p, grad_p, facts_p)
    far_c = moved(far_b, "ctx", lambda i: i ^ 2)
    far_d, *queries = lax.optimization_barrier((far_d, *queries))
    far_e = moved(far_d, "ctx", lambda i: i ^ 2)
    *queries, kept = queries
    q_hat, rows, raw_t, both = queries
    near = (kept, far_b, far_d)
    near_shared = [moved(source, "ctx", partner) for source in (message, far_b, far_d)]
    n_near, n_far = 3, 3
    steps = heads
    span = 2 * BLOCK
    near_rows, far_rows = n_near * span, n_far * span
    weight, near_t, near_expo, near_dots, sums = pl.pallas_call(
        functools.partial(near_kernel, kv_local, heads, n_near),
        in_specs=[vmem()] * (2 * n_near + 2) + [hbm()],
        out_specs=[vmem()] * 5,
        out_shape=[
            shape((query_weight.shape[0], half), BF16),
            shape((HD, near_rows), BF16),
            shape((steps, near_rows, span), BF16),
            shape((steps, near_rows, span), F32),
            shape((steps, 16, span), F32),
        ],
        scratch_shapes=[
            pltpu.VMEM((near_rows, HD), BF16),
            pltpu.VMEM((near_rows, HD), BF16),
            pltpu.VMEM((2 * n_near, 8, 2 * HD), F32),
            pltpu.VMEM((2, near_rows, span), F32),
            pltpu.SemaphoreType.DMA((2 * n_head,)),
        ],
        compiler_params=params(20),
    )(*near, *near_shared, q_hat, rows, query_weight)

    far_e, sums = lax.optimization_barrier((far_e, sums))
    far = (far_a, far_c, far_e)
    far_shared = [moved(source, "ctx", partner) for source in far]
    part_shape = shape((span, 2 * HD), BF16)
    far_t, pw_near, ds, part_a, part_ce = pl.pallas_call(
        functools.partial(far_kernel, kv_local, heads, n_near, n_far),
        in_specs=[vmem()] * (2 * n_far + 8),
        out_specs=[vmem()] * 5,
        out_shape=[
            shape((HD, far_rows), BF16),
            shape((steps, near_rows, span), BF16),
            shape((steps, far_rows + near_rows, span), BF16),
            part_shape,
            shape((2 * span, 2 * HD), BF16),
        ],
        input_output_aliases={2 * n_far + 5: 1},
        scratch_shapes=[
            pltpu.VMEM((far_rows, HD), BF16),
            pltpu.VMEM((far_rows, HD), BF16),
            pltpu.VMEM((2 * n_far + 2, 8, 2 * HD), F32),
            pltpu.VMEM((2, far_rows, span), F32),
            pltpu.VMEM((2, far_rows, span), F32),
            pltpu.VMEM((2, far_rows, span), BF16),
            pltpu.VMEM((far_rows, HD), F32),
            pltpu.VMEM((far_rows, HD), F32),
        ],
        compiler_params=params(20),
        cost_estimate=SMALL,
    )(
        kept,
        *far,
        near_shared[0],
        *far_shared,
        q_hat,
        rows,
        both,
        near_expo,
        near_dots,
        sums,
    )

    back_a = moved(
        part_a, "ctx", lambda i: i - 2 if (i // 2) % 2 == 1 else i - 10, around=True
    )
    turn = moved(part_ce, "ctx", lambda i: i ^ 2)

    dq, part_own, part_b, part_d = pl.pallas_call(
        functools.partial(last_kernel, heads, n_near, n_far),
        in_specs=[vmem()] * 8,
        out_specs=[vmem()] * 4,
        out_shape=[shape((half, 2 * tokens), BF16), shape((span, 2 * HD), F32)] + [part_shape] * 2,
        scratch_shapes=[pltpu.VMEM((near_rows, HD), F32)] * 2,
        compiler_params=params(20),
        cost_estimate=SMALL,
    )(q_hat, rows, raw_t, both, near_t, far_t, pw_near, ds)

    mine, mine_send = project(dq, weight, 0, width, 1)
    arrived = []
    for shift in range(1, n_head):
        keep, *sends = project(dq, weight, shift * width, width, 4)
        term = add_pieces(keep, [moved(send, "ctx", partner) for send in sends])
        term, turn, mine_send = lax.optimization_barrier((term, turn, mine_send))
        arrived.append(moved(term, "head", lambda i, s=shift: (i + s) % n_head))
    sum_b, sum_d = pl.pallas_call(
        two_sums_kernel,
        in_specs=[vmem()] * 3,
        out_specs=[vmem()] * 2,
        out_shape=[part_shape] * 2,
        compiler_params=params(16),
        cost_estimate=SMALL,
    )(part_b, part_d, turn)
    back_d = moved(sum_d, "ctx", lambda i: i - 8, around=True)
    back_b = moved(sum_b, "ctx", lambda i: i - 4, around=True)
    mine_recv = moved(mine_send, "ctx", partner)

    sum_keep, sum_send = pl.pallas_call(
        collect_kernel,
        in_specs=[vmem()] * 2,
        out_specs=[vmem()] * 2,
        out_shape=[shape((BLOCK, 2 * HD), F32), shape((BLOCK, 2 * HD), BF16)],
        compiler_params=params(16),
    )(add(add(part_own, back_d, F32), back_b, F32), back_a)
    sum_recv = moved(sum_send, "ctx", partner)
    arrived[-1], sum_send = lax.optimization_barrier((arrived[-1], sum_send))
    grad_input = mine
    for index, piece in enumerate(arrived):
        last = index == len(arrived) - 1
        grad_input = add(grad_input, piece, BF16 if last else F32, *([mine_recv] if last else []))
    sum_recv, grad_input = lax.optimization_barrier((sum_recv, grad_input))
    grad_key, grad_value = pl.pallas_call(
        functools.partial(finish_kernel, kv_local),
        in_specs=[vmem(), vmem(), hbm(), hbm()],
        out_specs=[vmem()] * 2,
        out_shape=[shape(key_raw.shape, BF16), shape(value_in.shape, BF16)],
        scratch_shapes=[
            pltpu.VMEM(key_raw.shape, BF16),
            pltpu.VMEM((1, HD), F32),
            pltpu.SemaphoreType.DMA((2,)),
        ],
        compiler_params=params(16),
    )(sum_keep, sum_recv, key_raw, key_row)

    return grad_input, grad_key, grad_value


def solution(mesh):
    placed = (
        P("ctx", "head"),
        P("ctx", "head"),
        P("ctx", "head"),
        P("ctx", "head"),
        P(),
        P(),
        P(),
        P("ctx"),
        P("ctx"),
        P(None, "head"),
    )
    return jax.shard_map(
        local,
        mesh=mesh,
        in_specs=placed,
        out_specs=(P("ctx", "head"), P("ctx", "head"), P("ctx", "head")),
        check_vma=False,
    )
```

```python
import functools
import math

import jax
import jax.numpy as jnp
from jax import lax
from jax.experimental import pallas as pl
from jax.experimental.pallas import tpu as pltpu
from jax.sharding import PartitionSpec as P

HD = 128
BLOCK = 128
EXTRA = 16
norm_eps = 1e-06
SCALE = HD ** (-0.5)
NEG = -1e30
NT = (((1,), (1,)), ((), ()))
F32 = jnp.float32
BF16 = jnp.bfloat16
SMALL = pl.CostEstimate(flops=1, bytes_accessed=1, transcendentals=0)


def moved(array, axis, target, around=False):
    size = lax.axis_size(axis)
    pairs = [(i, target(i)) for i in range(size)]
    if around:
        return lax.ppermute(array, axis, [(i, t % size) for i, t in pairs])
    return lax.ppermute(array, axis, [(i, t) for i, t in pairs if 0 <= t < size])


def vmem():
    return pl.BlockSpec(memory_space=pltpu.VMEM)


def hbm():
    return pl.BlockSpec(memory_space=pltpu.HBM)


def smem():
    return pl.BlockSpec(memory_space=pltpu.SMEM)


def params(mib):
    return pltpu.CompilerParams(vmem_limit_bytes=mib << 20)


def normed(raw, gain):
    mean_square = jnp.mean(raw * raw, axis=-1, keepdims=True)
    return raw * lax.rsqrt(mean_square + norm_eps) * gain


def message_kernel(
    kv_local, docs, table, key, value, key_gain, query_gain, bucket, out, facts
):
    core = lax.rem(lax.axis_index("ctx"), 2)
    for part in range(kv_local):
        head = part if kv_local == 1 else (core if part == 0 else 1 - core)
        lanes = pl.ds(pl.multiple_of(head * HD, HD), HD)
        rows = slice(part * BLOCK, (part + 1) * BLOCK)
        out[rows, :HD] = normed(key[:, lanes].astype(F32), key_gain[...]).astype(BF16)
        out[rows, HD:] = value[:, lanes]
    doc = jnp.broadcast_to((docs[...] + 1).astype(F32), (EXTRA, 2 * HD))
    out[kv_local * BLOCK :, :] = doc.astype(BF16)
    facts[:8, :] = jnp.broadcast_to(query_gain[...], (8, HD))
    picks = bucket[...]
    found = jnp.zeros((1, HD), F32)
    for b in range(table.shape[1]):
        found = found + jnp.where(picks == b, table[:, b : b + 1], 0.0)
    facts[8:, :] = jnp.broadcast_to(found, (8, HD))


def fetch(weight, held, sems, heads, first):
    n_head = lax.axis_size("head")
    width = weight.shape[0] // n_head
    core = lax.rem(lax.axis_index("ctx"), 2)
    features = pl.ds(pl.multiple_of(core * heads * HD, HD), heads * HD)
    pieces = sems.shape[0] * width // held.shape[0]
    part = width // pieces
    copies = []
    for i in range(sems.shape[0]):
        owner = lax.rem(lax.axis_index("head") + first + i // pieces, n_head)
        at = pl.multiple_of(owner * width + (i % pieces) * part, part)
        copies.append(
            pltpu.make_async_copy(
                weight.at[pl.ds(at, part), features],
                held.at[pl.ds(i * part, part), :],
                sems.at[i],
            )
        )
        copies[-1].start()
    return copies


def queries_kernel(
    heads,
    query,
    grad,
    facts,
    message,
    query_p,
    grad_p,
    facts_p,
    q_hat,
    rows,
    raw_t,
    both,
    kept,
):
    half = heads * HD
    core = lax.rem(lax.axis_index("ctx"), 2)
    own = pl.ds(pl.multiple_of(core * half, HD), half)
    gain = facts[0:1]
    for side in range(2):
        raw_all = query_p[:, own] if side else query[...]
        grad_all = grad_p[:, own] if side else grad[...]
        parity = 1 - core if side else core
        for head in range(heads):
            here = pl.ds(pl.multiple_of(parity * half + head * BLOCK, BLOCK), BLOCK)
            raw = raw_all[:, head * HD : (head + 1) * HD].astype(F32)
            q_hat[here, :] = normed(raw, gain).astype(BF16)
            rows[here, :] = grad_all[:, head * HD : (head + 1) * HD]
            raw_t[:, here] = raw.T.astype(BF16)
        source = facts_p if side else facts
        both[pl.ds(pl.multiple_of(8 + 8 * parity, 8), 8), :] = source[8:]
    both[:8, :] = facts[:8]
    kept[...] = message[...]


def place(kv_local, source, other, first, steps_back, core, keys, values, keys_t, docs):
    there = lax.div(lax.axis_index("ctx"), 4) >= steps_back
    after = (kv_local - 1) * BLOCK
    for block, skip, parity in ((source, 0, core), (other, after, 1 - core)):
        at = pl.ds(pl.multiple_of((first + parity) * BLOCK, BLOCK), BLOCK)
        key = block[skip : skip + BLOCK, :HD]
        keys[at, :] = key
        values[at, :] = block[skip : skip + BLOCK, HD:]
        keys_t[:, at] = key.astype(F32).T.astype(BF16)
        ids = block[kv_local * BLOCK :, :].astype(F32)[0:8]
        docs[first + parity] = jnp.where(there, ids, 0.0)


def masks(own_doc, docs):
    return [jnp.where((doc == own_doc) & (doc > 0.0), 0.0, NEG) for doc in docs]


def exponents(scores, expo, dots, at, bias, triangle, total, weighted):
    value = jnp.exp2(scores * (SCALE * math.log2(math.e)) + bias)
    if triangle is not None:
        value = jnp.where(triangle, value, 0.0)
    expo[at] = value.astype(expo.dtype)
    wide = value.shape[1]
    total = total + jnp.sum(value.reshape(BLOCK // 8, 8, wide), axis=0)
    weighted = weighted + jnp.sum((value * dots[at]).reshape(BLOCK // 8, 8, wide), axis=0)
    return total, weighted


def near_kernel(kv_local, heads, n_near, *refs):
    mine, others = refs[:n_near], refs[n_near : 2 * n_near]
    q_hat, rows, weight = refs[2 * n_near : 2 * n_near + 3]
    held, keys_t, expo, dots, sums, keys, values, docs, raw, sems = refs[2 * n_near + 3 :]
    core = lax.rem(lax.axis_index("ctx"), 2)

    copies = fetch(weight, held, sems, heads, 1)
    blocks = 2 * n_near
    for index in range(n_near):
        first = blocks - 2 - 2 * index
        place(kv_local, mine[index], others[index], first, index, core, keys, values, keys_t, docs)
    wide = 2 * BLOCK
    row = lax.broadcasted_iota(jnp.int32, (BLOCK, wide), 0)
    col = lax.rem(lax.broadcasted_iota(jnp.int32, (BLOCK, wide), 1), BLOCK)
    triangle = row <= col
    doc_rows = [docs[slot][0:1] for slot in range(blocks)]
    pairs = heads // 2
    for side in range(2):
        count = blocks - 1 + side
        reach = count * BLOCK
        bias = masks(doc_rows[blocks - 2 + side], doc_rows[:count])
        for pair in range(pairs):
            step = side * pairs + pair
            here = slice(step * wide, (step + 1) * wide)
            raw[step % 2, :reach, :] = lax.dot_general(
                keys[:reach, :], q_hat[here, :], NT, preferred_element_type=F32
            )
            dots[step, :reach, :] = lax.dot_general(
                values[:reach, :], rows[here, :], NT, preferred_element_type=F32
            )
            total = jnp.zeros((8, wide), F32)
            weighted = jnp.zeros((8, wide), F32)
            for block in range(count):
                r = slice(block * BLOCK, (block + 1) * BLOCK)
                total, weighted = exponents(
                    raw[step % 2, r, :],
                    expo,
                    dots,
                    (step, r, slice(None)),
                    bias[block],
                    triangle if block == count - 1 else None,
                    total,
                    weighted,
                )
            sums[step, :8, :] = total
            sums[step, 8:, :] = weighted
    for copy in copies:
        copy.wait()


def sum_products(step, side_rows, dk, dv, pw, ds, q_two, g_two):
    span = slice(0, side_rows)
    dv_part = jnp.dot(pw, g_two, preferred_element_type=F32)
    dk_part = jnp.dot(ds, q_two, preferred_element_type=F32)
    if step == 0:
        dv[span, :] = dv_part
        dk[span, :] = dk_part
        if side_rows < dk.shape[0]:
            dv[side_rows:, :] = jnp.zeros((dk.shape[0] - side_rows, HD), F32)
            dk[side_rows:, :] = jnp.zeros((dk.shape[0] - side_rows, HD), F32)
    else:
        dv[span, :] += dv_part
        dk[span, :] += dk_part


def hand_out(core, firsts, outs, dk, dv):
    for first, out in zip(firsts, outs):
        for block, parity in ((0, core), (1, 1 - core)):
            at = pl.ds(pl.multiple_of((first + parity) * BLOCK, BLOCK), BLOCK)
            r = slice(block * BLOCK, (block + 1) * BLOCK)
            out[r, :HD] = (dk[at, :] * SCALE).astype(out.dtype)
            out[r, HD:] = dv[at, :].astype(out.dtype)


def far_kernel(kv_local, heads, n_near, n_far, *refs):
    mine, others = refs[: 1 + n_far], refs[1 + n_far : 2 + 2 * n_far]
    q_hat, rows, facts, near_expo, near_dots, sums = refs[2 + 2 * n_far : 8 + 2 * n_far]
    keys_t, pw_near, ds, *parts = refs[8 + 2 * n_far : 13 + 2 * n_far]
    keys, values, docs, expo, dots, pw_far, dk, dv = refs[13 + 2 * n_far :]
    core = lax.rem(lax.axis_index("ctx"), 2)
    blocks = 2 * n_far
    for index in range(n_far):
        source, other = mine[1 + index], others[1 + index]
        place(kv_local, source, other, 2 * index, index, core, keys, values, keys_t, docs)
    for source, parity in ((mine[0], core), (others[0], 1 - core)):
        docs[blocks + parity] = source[kv_local * BLOCK :, :].astype(F32)[0:8]
    wide = 2 * BLOCK
    far_rows = blocks * BLOCK
    doc_rows = [docs[slot][0:1] for slot in range(blocks + 2)]
    pairs = heads // 2
    steps = 2 * pairs
    biases, weights = [], []
    for side in range(2):
        biases.append(masks(doc_rows[blocks + side], doc_rows[:blocks]))
        weights.append(jnp.concatenate([facts[8 * (side + 1) : 8 * (side + 1) + 1]] * 2, axis=1))

    def scores(step):
        here, buf = slice(step * wide, (step + 1) * wide), step % 2
        expo[buf] = lax.dot_general(keys[...], q_hat[here, :], NT, preferred_element_type=F32)
        dots[buf] = lax.dot_general(values[...], rows[here, :], NT, preferred_element_type=F32)

    def middle(step):
        side, buf = step // pairs, step % 2
        total, weighted = sums[step, :8, :], sums[step, 8:, :]
        for block in range(blocks):
            at = (buf, slice(block * BLOCK, (block + 1) * BLOCK), slice(None))
            total, weighted = exponents(
                expo[at], expo, dots, at, biases[side][block], None, total, weighted
            )
        inverse = 1.0 / jnp.sum(total, axis=0, keepdims=True)
        shift = jnp.sum(weighted, axis=0, keepdims=True) * inverse
        level = inverse * weights[side]
        for block in range(blocks):
            r = slice(block * BLOCK, (block + 1) * BLOCK)
            scaled = expo[buf, r, :] * level
            pw_far[buf, r, :] = scaled.astype(BF16)
            ds[step, r, :] = (scaled * (dots[buf, r, :] - shift)).astype(BF16)
        for block in range(2 * n_near - 1 + side):
            r = slice(block * BLOCK, (block + 1) * BLOCK)
            scaled = near_expo[step, r, :].astype(F32) * level
            pw_near[step, r, :] = scaled.astype(BF16)
            to = slice(far_rows + block * BLOCK, far_rows + (block + 1) * BLOCK)
            ds[step, to, :] = (scaled * (near_dots[step, r, :] - shift)).astype(BF16)

    scores(0)
    for step in range(steps):
        if step + 1 < steps:
            scores(step + 1)
        middle(step)
        here = slice(step * wide, (step + 1) * wide)
        sum_products(
            step,
            far_rows,
            dk,
            dv,
            pw_far[step % 2],
            ds[step, :far_rows, :],
            q_hat[here, :],
            rows[here, :],
        )
    part_a, part_ce = parts
    span = 2 * BLOCK
    outs = [part_a, part_ce.at[:span, :], part_ce.at[span:, :]]
    hand_out(core, [2 * index for index in range(n_far)], outs, dk, dv)


def last_kernel(heads, n_near, n_far, *refs):
    q_hat, rows, raw_t, facts, near_t, far_t, pw_near, ds, weight = refs[:9]
    dq, held, *parts = refs[9 : 11 + n_near]
    dk, dv, sems = refs[11 + n_near :]
    copies = fetch(weight, held, sems, heads, 0)
    core = lax.rem(lax.axis_index("ctx"), 2)
    wide = 2 * BLOCK
    far_rows = 2 * n_far * BLOCK
    gain_t = jnp.broadcast_to(facts[0:1] * SCALE, (HD, HD)).T
    gain_t = jnp.concatenate([gain_t] * 2, axis=1)
    pairs = heads // 2
    for step in range(2 * pairs):
        side, here = step // pairs, slice(step * wide, (step + 1) * wide)
        reach = (2 * n_near - 1 + side) * BLOCK
        to = slice(far_rows, far_rows + reach)
        sum_products(
            step,
            reach,
            dk,
            dv,
            pw_near[step, :reach, :],
            ds[step, to, :],
            q_hat[here, :],
            rows[here, :],
        )
        dq_t = jnp.dot(far_t[...], ds[step, :far_rows, :], preferred_element_type=F32)
        dq_t = dq_t + jnp.dot(near_t[:, :reach], ds[step, to, :], preferred_element_type=F32)
        x = raw_t[:, here].astype(F32)
        inverse = lax.rsqrt(jnp.mean(x * x, axis=0, keepdims=True) + norm_eps)
        dy = dq_t * gain_t
        inner = jnp.mean(x * dy, axis=0, keepdims=True)
        dx = inverse * dy - x * (inverse * inverse * inverse * inner)
        for part in range(2):
            at = (step % pairs) * wide + part * HD
            dq[at : at + HD, side * BLOCK : (side + 1) * BLOCK] = dx[
                :, part * BLOCK : (part + 1) * BLOCK
            ].astype(BF16)
    firsts = [2 * n_near - 2 - 2 * index for index in range(n_near)]
    hand_out(core, firsts, parts, dk, dv)
    for copy in copies:
        copy.wait()


def project_kernel(first, dq, weight, keep, *sends):
    core = lax.rem(lax.axis_index("ctx"), 2)
    width = keep.shape[1]
    piece = width // len(sends)
    rows = min(256, piece)
    for i in range(width // rows):
        lanes = slice(i * rows, (i + 1) * rows)
        at = slice(first + i * rows, first + (i + 1) * rows)
        term = jnp.dot(weight[at, :], dq[...], preferred_element_type=F32).T
        even, odd = term[:BLOCK], term[BLOCK:]
        keep[:, lanes] = jnp.where(core == 0, even, odd).astype(keep.dtype)
        send = sends[i * rows // piece]
        inside = slice(i * rows % piece, i * rows % piece + rows)
        send[:, inside] = jnp.where(core == 0, odd, even).astype(send.dtype)


def project(dq, weight, first, width, pieces):
    tokens = dq.shape[1] // 2
    keep = jax.ShapeDtypeStruct((tokens, width), BF16)
    send = jax.ShapeDtypeStruct((tokens, width // pieces), BF16)
    return pl.pallas_call(
        functools.partial(project_kernel, first),
        in_specs=[vmem()] * 2,
        out_specs=[vmem()] * (1 + pieces),
        out_shape=[keep] + [send] * pieces,
        compiler_params=params(16),
        cost_estimate=SMALL,
    )(dq, weight)


def add_kernel(*refs):
    *terms, out = refs
    result = terms[0][...].astype(F32)
    for term in terms[1:]:
        result = result + term[...].astype(F32)
    out[...] = result.astype(out.dtype)


def add_pieces_kernel(whole, *refs):
    *pieces, out = refs
    width = pieces[0].shape[1]
    for i, piece in enumerate(pieces):
        lanes = slice(i * width, (i + 1) * width)
        out[:, lanes] = (whole[:, lanes].astype(F32) + piece[...].astype(F32)).astype(out.dtype)


def add_pieces(whole, pieces):
    return pl.pallas_call(
        add_pieces_kernel,
        in_specs=[vmem()] * (1 + len(pieces)),
        out_specs=vmem(),
        out_shape=jax.ShapeDtypeStruct(whole.shape, whole.dtype),
        compiler_params=params(16),
        cost_estimate=SMALL,
    )(whole, *pieces)


def add(first, second, dtype, *more):
    return pl.pallas_call(
        add_kernel,
        in_specs=[vmem()] * (2 + len(more)),
        out_specs=vmem(),
        out_shape=jax.ShapeDtypeStruct(first.shape, dtype),
        compiler_params=params(16),
        cost_estimate=SMALL,
    )(first, second, *more)


def two_sums_kernel(b, d, turn, sum_b, sum_d):
    half = turn.shape[0] // 2
    sum_b[...] = (b[...].astype(F32) + turn[:half].astype(F32)).astype(sum_b.dtype)
    sum_d[...] = (d[...].astype(F32) + turn[half:].astype(F32)).astype(sum_d.dtype)


def collect_kernel(part, back, keep, send):
    result = part[...] + back[...].astype(F32)
    keep[...] = result[:BLOCK]
    send[...] = result[BLOCK:].astype(BF16)


def finish_kernel(
    kv_local, keep, recv, key, gain, grad_key, grad_value, key_v, gain_v, sems
):
    copies = [
        pltpu.make_async_copy(key, key_v, sems.at[0]),
        pltpu.make_async_copy(gain, gain_v, sems.at[1]),
    ]
    for copy in copies:
        copy.start()
    for copy in copies:
        copy.wait()
    core = lax.rem(lax.axis_index("ctx"), 2)
    if kv_local > 1:
        parts = [(core, keep[...]), (1 - core, recv[...].astype(F32))]
    else:
        parts = [(0, keep[...] + recv[...].astype(F32))]
    for head, part in parts:
        lanes = pl.ds(pl.multiple_of(head * HD, HD), HD)
        raw = key_v[:, lanes].astype(F32)
        inverse = lax.rsqrt(jnp.mean(raw * raw, axis=-1, keepdims=True) + norm_eps)
        dy = part[:, :HD] * gain_v[...]
        inner = jnp.mean(raw * dy, axis=-1, keepdims=True)
        dx = inverse * dy - raw * (inverse * inverse * inverse * inner)
        grad_key[:, lanes] = dx.astype(BF16)
        grad_value[:, lanes] = part[:, HD:].astype(BF16)


def local(
    query_raw,
    key_raw,
    value_in,
    grad_out,
    query_gain,
    key_gain,
    loss_table,
    loss_bucket,
    block_docs,
    query_weight,
):
    tokens = query_raw.shape[0]
    kv_local = key_raw.shape[1] // HD
    half = query_raw.shape[1] // 2
    heads = half // HD
    key_row = key_gain.reshape(1, HD)
    query_row = query_gain.reshape(1, HD)
    shape = jax.ShapeDtypeStruct
    n_head = lax.axis_size("head")
    width = query_weight.shape[0] // n_head

    partner = lambda i: i ^ 1
    message, facts = pl.pallas_call(
        functools.partial(message_kernel, kv_local),
        in_specs=[vmem()] * 7,
        out_specs=[vmem()] * 2,
        out_shape=[
            shape((kv_local * BLOCK + EXTRA, 2 * HD), BF16),
            shape((16, HD), F32),
        ],
    )(
        block_docs.reshape(1, 1),
        loss_table.reshape(1, -1),
        key_raw,
        value_in,
        key_row,
        query_row,
        loss_bucket.reshape(1, tokens),
    )

    far_d = moved(message, "ctx", lambda i: i + 8)
    far_b = moved(message, "ctx", lambda i: i + 4, around=True)
    far_a = moved(message, "ctx", lambda i: i + 2 if (i // 2) % 2 == 0 else i + 10)
    query_in, grad_in, _ = lax.optimization_barrier((query_raw, grad_out, message))
    query_p = moved(query_in, "ctx", partner)
    grad_p = moved(grad_in, "ctx", partner)
    facts_p = moved(facts, "ctx", partner)
    core = lax.axis_index("ctx") % 2
    query_o = lax.dynamic_slice_in_dim(query_in, core * half, half, 1)
    grad_o = lax.dynamic_slice_in_dim(grad_in, core * half, half, 1)
    total = 2 * heads * BLOCK
    queries = pl.pallas_call(
        functools.partial(queries_kernel, heads),
        in_specs=[vmem()] * 7,
        out_specs=[vmem()] * 5,
        out_shape=[
            shape((total, HD), BF16),
            shape((total, HD), BF16),
            shape((HD, total), BF16),
            shape((24, HD), F32),
            shape(message.shape, BF16),
        ],
        compiler_params=params(16),
    )(query_o, grad_o, facts, message, query_p, grad_p, facts_p)
    far_c = moved(far_b, "ctx", lambda i: i ^ 2)
    far_d, *queries = lax.optimization_barrier((far_d, *queries))
    far_e = moved(far_d, "ctx", lambda i: i ^ 2)
    *queries, kept = queries
    q_hat, rows, raw_t, both = queries
    near = (kept, far_b, far_d)
    near_shared = [moved(source, "ctx", partner) for source in (message, far_b, far_d)]
    n_near, n_far = 3, 3
    steps = heads
    span = 2 * BLOCK
    near_rows, far_rows = n_near * span, n_far * span
    weight, near_t, near_expo, near_dots, sums = pl.pallas_call(
        functools.partial(near_kernel, kv_local, heads, n_near),
        in_specs=[vmem()] * (2 * n_near + 2) + [hbm()],
        out_specs=[vmem()] * 5,
        out_shape=[
            shape((query_weight.shape[0] - width, half), BF16),
            shape((HD, near_rows), BF16),
            shape((steps, near_rows, span), BF16),
            shape((steps, near_rows, span), F32),
            shape((steps, 16, span), F32),
        ],
        scratch_shapes=[
            pltpu.VMEM((near_rows, HD), BF16),
            pltpu.VMEM((near_rows, HD), BF16),
            pltpu.VMEM((2 * n_near, 8, 2 * HD), F32),
            pltpu.VMEM((2, near_rows, span), F32),
            pltpu.SemaphoreType.DMA((2 * (n_head - 1),)),
        ],
        compiler_params=params(34),
    )(*near, *near_shared, q_hat, rows, query_weight)

    far_e, sums = lax.optimization_barrier((far_e, sums))
    far = (far_a, far_c, far_e)
    far_shared = [moved(source, "ctx", partner) for source in far]
    part_shape = shape((span, 2 * HD), BF16)
    far_t, pw_near, ds, part_a, part_ce = pl.pallas_call(
        functools.partial(far_kernel, kv_local, heads, n_near, n_far),
        in_specs=[vmem()] * (2 * n_far + 8),
        out_specs=[vmem()] * 5,
        out_shape=[
            shape((HD, far_rows), BF16),
            shape((steps, near_rows, span), BF16),
            shape((steps, far_rows + near_rows, span), BF16),
            part_shape,
            shape((2 * span, 2 * HD), BF16),
        ],
        input_output_aliases={2 * n_far + 5: 1},
        scratch_shapes=[
            pltpu.VMEM((far_rows, HD), BF16),
            pltpu.VMEM((far_rows, HD), BF16),
            pltpu.VMEM((2 * n_far + 2, 8, 2 * HD), F32),
            pltpu.VMEM((2, far_rows, span), F32),
            pltpu.VMEM((2, far_rows, span), F32),
            pltpu.VMEM((2, far_rows, span), BF16),
            pltpu.VMEM((far_rows, HD), F32),
            pltpu.VMEM((far_rows, HD), F32),
        ],
        compiler_params=params(20),
        cost_estimate=SMALL,
    )(
        kept,
        *far,
        near_shared[0],
        *far_shared,
        q_hat,
        rows,
        both,
        near_expo,
        near_dots,
        sums,
    )

    back_a = moved(
        part_a, "ctx", lambda i: i - 2 if (i // 2) % 2 == 1 else i - 10, around=True
    )
    turn = moved(part_ce, "ctx", lambda i: i ^ 2)

    dq, mine_weight, part_own, part_b, part_d = pl.pallas_call(
        functools.partial(last_kernel, heads, n_near, n_far),
        in_specs=[vmem()] * 8 + [hbm()],
        out_specs=[vmem()] * 5,
        out_shape=[
            shape((half, 2 * tokens), BF16),
            shape((width, half), BF16),
            shape((span, 2 * HD), F32),
        ]
        + [part_shape] * 2,
        scratch_shapes=[pltpu.VMEM((near_rows, HD), F32)] * 2 + [pltpu.SemaphoreType.DMA((2,))],
        compiler_params=params(32),
        cost_estimate=SMALL,
    )(q_hat, rows, raw_t, both, near_t, far_t, pw_near, ds, query_weight)

    mine, mine_send = project(dq, mine_weight, 0, width, 1)
    arrived = []
    for shift in range(1, n_head):
        keep, *sends = project(dq, weight, (shift - 1) * width, width, 4)
        term = add_pieces(keep, [moved(send, "ctx", partner) for send in sends])
        term, turn, mine_send = lax.optimization_barrier((term, turn, mine_send))
        arrived.append(moved(term, "head", lambda i, s=shift: (i + s) % n_head))
    sum_b, sum_d = pl.pallas_call(
        two_sums_kernel,
        in_specs=[vmem()] * 3,
        out_specs=[vmem()] * 2,
        out_shape=[part_shape] * 2,
        compiler_params=params(16),
        cost_estimate=SMALL,
    )(part_b, part_d, turn)
    back_d = moved(sum_d, "ctx", lambda i: i - 8, around=True)
    back_b = moved(sum_b, "ctx", lambda i: i - 4, around=True)
    mine_recv = moved(mine_send, "ctx", partner)

    sum_keep, sum_send = pl.pallas_call(
        collect_kernel,
        in_specs=[vmem()] * 2,
        out_specs=[vmem()] * 2,
        out_shape=[shape((BLOCK, 2 * HD), F32), shape((BLOCK, 2 * HD), BF16)],
        compiler_params=params(16),
    )(add(add(part_own, back_d, F32), back_b, F32), back_a)
    sum_recv = moved(sum_send, "ctx", partner)
    arrived[-1], sum_send = lax.optimization_barrier((arrived[-1], sum_send))
    grad_input = mine
    for index, piece in enumerate(arrived):
        last = index == len(arrived) - 1
        grad_input = add(grad_input, piece, BF16 if last else F32, *([mine_recv] if last else []))
    sum_recv, grad_input = lax.optimization_barrier((sum_recv, grad_input))
    grad_key, grad_value = pl.pallas_call(
        functools.partial(finish_kernel, kv_local),
        in_specs=[vmem(), vmem(), hbm(), hbm()],
        out_specs=[vmem()] * 2,
        out_shape=[shape(key_raw.shape, BF16), shape(value_in.shape, BF16)],
        scratch_shapes=[
            pltpu.VMEM(key_raw.shape, BF16),
            pltpu.VMEM((1, HD), F32),
            pltpu.SemaphoreType.DMA((2,)),
        ],
        compiler_params=params(16),
    )(sum_keep, sum_recv, key_raw, key_row)

    return grad_input, grad_key, grad_value


def solution(mesh):
    placed = (
        P("ctx", "head"),
        P("ctx", "head"),
        P("ctx", "head"),
        P("ctx", "head"),
        P(),
        P(),
        P(),
        P("ctx"),
        P("ctx"),
        P(None, "head"),
    )
    return jax.shard_map(
        local,
        mesh=mesh,
        in_specs=placed,
        out_specs=(P("ctx", "head"), P("ctx", "head"), P("ctx", "head")),
        check_vma=False,
    )
```
